32 devices in a mesh: ctx: 4 (over y, x), exp: 8 (over z, core).
Axes of the slice: x: 2, y: 2, z: 4, core: 2. Of those that a mesh axis runs over, the one named last changes fastest.
Arguments:
- tokens: bfloat16 [8, 1024, 2048], P('exp', 'ctx'), may hold values from -6 to 6
- cotangent: bfloat16 [8, 1024, 2048], P('exp', 'ctx'), may hold values from -6 to 6
- lengths: int32 [8], P('exp'), may hold values from 897 to 1024
- span_order: int32 [8], replicated, may hold values from 0 to 7, each once
- routes: int32 [8, 1024, 8], P('exp', 'ctx'), may hold values from 0 to 15, all different within a row; in each aligned block of 256 rows (0 to 255, 256 to 511, ..., all dimensions but the last counted through in order) at most 192 rows name the same one
- w_query: bfloat16 [2048, 2048], P('exp'), may hold values from -0.125 to 0.125
- w_key: bfloat16 [2048, 2048], P('exp'), may hold values from -0.125 to 0.125
- w_value: bfloat16 [2048, 2048], P('exp'), may hold values from -0.125 to 0.125
- w_output: bfloat16 [2048, 2048], P('exp'), may hold values from -1.5 to 1.5
- w_router: bfloat16 [2048, 16], P('exp'), may hold values from -0.0625 to 0.0625
- gain_attn: bfloat16 [2048], P('exp'), may hold values from 0.099609375 to 1.8984375
- gain_query: bfloat16 [2048], P('exp'), may hold values from 0.099609375 to 1.8984375
- gain_key: bfloat16 [2048], P('exp'), may hold values from 0.099609375 to 1.8984375
- gain_mlp: bfloat16 [2048], P('exp'), may hold values from 0.099609375 to 1.8984375
- w_gate: bfloat16 [16, 2048, 1024], P('exp'), may hold values from -0.125 to 0.125
- w_up: bfloat16 [16, 2048, 1024], P('exp'), may hold values from -0.125 to 0.125
- w_down: bfloat16 [16, 1024, 2048], P('exp'), may hold values from -3 to 3
Outputs:
- mixed: bfloat16 [8, 1024, 2048], P('exp', 'ctx')
- d_tokens: bfloat16 [8, 1024, 2048], P('exp', 'ctx')
- g_w_query: float32 [2048, 2048], P('exp')
- g_w_key: float32 [2048, 2048], P('exp')
- g_w_value: float32 [2048, 2048], P('exp')
- g_w_output: float32 [2048, 2048], P('exp')
- g_w_router: float32 [2048, 16], P('exp')
- g_gain_attn: float32 [2048], P('exp')
- g_gain_query: float32 [2048], P('exp')
- g_gain_key: float32 [2048], P('exp')
- g_gain_mlp: float32 [2048], P('exp')
- g_w_gate: float32 [16, 2048, 1024], P('exp', 'ctx')
- g_w_up: float32 [16, 2048, 1024], P('exp', 'ctx')
- g_w_down: float32 [16, 1024, 2048], P('exp', 'ctx')
The draws below stay inside these ranges and needn't reach their ends.
Inputs may be any that keep to these rules, and one draw needn't show every extreme that they name: `routes`: each row names 8 different experts; in the rows of one device no expert is named by more than 192 rows, a bound that some block reaches. `span_order`: each span number appears once. `lengths`: the slots whose position is at or beyond a sequence's length are padding.
All inputs are finite; a program needn't handle non-finite values.
Results may differ from the reference program's by a relative error of at most 0.025.
Values may be sent and summed in bfloat16 or wider, within the bound.
A program may use at most 448 MiB of HBM per device.

```python
import math
import jax
import jax.numpy as jnp
import numpy as np
from jax import lax

D = 2048
HEADS = 16
HEAD_DIM = 128
FF = 1024
TOP = 8
SEQ_LEN = 1024
TOK_DEV = 256
SPAN = 128
EXPERTS = 16
CAP = 192
N_CTX = 4
N_EXP = 8


def with_ends(drawn, stream_key, smallest, top_value):
    index_at = [jax.random.randint(jax.random.fold_in(stream_key, axis), (), 0, length) for axis, length in enumerate(drawn.shape)]
    main_axis = drawn.shape.index(max(drawn.shape))
    next_to = index_at[:main_axis] + [(index_at[main_axis] + 1) % drawn.shape[main_axis]] + index_at[main_axis + 1:]
    return drawn.at[tuple(index_at)].set(smallest).at[tuple(next_to)].set(top_value)


def shard_levels(rng, dims, cuts, least, largest):
    gain, own = 1.0, jax.random.fold_in(rng, 6)
    for axis_at, blocks in cuts:
        draws = jnp.exp(jax.random.uniform(jax.random.fold_in(own, axis_at), (blocks,), jnp.float32, least / len(cuts), largest / len(cuts)))
        gain = gain * jnp.repeat(draws, dims[axis_at] // blocks).reshape([-1 if axis == axis_at else 1 for axis in range(len(dims))])
    return gain


def deal_out(rng, own, number, rows, count, top, reach, skew):
    sequence = jax.random.permutation(rng, count)
    crowded, usual = portions_of(count, rows * top, reach, skew, True), portions_of(count, rows * top, reach, skew, False)
    places = jnp.arange(count)

    def named(sizes, turn):
        used = int((sizes > 0).sum())
        fixed = max(1, used // 4)
        moved = fixed + (places - fixed + turn * (used - fixed)) % max(1, count - fixed)
        return jnp.zeros((count,), jnp.int32).at[sequence[jnp.where(places < fixed, places, moved)]].set(jnp.asarray(sizes, jnp.int32))

    sizes = jnp.where(number % 4 == 0, named(crowded, number // 4), named(usual, number - number // 4 - 1))
    mixed = jax.random.permutation(jax.random.fold_in(own, 3), count)
    donor, receiver = mixed[0:count // 2 * 2:2], mixed[1:count // 2 * 2:2]
    margin = jnp.minimum(sizes[donor] - 1, reach - sizes[receiver]) // 2
    margin = jnp.where((donor == sequence[0]) | (receiver == sequence[0]) | (sizes[receiver] == 0), 0, jnp.maximum(margin, 0))
    moved = jax.random.randint(jax.random.fold_in(own, 4), (count // 2,), 0, 1 << 20) % (margin + 1)
    sizes = sizes.at[donor].add(-moved).at[receiver].add(moved)
    members = jnp.searchsorted(jnp.cumsum(sizes), jnp.arange(rows * top), side="right").astype(jnp.int32)
    grid = members.reshape(top, rows).T
    grid = grid[jax.random.permutation(jax.random.fold_in(own, 1), rows)]
    turn = jax.random.randint(jax.random.fold_in(own, 2), (rows, 1), 0, top)
    return jnp.take_along_axis(grid, (jnp.arange(top)[None, :] + turn) % top, axis=1)


def portions_of(count, total, reach, lean, full):
    loads = [(1 << 20) // math.isqrt(rank ** lean) + 1 for rank in range(1, count + 1)]
    largest = reach if full else min(reach, max(-(-total // count), total * loads[0] // sum(loads)))
    least = 1 if total - largest >= count - 1 else 0
    counts, spare = [largest] + [least] * (count - 1), total - largest - least * (count - 1)
    while spare > 0:
        free = [i for i in range(1, count) if counts[i] < largest] or [i for i in range(1, count) if counts[i] < reach]
        whole, remaining = sum([loads[i] for i in free]), spare
        for i in free:
            addition = min(reach - counts[i], max(1, remaining * loads[i] // whole), spare)
            counts[i] = counts[i] + addition
            spare = spare - addition
    return np.array(counts)


def scatter_about(own_key, extent, deviation, most, cuts=(), kind=jnp.bfloat16):
    array = jax.random.normal(own_key, extent, jnp.float32) * deviation
    if len(cuts) > 0:
        array = shard_levels(own_key, extent, cuts, -0.22, 0.18) * array
    return jnp.clip(array, min=-most, max=most).astype(kind)


def setup_inputs(seed: int = 0) -> dict:
    keys = jax.random.split(jax.random.key(seed), 18)
    tokens = scatter_about(keys[0], (N_EXP, SEQ_LEN, D), 1.0, 6.0, ((0, 8), (1, 4)))
    cotangent = scatter_about(keys[1], (N_EXP, SEQ_LEN, D), 1.0, 6.0, ((0, 8), (1, 4)))
    lengths = with_ends(jax.random.randint(keys[2], (N_EXP,), SEQ_LEN - SPAN + 1, SEQ_LEN + 1), jax.random.fold_in(keys[2], 1), SEQ_LEN - SPAN + 1, SEQ_LEN).astype(jnp.int32)
    span_order = jax.random.permutation(keys[3], 2 * N_CTX).astype(jnp.int32)
    routes_keys = jax.random.split(jax.random.fold_in(keys[4], 1), N_EXP * SEQ_LEN // TOK_DEV)
    routes_turns = jax.random.permutation(jax.random.fold_in(keys[4], 3), N_EXP * SEQ_LEN // TOK_DEV)
    routes = jax.vmap(lambda own, number: deal_out(jax.random.fold_in(keys[4], 2), own, number, TOK_DEV, EXPERTS, TOP, CAP, 1))(routes_keys, routes_turns).reshape((N_EXP, SEQ_LEN, TOP))
    w_query = scatter_about(keys[5], (D, D), D ** -0.5, 0.125, ((0, 8),))
    w_key = scatter_about(keys[6], (D, D), D ** -0.5, 0.125, ((0, 8),))
    w_value = scatter_about(keys[7], (D, D), D ** -0.5, 0.125, ((0, 8),))
    w_output = scatter_about(keys[8], (D, D), (D // 128) ** -0.5, 1.5, ((0, 8),))
    w_router = scatter_about(keys[9], (D, EXPERTS), (4 * D) ** -0.5, 0.0625, ((0, 8),))
    gain_attn = jnp.clip(1.0 + 0.18 * jax.random.normal(keys[10], (D,), jnp.float32), 0.099609375, 1.8984375).astype(jnp.bfloat16)
    gain_query = jnp.clip(1.0 + 0.18 * jax.random.normal(keys[11], (D,), jnp.float32), 0.099609375, 1.8984375).astype(jnp.bfloat16)
    gain_key = jnp.clip(1.0 + 0.18 * jax.random.normal(keys[12], (D,), jnp.float32), 0.099609375, 1.8984375).astype(jnp.bfloat16)
    gain_mlp = jnp.clip(1.0 + 0.18 * jax.random.normal(keys[13], (D,), jnp.float32), 0.099609375, 1.8984375).astype(jnp.bfloat16)
    w_gate = scatter_about(keys[14], (EXPERTS, D, FF), D ** -0.5, 0.125, ((0, 8),))
    w_up = scatter_about(keys[15], (EXPERTS, D, FF), D ** -0.5, 0.125, ((0, 8),))
    w_down = scatter_about(keys[16], (EXPERTS, FF, D), (max(FF // 256, 1)) ** -0.5, 3.0, ((0, 8),))
    return {"tokens": tokens, "cotangent": cotangent, "lengths": lengths, "span_order": span_order, "routes": routes, "w_query": w_query, "w_key": w_key, "w_value": w_value, "w_output": w_output, "w_router": w_router, "gain_attn": gain_attn, "gain_query": gain_query, "gain_key": gain_key, "gain_mlp": gain_mlp, "w_gate": w_gate, "w_up": w_up, "w_down": w_down}


EPSILON = 1e-05
ROPE_BASE = 10000.0
MASKED_SCORE = -1e+30
FULL_PRECISION = lax.Precision.HIGHEST

@jax.custom_vjp
def low(v):
    return lax.optimization_barrier(v.astype(jnp.bfloat16)).astype(jnp.float32)

@jax.custom_vjp
def low_back(v):
    return v

def low_keep(v):
    return (low(v), None)

def low_pass(kept, grad):
    return (grad,)

def back_keep(v):
    return (v, None)

def back_low(kept, grad):
    return (low(grad),)
low.defvjp(low_keep, low_pass)
low_back.defvjp(back_keep, back_low)

def rms_norm(value_rows, gain_vec):
    return value_rows * lax.rsqrt(lax.optimization_barrier(jnp.mean(value_rows * value_rows, axis=-1, keepdims=True)) + EPSILON) * gain_vec

def rope_tables(positions, head_features):
    half_dim = head_features // 2
    frequency = jnp.exp(jnp.arange(half_dim, dtype=jnp.float32) * (-2.0 * math.log(ROPE_BASE) / head_features))
    angle = positions.astype(jnp.float32)[:, None] * frequency[None, :]
    return (jnp.cos(angle)[:, None, :], jnp.sin(angle)[:, None, :])

def rotate(value_rows, cosine_table, sine_table):
    half_dim = value_rows.shape[-1] // 2
    first_half = value_rows[..., :half_dim]
    second_half = value_rows[..., half_dim:]
    return jnp.concatenate([first_half * cosine_table - second_half * sine_table, second_half * cosine_table + first_half * sine_table], axis=-1)

def positions_of(span_order, storage, span_length):
    return jnp.take(span_order, storage // span_length) * span_length + storage % span_length

def project(value_rows, weight_matrix):
    return jnp.einsum('zfi,ig->zfg', value_rows, weight_matrix, precision=FULL_PRECISION)

def reference(tokens, cotangent, lengths, span_order, routes, w_query, w_key, w_value, w_output, w_router, gain_attn, gain_query, gain_key, gain_mlp, w_gate, w_up, w_down):
    positions = positions_of(span_order, jnp.arange(SEQ_LEN, dtype=jnp.int32), SPAN)
    cosine_table, sine_table = rope_tables(positions, HEAD_DIM)
    block_count = N_EXP * N_CTX
    per_block = TOK_DEV * TOP
    block_routes = routes.reshape(block_count, per_block)
    onehot = (block_routes[:, :, None] == jnp.arange(EXPERTS, dtype=jnp.int32)[None, None, :]).astype(jnp.int32)
    route_rank = lax.optimization_barrier(jnp.sum(jnp.cumsum(onehot, axis=1) * onehot, axis=-1)) - 1
    block_ids = jnp.arange(block_count, dtype=jnp.int32)[:, None]
    expert_rows = block_count * CAP
    where_rows = block_routes * expert_rows + block_ids * CAP + route_rank
    source = block_ids * TOK_DEV + jnp.arange(per_block, dtype=jnp.int32)[None, :] // TOP
    row_table = jnp.zeros((EXPERTS * expert_rows,), jnp.int32).at[where_rows.reshape(-1)].set(source.reshape(-1)).reshape(EXPERTS, expert_rows)
    fill_table = jnp.zeros((EXPERTS * expert_rows,), jnp.float32).at[where_rows.reshape(-1)].set(1.0).reshape(EXPERTS, expert_rows)
    where_rows = where_rows.reshape(N_EXP * SEQ_LEN, TOP)
    flat_routes = routes.reshape(N_EXP * SEQ_LEN, TOP)
    head_shape = (N_EXP, SEQ_LEN, HEADS, HEAD_DIM)
    factor = HEAD_DIM ** (-0.5)

    def forward(block_input, query_weight, key_weight, value_weight, output_weight, router_weight, attn_gain, query_gain, key_gain, mlp_gain, gate_weight, up_weight, down_weight):
        normed_in = low(rms_norm(block_input, attn_gain))
        query_proj = low_back(project(normed_in, query_weight))
        key_proj = low_back(project(normed_in, key_weight))
        value_proj = low_back(project(normed_in, value_weight))
        query_rot = low(rotate(rms_norm(query_proj, query_gain).reshape(head_shape), cosine_table, sine_table))
        key_rot = low(rotate(rms_norm(key_proj, key_gain).reshape(head_shape), cosine_table, sine_table))
        value_low = low(value_proj).reshape(head_shape)

        def attend(pieces):
            query_seq, key_seq, value_seq, seq_length = pieces
            scores = low_back(jnp.einsum('thd,shd->hts', query_seq, key_seq, precision=FULL_PRECISION) * factor)
            allowed = (positions[None, :] <= positions[:, None]) & (positions[None, :] < seq_length)
            scores = jnp.where(allowed[None], scores, MASKED_SCORE)
            weights = jax.nn.softmax(scores, axis=-1)
            return jnp.einsum('hts,shd->thd', low(weights), value_seq, precision=FULL_PRECISION)
        attended = lax.map(jax.checkpoint(attend), (query_rot, key_rot, value_low, lengths))
        attended = low(low_back(attended.reshape(N_EXP, SEQ_LEN, D)))
        residual = block_input + low_back(project(attended, output_weight))
        normed_mid = low(rms_norm(residual, mlp_gain)).reshape(N_EXP * SEQ_LEN, D)
        router_probs = jax.nn.softmax(jnp.dot(normed_mid, router_weight, precision=FULL_PRECISION), axis=-1)
        gate_probs = jnp.take_along_axis(router_probs, flat_routes, axis=1)

        def expert_network(pieces):
            row_index, row_fill, first_weight, third_weight, second_weight = pieces
            expert_in = low_back(jnp.take(normed_mid, row_index, axis=0) * row_fill[:, None])
            gate_pre = low_back(jnp.dot(expert_in, first_weight, precision=FULL_PRECISION))
            up_pre = low_back(jnp.dot(expert_in, third_weight, precision=FULL_PRECISION))
            hidden = low(jax.nn.silu(gate_pre) * up_pre)
            return low(low_back(jnp.dot(hidden, second_weight, precision=FULL_PRECISION)))
        expert_out = lax.map(jax.checkpoint(expert_network), (row_table, fill_table, gate_weight, up_weight, down_weight)).reshape(-1, D)
        mixed_out = residual.reshape(N_EXP * SEQ_LEN, D)
        for which_route in range(TOP):
            mixed_out = mixed_out + gate_probs[:, which_route:which_route + 1] * jnp.take(expert_out, where_rows[:, which_route], axis=0)
        return mixed_out.reshape(N_EXP, SEQ_LEN, D)
    arrays = [array_in.astype(jnp.float32) for array_in in (tokens, w_query, w_key, w_value, w_output, w_router, gain_attn, gain_query, gain_key, gain_mlp, w_gate, w_up, w_down)]
    result, pullback = jax.vjp(forward, *arrays)
    valid_rows = (positions[None, :] < lengths[:, None]).astype(jnp.float32)
    gradients = pullback(cotangent.astype(jnp.float32) * valid_rows[:, :, None])
    return (result.astype(jnp.bfloat16), gradients[0].astype(jnp.bfloat16), gradients[1], gradients[2], gradients[3], gradients[4], gradients[5], gradients[6], gradients[7], gradients[8], gradients[9], gradients[10], gradients[11], gradients[12])
```

```python
import math

import jax
import jax.numpy as jnp
from jax import lax
from jax.sharding import PartitionSpec as P

HEADS = 16
HEAD_DIM = 128
EPSILON = 1e-05
ROPE_BASE = 10000.0
MASKED_SCORE = -1e30
FACTOR = HEAD_DIM ** (-0.5)
F32 = jnp.float32
BF16 = jnp.bfloat16


def mm(left, right):
    return jnp.dot(left, right, preferred_element_type=F32)


def mm_t(left, right):
    return lax.dot_general(left, right, (((1,), (1,)), ((), ())), preferred_element_type=F32)


def t_mm(left, right):
    return lax.dot_general(left, right, (((0,), (0,)), ((), ())), preferred_element_type=F32)


def rms_scale(rows):
    return lax.rsqrt(jnp.mean(rows * rows, axis=-1, keepdims=True) + EPSILON)


def rms_backward(rows, inv_scale, gain_vec, grad_in):
    weighted = grad_in * gain_vec
    inner_mean = jnp.mean(weighted * rows, axis=-1, keepdims=True)
    d_rows = inv_scale * weighted - rows * (inv_scale * inv_scale * inv_scale) * inner_mean
    return d_rows, jnp.sum(grad_in * rows * inv_scale, axis=0)


def rope_tables(positions):
    half_dim = HEAD_DIM // 2
    frequency = jnp.exp(
        jnp.arange(half_dim, dtype=F32) * (-2.0 * math.log(ROPE_BASE) / HEAD_DIM)
    )
    angle = positions.astype(F32)[:, None] * frequency[None, :]
    return jnp.cos(angle)[:, None, :], jnp.sin(angle)[:, None, :]


def rotate(rows, cosine, sine):
    half_dim = rows.shape[-1] // 2
    first, second = rows[..., :half_dim], rows[..., half_dim:]
    return jnp.concatenate([first * cosine - second * sine, second * cosine + first * sine], axis=-1)


def positions_of(span_order, storage, span_length):
    return jnp.take(span_order, storage // span_length) * span_length + storage % span_length


def gather(block, axis):
    return lax.all_gather(block, axis, axis=0, tiled=True)


def scatter_sum(block, axis, dimension=0):
    return lax.psum_scatter(block, axis, scatter_dimension=dimension, tiled=True)


def local(
    tokens, cotangent, lengths, span_order, routes,
    w_query, w_key, w_value, w_output, w_router,
    gain_attn, gain_query, gain_key, gain_mlp,
    w_gate, w_up, w_down,
):
    n_ctx, n_exp = lax.axis_size("ctx"), lax.axis_size("exp")
    c_at, e_at = lax.axis_index("ctx"), lax.axis_index("exp")
    rows = tokens.shape[1]
    width = tokens.shape[2]
    seq = rows * n_ctx
    cols = width // n_ctx
    heads = HEADS // n_ctx
    shard = width // n_exp
    own = w_gate.shape[0]
    experts = w_router.shape[1]
    seq_length = lengths[0]

    chunk = width // (n_ctx * n_exp)
    moves = []
    for g in range(n_ctx * n_exp):
        source = (g % n_ctx) * n_exp + g // n_ctx
        moves.append((source, g))
    out_piece = lax.dynamic_slice_in_dim(w_output, c_at * chunk, chunk, 0)
    out_piece = lax.ppermute(out_piece, ("ctx", "exp"), moves)

    member = jnp.sum(
        (routes[0][:, :, None] == jnp.arange(experts, dtype=jnp.int32)[None, None, :]).astype(BF16),
        axis=1,
    )
    small = jnp.concatenate(
        [
            w_router.reshape(-1), gain_attn, gain_query, gain_key, gain_mlp, member.reshape(-1),
        ]
    )
    small_all = gather(small[None], "exp")
    at = shard * experts
    router_w = small_all[:, :at].reshape(width, experts)
    gains = []
    for _ in range(4):
        gains.append(small_all[:, at : at + shard].reshape(width).astype(F32))
        at += shard
    attn_gain, query_gain_all, key_gain_all, mlp_gain = gains
    member_all = small_all[:, at:].reshape(n_exp * rows, experts).astype(F32)
    query_gain = lax.dynamic_slice_in_dim(query_gain_all, c_at * cols, cols, 0)
    key_gain = lax.dynamic_slice_in_dim(key_gain_all, c_at * cols, cols, 0)

    qkv_piece = jnp.concatenate(
        [
            lax.dynamic_slice_in_dim(w, c_at * cols, cols, 1)
            for w in (w_query, w_key, w_value)
        ],
        axis=1,
    )
    qkv_w = gather(qkv_piece, "exp")
    x_all = gather(tokens[0], "ctx").astype(F32)
    out_w = gather(out_piece, "exp")
    grad_all_raw = gather(cotangent[0], "exp")

    positions = positions_of(span_order, jnp.arange(seq, dtype=jnp.int32), rows // 2)
    allowed = (positions[None, :] <= positions[:, None]) & (positions[None, :] < seq_length)
    cosine, sine = rope_tables(positions)
    head_shape = (seq, heads, HEAD_DIM)

    in_scale_all = rms_scale(x_all)
    xn = (x_all * in_scale_all * attn_gain).astype(BF16)
    qkv = mm(xn, qkv_w)
    qp, kp, vp = qkv[:, :cols], qkv[:, cols : 2 * cols], qkv[:, 2 * cols :]
    squares = jnp.stack([jnp.sum(qp * qp, axis=-1), jnp.sum(kp * kp, axis=-1)], axis=0)
    squares = lax.psum(squares, "ctx") / width
    q_scale = lax.rsqrt(squares[0] + EPSILON)[:, None]
    k_scale = lax.rsqrt(squares[1] + EPSILON)[:, None]
    q_rot = rotate((qp * q_scale * query_gain).reshape(head_shape), cosine, sine).astype(BF16)
    k_rot = rotate((kp * k_scale * key_gain).reshape(head_shape), cosine, sine).astype(BF16)
    v_low = vp.astype(BF16).reshape(head_shape)

    def scores_of():
        raw = jnp.einsum("thd,shd->hts", q_rot, k_rot, preferred_element_type=F32) * FACTOR
        return jnp.where(allowed[None], raw, MASKED_SCORE)

    scores = scores_of()
    row_max = jnp.max(scores, axis=-1, keepdims=True)
    expo = jnp.exp(scores - row_max)
    total = jnp.sum(expo, axis=-1, keepdims=True)
    probs = expo / total
    probs_low = probs.astype(BF16)
    attended = (
        jnp.einsum("hts,shd->thd", probs_low, v_low, preferred_element_type=F32)
        .reshape(seq, cols)
        .astype(BF16)
    )
    attn_out = scatter_sum(mm(attended, out_w).astype(BF16), "ctx").astype(F32)
    block_input = tokens[0].astype(F32)
    residual = block_input + attn_out
    mid_scale = rms_scale(residual)
    mid_low = (residual * mid_scale * mlp_gain).astype(BF16)
    mid_all = gather(mid_low, "exp")

    lengths_all = gather(lengths, "exp")
    my_positions = positions_of(
        span_order, c_at * rows + jnp.arange(rows, dtype=jnp.int32), rows // 2
    )
    valid_all = (my_positions[None, :] < lengths_all[:, None]).reshape(n_exp * rows, 1)
    grad_all = jnp.where(valid_all, grad_all_raw, jnp.zeros_like(grad_all_raw))

    router = jax.nn.softmax(mm(mid_all, router_w), axis=-1)
    own_cols = e_at * own + jnp.arange(own)
    chosen = router * member_all
    gate_own = lax.dynamic_slice_in_dim(chosen, e_at * own, own, 1)
    member_own = lax.dynamic_slice_in_dim(member_all, e_at * own, own, 1)

    hiddens, d_pres, flows = [], [], []
    for j in range(own):
        gate = gate_own[:, j : j + 1]
        d_hidden = mm_t(grad_all, w_down[j])
        a = mm(mid_all, w_gate[j])
        b = mm(mid_all, w_up[j])
        sig = jax.nn.sigmoid(a)
        silu = a * sig
        hidden = silu * b
        hidden_low = hidden.astype(BF16)
        flows.append(
            gate[:, 0] * jnp.sum(hidden_low.astype(F32) * d_hidden, axis=-1)
        )
        hiddens.append((gate * hidden).astype(BF16))
        dh = gate * d_hidden
        d_pres.append(
            ((dh * b * sig * (1.0 + a * (1.0 - sig))).astype(BF16), (dh * silu).astype(BF16))
        )
    flow = jnp.stack(flows, axis=1)
    one_own = (jnp.arange(experts)[None, :] == own_cols[:, None]).astype(F32)
    d_logit = jnp.sum(flow[:, :, None] * one_own[None], axis=1) - router * jnp.sum(
        flow, axis=1, keepdims=True
    )
    dx = mm_t(d_logit, router_w.astype(F32))
    for j in range(own):
        dx = dx + mm_t(d_pres[j][0], w_gate[j]) + mm_t(d_pres[j][1], w_up[j])
    d_mid = scatter_sum(dx.astype(BF16), "exp").astype(F32)
    y = mm(hiddens[0], w_down[0])
    for j in range(1, own):
        y = y + mm(hiddens[j], w_down[j])
    y_mine = scatter_sum(y.astype(BF16), "exp").astype(F32)
    mixed = (residual + y_mine).astype(BF16)
    g_router = t_mm(mid_all.astype(F32), d_logit)
    g_gate = jnp.stack([t_mm(mid_all, d_pres[j][0]).astype(BF16) for j in range(own)])
    g_up = jnp.stack([t_mm(mid_all, d_pres[j][1]).astype(BF16) for j in range(own)])
    g_down = jnp.stack([t_mm(hiddens[j], grad_all).astype(BF16) for j in range(own)])
    expert_grads = [scatter_sum(g, "ctx", 1).astype(F32) for g in (g_gate, g_up, g_down)]

    valid_mine = (my_positions < seq_length).astype(F32)[:, None]
    grad_mine = cotangent[0].astype(F32) * valid_mine
    d_mid_norm, g_mid_gain = rms_backward(residual, mid_scale, mlp_gain, d_mid)
    d_residual = grad_mine + d_mid_norm
    dl_all = gather(d_residual.astype(BF16), "ctx")

    d_att = mm_t(dl_all, out_w).astype(BF16).reshape(head_shape)
    g_out = t_mm(attended, dl_all)
    d_probs = jnp.einsum("thd,shd->hts", d_att, v_low, preferred_element_type=F32)
    row_inner = jnp.sum(probs * d_probs, axis=-1, keepdims=True)
    d_scores = (probs * (d_probs - row_inner)).astype(BF16)
    dq_rot = jnp.einsum("hts,shd->thd", d_scores, k_rot, preferred_element_type=F32) * FACTOR
    dk_rot = jnp.einsum("hts,thd->shd", d_scores, q_rot, preferred_element_type=F32) * FACTOR
    dv = jnp.einsum("hts,thd->shd", probs_low, d_att, preferred_element_type=F32)
    dq_n = rotate(dq_rot, cosine, -sine).reshape(seq, cols)
    dk_n = rotate(dk_rot, cosine, -sine).reshape(seq, cols)
    inner = jnp.stack(
        [
            jnp.sum(dq_n * query_gain * qp, axis=-1),
            jnp.sum(dk_n * key_gain * kp, axis=-1),
        ],
        axis=0,
    )
    inner = lax.psum(inner, "ctx") / width
    dqp = q_scale * dq_n * query_gain - qp * (q_scale**3) * inner[0][:, None]
    dkp = k_scale * dk_n * key_gain - kp * (k_scale**3) * inner[1][:, None]
    g_query_gain = jnp.sum(dq_n * qp * q_scale, axis=0)
    g_key_gain = jnp.sum(dk_n * kp * k_scale, axis=0)
    d_qkv = jnp.concatenate(
        [dqp.astype(BF16), dkp.astype(BF16), dv.reshape(seq, cols).astype(BF16)], axis=1
    )
    dxn = scatter_sum(mm_t(d_qkv, qkv_w).astype(BF16), "ctx").astype(F32)
    in_scale = rms_scale(block_input)
    d_in_norm, g_attn_gain = rms_backward(block_input, in_scale, attn_gain, dxn)
    d_tokens = (d_residual + d_in_norm).astype(BF16)

    g_qkv = scatter_sum(t_mm(xn, d_qkv).astype(BF16), "exp")
    g_qkv = gather(g_qkv[None], "ctx")
    g_qkv = g_qkv.reshape(n_ctx, shard, 3, cols).transpose(2, 1, 0, 3).reshape(3, shard, width)
    g_qkv = g_qkv.astype(F32)
    g_out = scatter_sum(g_out.astype(BF16), "exp")
    g_out = lax.ppermute(g_out, ("ctx", "exp"), [(b, a) for a, b in moves])
    g_out = gather(g_out, "ctx").astype(F32)

    placed = []
    for part in (g_query_gain, g_key_gain):
        placed.append(
            lax.dynamic_update_slice_in_dim(jnp.zeros((width,), F32), part, c_at * cols, 0)
        )
    small_grads = jnp.concatenate(
        [g_router, jnp.stack([g_attn_gain, placed[0], placed[1], g_mid_gain], axis=1)], axis=1
    )
    small_grads = lax.psum(scatter_sum(small_grads, "exp"), "ctx")
    return (
        mixed[None], d_tokens[None],
        g_qkv[0], g_qkv[1], g_qkv[2], g_out,
        small_grads[:, :experts],
        small_grads[:, experts], small_grads[:, experts + 1],
        small_grads[:, experts + 2], small_grads[:, experts + 3],
        expert_grads[0], expert_grads[1], expert_grads[2],
    )


def solution(mesh):
    tok = P("exp", "ctx", None)
    two, three, one = P("exp", None), P("exp", None, None), P("exp")
    return jax.shard_map(
        local,
        mesh=mesh,
        in_specs=(tok, tok, one, P(), tok) + (two,) * 5 + (one,) * 4 + (three,) * 3,
        out_specs=(tok, tok) + (two,) * 5 + (one,) * 4 + (tok,) * 3,
        check_vma=False,
    )
```

```python
import functools
import math

import jax
import jax.numpy as jnp
from jax import lax
from jax.experimental import pallas as pl
from jax.experimental.pallas import tpu as pltpu
from jax.sharding import PartitionSpec as P

HEADS = 16
HEAD_DIM = 128
LANES = 128
EPSILON = 1e-05
ROPE_BASE = 10000.0
MASKED_SCORE = -1e30
FACTOR = HEAD_DIM ** (-0.5)
F32 = jnp.float32
BF16 = jnp.bfloat16
MIB = 1 << 20


def mm(left, right):
    return jnp.dot(left, right, preferred_element_type=F32)


def mm_t(left, right):
    return lax.dot_general(left, right, (((1,), (1,)), ((), ())), preferred_element_type=F32)


def t_mm(left, right):
    return lax.dot_general(left, right, (((0,), (0,)), ((), ())), preferred_element_type=F32)


def rms_scale(rows):
    return lax.rsqrt(jnp.mean(rows * rows, axis=-1, keepdims=True) + EPSILON)


def rms_backward(rows, inv_scale, gain_vec, grad_in):
    weighted = grad_in * gain_vec
    inner_mean = jnp.mean(weighted * rows, axis=-1, keepdims=True)
    d_rows = inv_scale * weighted - rows * (inv_scale * inv_scale * inv_scale) * inner_mean
    return d_rows, jnp.sum(grad_in * rows * inv_scale, axis=0)


def rope_tables(positions):
    half_dim = HEAD_DIM // 2
    frequency = jnp.exp(
        jnp.arange(half_dim, dtype=F32) * (-2.0 * math.log(ROPE_BASE) / HEAD_DIM)
    )
    angle = positions.astype(F32)[:, None] * frequency[None, :]
    cosine, sine = jnp.cos(angle), jnp.sin(angle)
    return (
        jnp.concatenate([cosine, cosine], axis=1),
        jnp.concatenate([-sine, sine], axis=1),
    )


def positions_of(span_order, storage, span_length):
    return jnp.take(span_order, storage // span_length) * span_length + storage % span_length


def rotated(rows, scale, gain, cosine, sine):
    normed = rows * scale * gain
    return (normed * cosine + pltpu.roll(normed, HEAD_DIM // 2, 1) * sine).astype(BF16)


def unrotated(rows, cosine, sine):
    return rows * cosine - pltpu.roll(rows, HEAD_DIM // 2, 1) * sine


def head_probs(query, key, q_pos, k_pos):
    scores = jnp.where(k_pos <= q_pos, mm_t(query, key) * FACTOR, MASKED_SCORE)
    expo = jnp.exp(scores - jnp.max(scores, axis=1, keepdims=True))
    return expo / jnp.sum(expo, axis=1, keepdims=True)


def attend_kernel(
    q_ref, k_ref, v_ref, qs_ref, ks_ref, qg_ref, kg_ref, qc_ref, qn_ref, kc_ref, kn_ref,
    qp_ref, kp_ref, out_ref,
):
    query = rotated(q_ref[...], qs_ref[...], qg_ref[...], qc_ref[...], qn_ref[...])
    key = rotated(k_ref[...], ks_ref[...], kg_ref[...], kc_ref[...], kn_ref[...])
    probs = head_probs(query, key, qp_ref[...], kp_ref[...])
    out_ref[...] = mm(probs.astype(BF16), v_ref[...].astype(BF16)).astype(BF16)


def attend_back_kernel(
    q_ref, k_ref, v_ref, qs_ref, ks_ref, qg_ref, kg_ref, qc_ref, qn_ref, kc_ref, kn_ref,
    qp_ref, kp_ref, da_ref, dk_in, dv_in, *refs,
):
    dq_ref, dk_ref, dv_ref = refs[-3:]
    query = rotated(q_ref[...], qs_ref[...], qg_ref[...], qc_ref[...], qn_ref[...])
    key = rotated(k_ref[...], ks_ref[...], kg_ref[...], kc_ref[...], kn_ref[...])
    probs = head_probs(query, key, qp_ref[...], kp_ref[...])
    d_att = da_ref[...]
    d_probs = mm_t(d_att, v_ref[...].astype(BF16))
    inner = jnp.sum(probs * d_probs, axis=1, keepdims=True)
    d_scores = (probs * (d_probs - inner)).astype(BF16)
    dq_ref[...] = unrotated(mm(d_scores, key) * FACTOR, qc_ref[...], qn_ref[...])
    dk = unrotated(t_mm(d_scores, query) * FACTOR, kc_ref[...], kn_ref[...])
    dk_ref[...] = dk_in[...] + dk
    dv_ref[...] = dv_in[...] + t_mm(probs.astype(BF16), d_att)


def attention_specs(rows, seq, heads, h):
    def head_rows(n, at, row=0):
        return pl.BlockSpec((n, HEAD_DIM), lambda i: (row, at + i))

    def fixed(shape, row=0):
        return pl.BlockSpec(shape, lambda i: (row, 0))

    return [
        head_rows(rows, 0, h), head_rows(seq, heads), head_rows(seq, 2 * heads),
        fixed((rows, 1), h), fixed((seq, 1)), head_rows(1, 0), head_rows(1, 0),
        fixed((rows, HEAD_DIM), h), fixed((rows, HEAD_DIM), h),
        fixed((seq, HEAD_DIM)), fixed((seq, HEAD_DIM)),
        fixed((rows, 1), h), fixed((1, seq)),
    ]


def attend(base, rows, h):
    seq, cols = base[0].shape[0], base[0].shape[1] // 3
    heads = cols // HEAD_DIM
    return pl.pallas_call(
        attend_kernel,
        grid=(heads,),
        in_specs=attention_specs(rows, seq, heads, h),
        out_specs=pl.BlockSpec((rows, HEAD_DIM), lambda i: (0, i)),
        out_shape=jax.ShapeDtypeStruct((rows, cols), BF16),
        compiler_params=pltpu.CompilerParams(vmem_limit_bytes=48 * MIB),
        cost_estimate=pl.CostEstimate(
            flops=4 * rows * seq * cols, bytes_accessed=8 * MIB, transcendentals=rows * seq * heads
        ),
    )(*base)


def attend_back(base, rows, h, d_att, dk, dv, earlier):
    seq, cols = base[0].shape[0], base[0].shape[1] // 3
    heads = cols // HEAD_DIM
    q_out = pl.BlockSpec((rows, HEAD_DIM), lambda i: (0, i))
    k_out = pl.BlockSpec((seq, HEAD_DIM), lambda i: (0, i))
    return pl.pallas_call(
        attend_back_kernel,
        grid=(heads,),
        in_specs=attention_specs(rows, seq, heads, h)
        + [q_out, k_out, k_out]
        + [pl.BlockSpec(memory_space=pl.ANY)] * len(earlier),
        out_specs=[q_out, k_out, k_out],
        out_shape=[
            jax.ShapeDtypeStruct((rows, cols), F32),
            jax.ShapeDtypeStruct((seq, cols), F32),
            jax.ShapeDtypeStruct((seq, cols), F32),
        ],
        compiler_params=pltpu.CompilerParams(vmem_limit_bytes=48 * MIB),
        cost_estimate=pl.CostEstimate(
            flops=10 * rows * seq * cols, bytes_accessed=16 * MIB, transcendentals=rows * seq * heads
        ),
    )(*base, d_att, dk, dv, *earlier)


def expert_kernel(
    experts, own, step, x_ref, dh_ref, member_ref, router_ref, pick_ref, wg_hbm, wu_hbm,
    hid_ref, da_ref, db_ref, dx_ref, coef_ref, wg, wu, sems,
):
    i = pl.program_id(0)

    def loads(j):
        return (
            pltpu.make_async_copy(wg_hbm.at[j], wg.at[j], sems.at[0, j]),
            pltpu.make_async_copy(wu_hbm.at[j], wu.at[j], sems.at[1, j]),
        )

    @pl.when(i == 0)
    def _():
        for j in range(own):
            for copy in loads(j):
                copy.start()

    logits = mm(x_ref[...], router_ref[...])
    lane = lax.broadcasted_iota(jnp.int32, logits.shape, 1)
    logits = jnp.where(lane < experts, logits, MASKED_SCORE)
    expo = jnp.exp(logits - jnp.max(logits, axis=1, keepdims=True))
    router = expo / jnp.sum(expo, axis=1, keepdims=True)
    chosen = router * member_ref[...].astype(F32)
    coef = jnp.zeros_like(router)
    ff = wg.shape[2]
    for j in range(own):

        @pl.when(i == 0)
        def _():
            for copy in loads(j):
                copy.wait()

        pick = pick_ref[j : j + 1, :]
        gate = jnp.sum(chosen * pick, axis=1, keepdims=True)
        flow = jnp.zeros_like(gate)
        for f in range(0, ff, step):
            cut = slice(f, f + step)
            a = mm(x_ref[...], wg[j, :, cut])
            b = mm(x_ref[...], wu[j, :, cut])
            d_hid = dh_ref[j, :, cut].astype(F32)
            sig = jax.nn.sigmoid(a)
            silu = a * sig
            hid = silu * b
            flow = flow + jnp.sum(hid * d_hid, axis=1, keepdims=True)
            hid_ref[j, :, cut] = (gate * hid).astype(BF16)
            d_hid = d_hid * gate
            da_ref[j, :, cut] = (d_hid * b * (sig + silu * (1.0 - sig))).astype(BF16)
            db_ref[j, :, cut] = (d_hid * silu).astype(BF16)
        coef = coef + flow * gate * (pick - router)
    low = coef.astype(BF16)
    coef_ref[...] = low
    width = x_ref.shape[1]
    for n in range(0, width, step):
        cut = slice(n, n + step)
        part = mm_t(low, router_ref[cut, :])
        for j in range(own):
            part = part + mm_t(da_ref[j], wg[j, cut, :]) + mm_t(db_ref[j], wu[j, cut, :])
        dx_ref[:, cut] = part.astype(BF16)


def expert_pass(x, d_hid, member, router_w, pick, w_gate, w_up, experts):
    rows, width = x.shape
    own, _, ff = w_gate.shape
    tile = 256
    by_row = pl.BlockSpec((tile, width), lambda i: (i, 0))
    by_lane = pl.BlockSpec((tile, LANES), lambda i: (i, 0))
    by_expert = pl.BlockSpec((own, tile, ff), lambda i: (0, i, 0))
    return pl.pallas_call(
        functools.partial(expert_kernel, experts, own, 512),
        grid=(rows // tile,),
        in_specs=[
            by_row, by_expert, by_lane,
            pl.BlockSpec((width, LANES), lambda i: (0, 0)),
            pl.BlockSpec(pick.shape, lambda i: (0, 0)),
            pl.BlockSpec(memory_space=pl.ANY),
            pl.BlockSpec(memory_space=pl.ANY),
        ],
        out_specs=[by_expert] * 3 + [by_row, by_lane],
        out_shape=[jax.ShapeDtypeStruct((own, rows, ff), BF16)] * 3
        + [jax.ShapeDtypeStruct((rows, width), BF16), jax.ShapeDtypeStruct((rows, LANES), BF16)],
        scratch_shapes=[
            pltpu.VMEM((own, width, ff), BF16),
            pltpu.VMEM((own, width, ff), BF16),
            pltpu.SemaphoreType.DMA((2, own)),
        ],
        compiler_params=pltpu.CompilerParams(vmem_limit_bytes=56 * MIB),
        cost_estimate=pl.CostEstimate(
            flops=8 * rows * width * ff * own, bytes_accessed=40 * MIB, transcendentals=0
        ),
    )(x, d_hid, member, router_w, pick, w_gate, w_up)


def grad_kernel(n, count, table, *refs):
    lefts, rights, outs = refs[:n], refs[n : n + n * count], refs[len(refs) - count :]
    for k, out in enumerate(outs):
        total = None
        for h in range(n):
            left = lefts[h]
            left = left[0] if len(left.shape) == 3 else left[...]
            right = rights[k * n + h]
            right = right[0] if len(right.shape) == 3 else right[...]
            part = t_mm(left, right)
            total = part if total is None else total + part
        out[...] = total.astype(BF16)


def expert_grads(table, lefts, rights, block, j, earlier=()):
    n = len(lefts)

    def left_spec(a):
        if a.ndim == 3:
            return pl.BlockSpec((1, a.shape[1], block), lambda i, t: (j, 0, t[i]))
        return pl.BlockSpec((a.shape[0], block), lambda i, t: (0, t[i]))

    def right_spec(a):
        if a.ndim == 3:
            return pl.BlockSpec((1,) + a.shape[1:], lambda i, t: (j, 0, 0))
        return pl.BlockSpec(a.shape, lambda i, t: (0, 0))

    flat = [a for group in rights for a in group]
    blocks = table.shape[0]
    outs = [jax.ShapeDtypeStruct((blocks * block, g[0].shape[-1]), BF16) for g in rights]
    depth = sum(a.shape[-2] for a in lefts)
    return pl.pallas_call(
        functools.partial(grad_kernel, n, len(rights)),
        grid_spec=pltpu.PrefetchScalarGridSpec(
            num_scalar_prefetch=1,
            grid=(blocks,),
            in_specs=[left_spec(a) for a in lefts]
            + [right_spec(a) for a in flat]
            + [pl.BlockSpec(memory_space=pl.ANY)] * len(earlier),
            out_specs=[pl.BlockSpec((block, o.shape[1]), lambda i, t: (i, 0)) for o in outs],
        ),
        out_shape=outs,
        compiler_params=pltpu.CompilerParams(vmem_limit_bytes=56 * MIB),
        cost_estimate=pl.CostEstimate(
            flops=sum(2 * depth * o.shape[0] * o.shape[1] for o in outs),
            bytes_accessed=16 * MIB,
            transcendentals=0,
        ),
    )(table, *lefts, *flat, *earlier)


def out_kernel(own, hid_ref, w_ref, *refs):
    total = mm(hid_ref[0], w_ref[0])
    for j in range(1, own):
        total = total + mm(hid_ref[j], w_ref[j])
    refs[-1][...] = total.astype(BF16)


def experts_out(hid, w_down, earlier=()):
    own, rows, ff = hid.shape
    width = w_down.shape[2]
    tile = 512
    return pl.pallas_call(
        functools.partial(out_kernel, own),
        grid=(width // tile,),
        in_specs=[
            pl.BlockSpec((own, rows, ff), lambda i: (0, 0, 0)),
            pl.BlockSpec((own, ff, tile), lambda i: (0, 0, i)),
        ]
        + [pl.BlockSpec(memory_space=pl.ANY)] * len(earlier),
        out_specs=pl.BlockSpec((rows, tile), lambda i: (0, i)),
        out_shape=jax.ShapeDtypeStruct((rows, width), BF16),
        compiler_params=pltpu.CompilerParams(vmem_limit_bytes=48 * MIB),
        cost_estimate=pl.CostEstimate(
            flops=2 * own * rows * ff * width, bytes_accessed=16 * MIB, transcendentals=0
        ),
    )(hid, w_down, *earlier)


def mid_kernel(n, x_ref, own_ref, gain_ref, *refs):
    total = x_ref[...].astype(F32) + own_ref[...]
    for got in refs[: n - 1]:
        total = total + got[...].astype(F32)
    res_ref, scale_ref, low_ref = refs[-3:]
    scale = lax.rsqrt(jnp.mean(total * total, axis=1, keepdims=True) + EPSILON)
    res_ref[...] = total
    scale_ref[...] = scale
    low_ref[...] = (total * scale * gain_ref[...]).astype(BF16)


def middle(x, own_block, got, gain, earlier):
    rows, width = x.shape
    whole = pl.BlockSpec(memory_space=pltpu.VMEM)
    return pl.pallas_call(
        functools.partial(mid_kernel, len(got) + 1),
        in_specs=[whole] * (3 + len(got)) + [pl.BlockSpec(memory_space=pl.ANY)] * len(earlier),
        out_specs=[whole] * 3,
        out_shape=[
            jax.ShapeDtypeStruct((rows, width), F32),
            jax.ShapeDtypeStruct((rows, 1), F32),
            jax.ShapeDtypeStruct((rows, width), BF16),
        ],
        compiler_params=pltpu.CompilerParams(vmem_limit_bytes=32 * MIB),
    )(x, own_block, gain[None], *got, *earlier)


def res_kernel(res_ref, scale_ref, gain_ref, grad_ref, mid_ref, *refs):
    out_ref, low_ref, gain_out = refs[-3:]
    rows, scale = res_ref[...], scale_ref[...]
    grad_in = mid_ref[...].astype(F32)
    weighted = grad_in * gain_ref[...]
    inner = jnp.mean(weighted * rows, axis=1, keepdims=True)
    total = grad_ref[...] + scale * weighted - rows * (scale * scale * scale) * inner
    out_ref[...] = total
    low_ref[...] = total.astype(BF16)
    gain_out[...] = jnp.sum(grad_in * rows * scale, axis=0, keepdims=True)


def residual_back(residual, scale, gain, grad, d_mid, earlier):
    rows, width = residual.shape
    whole = pl.BlockSpec(memory_space=pltpu.VMEM)
    return pl.pallas_call(
        res_kernel,
        in_specs=[whole] * 5 + [pl.BlockSpec(memory_space=pl.ANY)] * len(earlier),
        out_specs=[whole] * 3,
        out_shape=[
            jax.ShapeDtypeStruct((rows, width), F32),
            jax.ShapeDtypeStruct((rows, width), BF16),
            jax.ShapeDtypeStruct((1, width), F32),
        ],
        compiler_params=pltpu.CompilerParams(vmem_limit_bytes=32 * MIB),
    )(residual, scale, gain[None], grad, d_mid, *earlier)


def meet(peers):
    barrier = pltpu.get_barrier_semaphore()
    for peer in peers:
        pl.semaphore_signal(barrier, inc=1, device_id=peer, device_id_type=pl.DeviceIdType.MESH)
    pl.semaphore_wait(barrier, len(peers))


def ctx_sum_kernel(n, x_ref, out_ref, slots, send, recv):
    me = lax.axis_index("ctx")
    peers = [{"ctx": lax.rem(me + d, n)} for d in range(1, n)]
    meet(peers)
    slots[me] = x_ref[...]
    copies = [
        pltpu.make_async_remote_copy(
            src_ref=x_ref, dst_ref=slots.at[me], send_sem=send.at[d], recv_sem=recv.at[d],
            device_id=peer, device_id_type=pl.DeviceIdType.MESH,
        )
        for d, peer in enumerate(peers)
    ]
    for copy in copies:
        copy.start()
    for copy in copies:
        copy.wait()
    total = slots[0]
    for k in range(1, n):
        total = total + slots[k]
    out_ref[...] = total


def ctx_sum(x, number):
    n = lax.axis_size("ctx")
    whole = pl.BlockSpec(memory_space=pltpu.VMEM)
    return pl.pallas_call(
        functools.partial(ctx_sum_kernel, n),
        in_specs=[whole],
        out_specs=whole,
        out_shape=jax.ShapeDtypeStruct(x.shape, F32),
        scratch_shapes=[
            pltpu.VMEM((n,) + x.shape, F32),
            pltpu.SemaphoreType.DMA((n - 1,)),
            pltpu.SemaphoreType.DMA((n - 1,)),
        ],
        compiler_params=pltpu.CompilerParams(collective_id=number, has_side_effects=True),
    )(x)


def all_sum_kernel(n_ctx, n_exp, x_ref, *refs):
    out_ref, first, second, sems = refs[-4:]
    c_at, e_at = lax.axis_index("ctx"), lax.axis_index("exp")
    across = [{"exp": lax.rem(e_at + d, n_exp)} for d in range(1, n_exp)]
    along = [{"ctx": lax.rem(c_at + d, n_ctx)} for d in range(1, n_ctx)]
    meet(across + along)
    first[e_at] = x_ref[e_at]
    copies = [
        pltpu.make_async_remote_copy(
            src_ref=x_ref.at[peer["exp"]], dst_ref=first.at[e_at],
            send_sem=sems.at[0, d], recv_sem=sems.at[1, d],
            device_id=peer, device_id_type=pl.DeviceIdType.MESH,
        )
        for d, peer in enumerate(across)
    ]
    for copy in copies:
        copy.start()
    for copy in copies:
        copy.wait()
    total = first[0]
    for k in range(1, n_exp):
        total = total + first[k]
    second[c_at] = total
    copies = [
        pltpu.make_async_remote_copy(
            src_ref=second.at[c_at], dst_ref=second.at[c_at],
            send_sem=sems.at[2, d], recv_sem=sems.at[3, d],
            device_id=peer, device_id_type=pl.DeviceIdType.MESH,
        )
        for d, peer in enumerate(along)
    ]
    for copy in copies:
        copy.start()
    for copy in copies:
        copy.wait()
    total = second[0]
    for k in range(1, n_ctx):
        total = total + second[k]
    out_ref[...] = total


def all_sum(x, number, earlier):
    n_ctx, n_exp = lax.axis_size("ctx"), lax.axis_size("exp")
    whole = pl.BlockSpec(memory_space=pltpu.VMEM)
    return pl.pallas_call(
        functools.partial(all_sum_kernel, n_ctx, n_exp),
        in_specs=[whole] + [pl.BlockSpec(memory_space=pl.ANY)] * len(earlier),
        out_specs=whole,
        out_shape=jax.ShapeDtypeStruct(x.shape[1:], F32),
        scratch_shapes=[
            pltpu.VMEM(x.shape, F32),
            pltpu.VMEM((n_ctx,) + x.shape[1:], F32),
            pltpu.SemaphoreType.DMA((4, max(n_ctx, n_exp) - 1)),
        ],
        compiler_params=pltpu.CompilerParams(collective_id=number, has_side_effects=True),
    )(x, *earlier)


def gather(block, axis):
    return lax.all_gather(block, axis, axis=0, tiled=True)


def scatter_sum(block, axis, dimension=0):
    return lax.psum_scatter(block, axis, scatter_dimension=dimension, tiled=True)


def after(value, *earlier):
    return lax.optimization_barrier((value,) + earlier)[0]


def swap(block, bits):
    n = lax.axis_size("ctx")
    return lax.ppermute(block, "ctx", [(i, i ^ bits) for i in range(n)])


def take(block, at, size=1, axis=0):
    return lax.dynamic_slice_in_dim(block, at, size, axis)


def gather_ctx(block, axis):
    n, me = lax.axis_size("ctx"), lax.axis_index("ctx")
    parts = [block] + [swap(block, d) for d in range(1, n)]
    shape = block.shape[:axis] + (n,) + block.shape[axis:]
    out = jnp.zeros(shape, block.dtype)
    for d, piece in enumerate(parts):
        out = lax.dynamic_update_slice_in_dim(out, jnp.expand_dims(piece, axis), me ^ d, axis)
    return out


def halving_masks(order):
    masks = [0]
    for bit in order[::-1]:
        masks = masks + [m | (1 << bit) for m in masks]
    return masks


def halve(keep, got, order):
    bits = list(order[1:])
    while True:
        total = keep.astype(F32) + got.astype(F32)
        if not bits:
            return total
        total = total.astype(BF16)
        rows = total.shape[0] // 2
        keep, got = total[:rows], swap(total[rows:], 1 << bits.pop(0))


def local(
    tokens, cotangent, lengths, span_order, routes,
    w_query, w_key, w_value, w_output, w_router,
    gain_attn, gain_query, gain_key, gain_mlp,
    w_gate, w_up, w_down,
):
    n_ctx, n_exp = lax.axis_size("ctx"), lax.axis_size("exp")
    c_at, e_at = lax.axis_index("ctx"), lax.axis_index("exp")
    rows = tokens.shape[1]
    width = tokens.shape[2]
    seq = rows * n_ctx
    cols = width // n_ctx
    shard = width // n_exp
    own = w_gate.shape[0]
    ff = w_gate.shape[2]
    experts = w_router.shape[1]
    seq_length = lengths[0]
    halves = 2
    part = rows // halves
    half_seq = part * n_ctx

    chunk = width // (n_ctx * n_exp)
    moves = []
    for g in range(n_ctx * n_exp):
        source = (g % n_ctx) * n_exp + g // n_ctx
        moves.append((source, g))
    out_piece = lax.ppermute(take(w_output, c_at * chunk, chunk), ("ctx", "exp"), moves)

    x_low = gather_ctx(tokens[0].reshape(halves, part, width), 1).reshape(seq, width)
    storage = jnp.arange(seq, dtype=jnp.int32)
    storage = (storage % half_seq // part) * rows + storage // half_seq * part + storage % part
    positions = positions_of(span_order, storage, rows // 2)
    my_positions = positions_of(
        span_order, c_at * rows + jnp.arange(rows, dtype=jnp.int32), rows // 2
    )
    valid = (my_positions < seq_length).astype(F32)[:, None]
    member = jnp.sum(
        (routes[0][:, :, None] == jnp.arange(LANES, dtype=jnp.int32)[None, None, :]).astype(BF16),
        axis=1,
    )
    small = jnp.concatenate(
        [
            w_router.reshape(-1), gain_attn, gain_query, gain_key, gain_mlp,
            member[:, :experts].reshape(-1),
        ]
    )
    small_all = gather(small[None], "exp")
    at = shard * experts
    router_w = small_all[:, :at].reshape(width, experts)
    router_w = jnp.pad(router_w, ((0, 0), (0, LANES - experts)))
    gains = []
    for _ in range(4):
        gains.append(small_all[:, at : at + shard].reshape(width).astype(F32))
        at += shard
    attn_gain, query_gain_all, key_gain_all, mlp_gain = gains
    member_all = small_all[:, at:].reshape(n_exp, rows, experts)
    member_all = jnp.pad(member_all, ((0, 0), (0, 0), (0, LANES - experts)))
    query_gain = take(query_gain_all, c_at * cols, cols)
    key_gain = take(key_gain_all, c_at * cols, cols)

    qkv_piece = jnp.concatenate(
        [take(w, c_at * cols, cols, 1) for w in (w_query, w_key, w_value)], axis=1
    )
    qkv_w = gather(qkv_piece, "exp")
    out_w = gather(out_piece, "exp")
    x_all = x_low.astype(F32)

    grad_mine = cotangent[0].astype(F32) * valid
    grad_low = grad_mine.astype(BF16)
    grad_parts = [gather(grad_low[h * part : (h + 1) * part], "exp") for h in range(halves)]
    d_hid_parts = [
        jnp.stack([mm_t(g, w_down[j]).astype(BF16) for j in range(own)]) for g in grad_parts
    ]

    cosine, sine = rope_tables(positions)
    xn = (x_all * rms_scale(x_all) * attn_gain).astype(BF16)
    qkv = mm(xn, qkv_w)
    qp, kp = qkv[:, :cols], qkv[:, cols : 2 * cols]
    squares = jnp.stack([jnp.sum(qp * qp, axis=-1), jnp.sum(kp * kp, axis=-1)], axis=0)
    squares = ctx_sum(jnp.pad(squares, ((0, 6), (0, 0))), 0)[:2] / width
    q_scale = lax.rsqrt(squares[0] + EPSILON)[:, None]
    k_scale = lax.rsqrt(squares[1] + EPSILON)[:, None]
    key_positions = jnp.where(positions < seq_length, positions, jnp.int32(1 << 30))
    base = (
        qkv, qkv, qkv, q_scale, k_scale, query_gain[None], key_gain[None],
        cosine, sine, cosine, sine, positions[:, None], key_positions[None],
    )

    attended_parts, mids, residual_parts, scale_parts = [], [], [], []
    for h in range(halves):
        attended = attend(base, half_seq, h)
        attended_parts.append(attended)
        got = []
        for d in range(n_ctx - 1, -1, -1):
            block = mm(take(attended, (c_at ^ d) * part, part), out_w)
            if d:
                got.append(swap(block.astype(BF16), d))
        residual, scale, mid = middle(
            tokens[0, h * part : (h + 1) * part], block, got, mlp_gain, grad_parts[-1:]
        )
        residual_parts.append(residual)
        scale_parts.append(scale)
        mids.append(gather(mid, "exp"))

    lane = jnp.arange(LANES, dtype=jnp.int32)[None, :]
    pick = (lane == e_at * own + jnp.arange(max(own, 8), dtype=jnp.int32)[:, None]).astype(F32)
    hid_parts, da_parts, db_parts, coef_parts = [], [], [], []
    dxs = []
    for h in range(halves):
        member_h = member_all[:, h * part : (h + 1) * part].reshape(n_exp * part, LANES)
        hid, da, db, dx, coef = expert_pass(
            mids[h], d_hid_parts[h], member_h, router_w, pick, w_gate, w_up, experts
        )
        hid_parts.append(hid)
        da_parts.append(da)
        db_parts.append(db)
        coef_parts.append(coef)
        dxs.append(dx)
    d_mids = [scatter_sum(after(dx, mids[-1]), "exp") for dx in dxs]

    def back_to_rows(h, *earlier):
        d_residual, low, g_gain = residual_back(
            residual_parts[h], scale_parts[h], mlp_gain,
            grad_mine[h * part : (h + 1) * part], d_mids[h], earlier,
        )
        dl = gather_ctx(low, 0).reshape(half_seq, width)
        return d_residual, low, g_gain, dl

    g_router = sum(t_mm(c, m) for m, c in zip(mids, coef_parts))[:experts]

    bits = list(range(n_ctx.bit_length() - 1))
    orders = [bits if j % 2 == 0 else bits[::-1] for j in range(own)]
    cut = n_ctx // 2
    tables = [c_at ^ jnp.asarray(halving_masks(order), jnp.int32) for order in orders]

    def down_grads(j, table, *earlier):
        return expert_grads(table, hid_parts, [grad_parts], ff // n_ctx, j, earlier)[0]

    def up_grads(j, table, *earlier):
        return expert_grads(table, mids, [da_parts, db_parts], width // n_ctx, j, earlier)

    d_res0, low0, gain0, dl0 = back_to_rows(0, dxs[-1])
    give_down = [down_grads(j, tables[j][cut:], low0) for j in range(own)]
    y_parts = [experts_out(hid_parts[0], w_down, give_down)]
    give_up = [up_grads(j, tables[j][cut:], y_parts[0]) for j in range(own)]
    d_res1, low1, gain1, dl1 = back_to_rows(1, *[g[0] for g in give_up])
    y_parts.append(experts_out(hid_parts[1], w_down, (low1,)))
    g_mid_gain = gain0 + gain1
    d_res_parts, dl_parts = [d_res0, d_res1], [dl0, dl1]
    d_att_parts = [mm_t(dl, out_w).astype(BF16) for dl in dl_parts]
    firsts = [1 << order[0] for order in orders]
    got_down = [swap(give_down[j], firsts[j]) for j in range(own)]
    got_gate = [swap(give_up[j][0], firsts[j]) for j in range(own)]
    got_up = [swap(give_up[j][1], firsts[j]) for j in range(own)]
    g_out = expert_grads(
        jnp.zeros((1,), jnp.int32), attended_parts, [dl_parts], cols, 0, (y_parts[1],)
    )[0].reshape(n_exp, chunk, width)

    dq_parts = []
    dk_n = jnp.zeros((seq, cols), F32)
    dv = jnp.zeros((seq, cols), F32)
    dq, dk_n, dv = attend_back(base, half_seq, 0, d_att_parts[0], dk_n, dv, (y_parts[1],))
    dq_parts.append(dq)
    keep_down = [down_grads(j, tables[j][:cut], dq) for j in range(own)]
    dq, dk_n, dv = attend_back(
        base, half_seq, 1, d_att_parts[1], dk_n, dv, (*keep_down, *got_down)
    )
    dq_parts.append(dq)
    dq_n = jnp.concatenate(dq_parts, axis=0)
    inner = jnp.stack(
        [
            jnp.sum(dq_n * query_gain * qp, axis=-1),
            jnp.sum(dk_n * key_gain * kp, axis=-1),
        ],
        axis=0,
    )
    inner = ctx_sum(jnp.pad(inner, ((0, 6), (0, 0))), 1)[:2] / width
    dqp = q_scale * dq_n * query_gain - qp * (q_scale**3) * inner[0][:, None]
    dkp = k_scale * dk_n * key_gain - kp * (k_scale**3) * inner[1][:, None]
    g_query_gain = jnp.sum(dq_n * qp * q_scale, axis=0)
    g_key_gain = jnp.sum(dk_n * kp * k_scale, axis=0)
    d_qkv = jnp.concatenate([dqp.astype(BF16), dkp.astype(BF16), dv.astype(BF16)], axis=1)
    d_blocks = d_qkv.reshape(halves, n_ctx, part, 3 * cols)
    dxn = 0.0
    for d in range(n_ctx - 1, -1, -1):
        block = mm_t(take(d_blocks, c_at ^ d, 1, 1).reshape(rows, 3 * cols), qkv_w)
        dxn = dxn + (swap(block.astype(BF16), d).astype(F32) if d else block)
    block_input = tokens[0].astype(F32)
    in_scale = rms_scale(block_input)
    d_in_norm, g_attn_gain = rms_backward(block_input, in_scale, attn_gain, dxn)
    d_tokens = (jnp.concatenate(d_res_parts, axis=0) + d_in_norm).astype(BF16)

    g_qkv = expert_grads(
        jnp.arange(n_ctx, dtype=jnp.int32), [xn], [[d_qkv]], width // n_ctx, 0, got_gate
    )[0]
    keep_up = [up_grads(j, tables[j][:cut], g_qkv) for j in range(own)]
    g_down = jnp.stack([halve(keep_down[j], got_down[j], orders[j]) for j in range(own)])
    g_gate = jnp.stack([halve(keep_up[j][0], got_gate[j], orders[j]) for j in range(own)])
    g_up = jnp.stack([halve(keep_up[j][1], got_up[j], orders[j]) for j in range(own)])
    g_both = jnp.concatenate(
        [g_qkv.reshape(n_exp, shard * 3 * cols), g_out.reshape(n_exp, chunk * width)], axis=1
    )
    g_both = scatter_sum(g_both.reshape(-1, width), "exp").reshape(-1)
    g_qkv = g_both[: shard * 3 * cols].reshape(shard, 3 * cols)
    g_out = g_both[shard * 3 * cols :].reshape(chunk, width)
    mixed_parts = []
    for h in range(halves):
        y = scatter_sum(y_parts[h], "exp").astype(F32)
        mixed_parts.append((residual_parts[h] + y).astype(BF16))
    mixed = jnp.concatenate(mixed_parts, axis=0)
    g_full = [jnp.zeros((shard, width), F32) for _ in range(3)]
    for d in range(n_ctx):
        piece = (swap(g_qkv, d) if d else g_qkv).astype(F32)
        for k in range(3):
            g_full[k] = lax.dynamic_update_slice_in_dim(
                g_full[k], piece[:, k * cols : (k + 1) * cols], (c_at ^ d) * cols, 1
            )
    g_out = lax.ppermute(g_out, ("ctx", "exp"), [(b, a) for a, b in moves])
    g_out = gather(g_out, "ctx").astype(F32)

    gain_grads = [g_attn_gain[None], g_mid_gain]
    for piece in (g_query_gain, g_key_gain):
        gain_grads.append(
            lax.dynamic_update_slice_in_dim(jnp.zeros((1, width), F32), piece[None], c_at * cols, 1)
        )
    spare = -(experts + 4) % 8
    smalls = jnp.concatenate([g_router] + gain_grads + [jnp.zeros((spare, width), F32)], axis=0)
    smalls = smalls.reshape(-1, n_exp, shard).transpose(1, 0, 2)
    smalls = all_sum(smalls, 2, (g_up,))
    return (
        mixed[None], d_tokens[None],
        g_full[0], g_full[1], g_full[2], g_out,
        smalls[:experts].T,
        smalls[experts], smalls[experts + 2], smalls[experts + 3], smalls[experts + 1],
        g_gate, g_up, g_down,
    )


def solution(mesh):
    tok = P("exp", "ctx", None)
    two, three, one = P("exp", None), P("exp", None, None), P("exp")
    return jax.shard_map(
        local,
        mesh=mesh,
        in_specs=(tok, tok, one, P(), tok) + (two,) * 5 + (one,) * 4 + (three,) * 3,
        out_specs=(tok, tok) + (two,) * 5 + (one,) * 4 + (tok,) * 3,
        check_vma=False,
    )
```

```python
import functools
import math

import jax
import jax.numpy as jnp
from jax import lax
from jax.experimental import pallas as pl
from jax.experimental.pallas import tpu as pltpu
from jax.sharding import PartitionSpec as P

HEADS = 16
HEAD_DIM = 128
LANES = 128
EPSILON = 1e-05
ROPE_BASE = 10000.0
MASKED_SCORE = -1e30
FACTOR = HEAD_DIM ** (-0.5)
F32 = jnp.float32
BF16 = jnp.bfloat16
MIB = 1 << 20


def mm(left, right):
    return jnp.dot(left, right, preferred_element_type=F32)


def mm_t(left, right):
    return lax.dot_general(left, right, (((1,), (1,)), ((), ())), preferred_element_type=F32)


def t_mm(left, right):
    return lax.dot_general(left, right, (((0,), (0,)), ((), ())), preferred_element_type=F32)


def rms_scale(rows):
    return lax.rsqrt(jnp.mean(rows * rows, axis=-1, keepdims=True) + EPSILON)


def rms_backward(rows, inv_scale, gain_vec, grad_in):
    weighted = grad_in * gain_vec
    inner_mean = jnp.mean(weighted * rows, axis=-1, keepdims=True)
    d_rows = inv_scale * weighted - rows * (inv_scale * inv_scale * inv_scale) * inner_mean
    return d_rows, jnp.sum(grad_in * rows * inv_scale, axis=0)


def rope_tables(positions):
    half_dim = HEAD_DIM // 2
    frequency = jnp.exp(
        jnp.arange(half_dim, dtype=F32) * (-2.0 * math.log(ROPE_BASE) / HEAD_DIM)
    )
    angle = positions.astype(F32)[:, None] * frequency[None, :]
    cosine, sine = jnp.cos(angle), jnp.sin(angle)
    return (
        jnp.concatenate([cosine, cosine], axis=1),
        jnp.concatenate([-sine, sine], axis=1),
    )


def positions_of(span_order, storage, span_length):
    return jnp.take(span_order, storage // span_length) * span_length + storage % span_length


def rotated(rows, scale, gain, cosine, sine):
    normed = rows * scale * gain
    return (normed * cosine + pltpu.roll(normed, HEAD_DIM // 2, 1) * sine).astype(BF16)


def unrotated(rows, cosine, sine):
    return rows * cosine - pltpu.roll(rows, HEAD_DIM // 2, 1) * sine


def head_probs(query, key, q_pos, k_pos):
    scores = jnp.where(k_pos <= q_pos, mm_t(query, key) * FACTOR, MASKED_SCORE)
    expo = jnp.exp(scores - jnp.max(scores, axis=1, keepdims=True))
    return expo / jnp.sum(expo, axis=1, keepdims=True)


def attend_kernel(
    q_ref, k_ref, v_ref, qs_ref, ks_ref, qg_ref, kg_ref, qc_ref, qn_ref, kc_ref, kn_ref,
    qp_ref, kp_ref, out_ref,
):
    query = rotated(q_ref[...], qs_ref[...], qg_ref[...], qc_ref[...], qn_ref[...])
    key = rotated(k_ref[...], ks_ref[...], kg_ref[...], kc_ref[...], kn_ref[...])
    probs = head_probs(query, key, qp_ref[...], kp_ref[...])
    out_ref[...] = mm(probs.astype(BF16), v_ref[...].astype(BF16)).astype(BF16)


def attend_back_kernel(
    q_ref, k_ref, v_ref, qs_ref, ks_ref, qg_ref, kg_ref, qc_ref, qn_ref, kc_ref, kn_ref,
    qp_ref, kp_ref, da_ref, dk_in, dv_in, *refs,
):
    dq_ref, dk_ref, dv_ref = refs[-3:]
    query = rotated(q_ref[...], qs_ref[...], qg_ref[...], qc_ref[...], qn_ref[...])
    key = rotated(k_ref[...], ks_ref[...], kg_ref[...], kc_ref[...], kn_ref[...])
    probs = head_probs(query, key, qp_ref[...], kp_ref[...])
    d_att = da_ref[...]
    d_probs = mm_t(d_att, v_ref[...].astype(BF16))
    inner = jnp.sum(probs * d_probs, axis=1, keepdims=True)
    d_scores = (probs * (d_probs - inner)).astype(BF16)
    dq_ref[...] = unrotated(mm(d_scores, key) * FACTOR, qc_ref[...], qn_ref[...])
    dk = unrotated(t_mm(d_scores, query) * FACTOR, kc_ref[...], kn_ref[...])
    dk_ref[...] = dk_in[...] + dk
    dv_ref[...] = dv_in[...] + t_mm(probs.astype(BF16), d_att)


def attention_specs(rows, seq, heads, h):
    def head_rows(n, at, row=0):
        return pl.BlockSpec((n, HEAD_DIM), lambda i: (row, at + i))

    def fixed(shape, row=0):
        return pl.BlockSpec(shape, lambda i: (row, 0))

    return [
        head_rows(rows, 0, h), head_rows(seq, heads), head_rows(seq, 2 * heads),
        fixed((rows, 1), h), fixed((seq, 1)), head_rows(1, 0), head_rows(1, 0),
        fixed((rows, HEAD_DIM), h), fixed((rows, HEAD_DIM), h),
        fixed((seq, HEAD_DIM)), fixed((seq, HEAD_DIM)),
        fixed((rows, 1), h), fixed((1, seq)),
    ]


def attend(base, rows, h):
    seq, cols = base[0].shape[0], base[0].shape[1] // 3
    heads = cols // HEAD_DIM
    return pl.pallas_call(
        attend_kernel,
        grid=(heads,),
        in_specs=attention_specs(rows, seq, heads, h),
        out_specs=pl.BlockSpec((rows, HEAD_DIM), lambda i: (0, i)),
        out_shape=jax.ShapeDtypeStruct((rows, cols), BF16),
        compiler_params=pltpu.CompilerParams(vmem_limit_bytes=48 * MIB),
        cost_estimate=pl.CostEstimate(
            flops=4 * rows * seq * cols, bytes_accessed=8 * MIB, transcendentals=rows * seq * heads
        ),
    )(*base)


def attend_back(base, rows, h, d_att, dk, dv, earlier):
    seq, cols = base[0].shape[0], base[0].shape[1] // 3
    heads = cols // HEAD_DIM
    q_out = pl.BlockSpec((rows, HEAD_DIM), lambda i: (0, i))
    k_out = pl.BlockSpec((seq, HEAD_DIM), lambda i: (0, i))
    return pl.pallas_call(
        attend_back_kernel,
        grid=(heads,),
        in_specs=attention_specs(rows, seq, heads, h)
        + [q_out, k_out, k_out]
        + [pl.BlockSpec(memory_space=pl.ANY)] * len(earlier),
        out_specs=[q_out, k_out, k_out],
        out_shape=[
            jax.ShapeDtypeStruct((rows, cols), F32),
            jax.ShapeDtypeStruct((seq, cols), F32),
            jax.ShapeDtypeStruct((seq, cols), F32),
        ],
        compiler_params=pltpu.CompilerParams(vmem_limit_bytes=48 * MIB),
        cost_estimate=pl.CostEstimate(
            flops=10 * rows * seq * cols, bytes_accessed=16 * MIB, transcendentals=rows * seq * heads
        ),
    )(*base, d_att, dk, dv, *earlier)


def expert_kernel(
    experts, own, step, x_ref, dh_ref, member_ref, router_ref, pick_ref, wg_hbm, wu_hbm,
    hid_ref, da_ref, db_ref, dx_ref, coef_ref, wg, wu, sems,
):
    i = pl.program_id(0)

    def loads(j):
        return (
            pltpu.make_async_copy(wg_hbm.at[j], wg.at[j], sems.at[0, j]),
            pltpu.make_async_copy(wu_hbm.at[j], wu.at[j], sems.at[1, j]),
        )

    @pl.when(i == 0)
    def _():
        for j in range(own):
            for copy in loads(j):
                copy.start()

    logits = mm(x_ref[...], router_ref[...])
    lane = lax.broadcasted_iota(jnp.int32, logits.shape, 1)
    logits = jnp.where(lane < experts, logits, MASKED_SCORE)
    expo = jnp.exp(logits - jnp.max(logits, axis=1, keepdims=True))
    router = expo / jnp.sum(expo, axis=1, keepdims=True)
    chosen = router * member_ref[...].astype(F32)
    coef = jnp.zeros_like(router)
    ff = wg.shape[2]
    for j in range(own):

        @pl.when(i == 0)
        def _():
            for copy in loads(j):
                copy.wait()

        pick = pick_ref[j : j + 1, :]
        gate = jnp.sum(chosen * pick, axis=1, keepdims=True)
        flow = jnp.zeros_like(gate)
        for f in range(0, ff, step):
            cut = slice(f, f + step)
            a = mm(x_ref[...], wg[j, :, cut])
            b = mm(x_ref[...], wu[j, :, cut])
            d_hid = dh_ref[j, :, cut].astype(F32)
            sig = jax.nn.sigmoid(a)
            silu = a * sig
            hid = silu * b
            flow = flow + jnp.sum(hid * d_hid, axis=1, keepdims=True)
            hid_ref[j, :, cut] = (gate * hid).astype(BF16)
            d_hid = d_hid * gate
            da_ref[j, :, cut] = (d_hid * b * (sig + silu * (1.0 - sig))).astype(BF16)
            db_ref[j, :, cut] = (d_hid * silu).astype(BF16)
        coef = coef + flow * gate * (pick - router)
    low = coef.astype(BF16)
    coef_ref[...] = low
    width = x_ref.shape[1]
    for n in range(0, width, step):
        cut = slice(n, n + step)
        part = mm_t(low, router_ref[cut, :])
        for j in range(own):
            part = part + mm_t(da_ref[j], wg[j, cut, :]) + mm_t(db_ref[j], wu[j, cut, :])
        dx_ref[:, cut] = part.astype(BF16)


def expert_pass(x, d_hid, member, router_w, pick, w_gate, w_up, experts):
    rows, width = x.shape
    own, _, ff = w_gate.shape
    tile = 256
    by_row = pl.BlockSpec((tile, width), lambda i: (i, 0))
    by_lane = pl.BlockSpec((tile, LANES), lambda i: (i, 0))
    by_expert = pl.BlockSpec((own, tile, ff), lambda i: (0, i, 0))
    return pl.pallas_call(
        functools.partial(expert_kernel, experts, own, 512),
        grid=(rows // tile,),
        in_specs=[
            by_row, by_expert, by_lane,
            pl.BlockSpec((width, LANES), lambda i: (0, 0)),
            pl.BlockSpec(pick.shape, lambda i: (0, 0)),
            pl.BlockSpec(memory_space=pl.ANY),
            pl.BlockSpec(memory_space=pl.ANY),
        ],
        out_specs=[by_expert] * 3 + [by_row, by_lane],
        out_shape=[jax.ShapeDtypeStruct((own, rows, ff), BF16)] * 3
        + [jax.ShapeDtypeStruct((rows, width), BF16), jax.ShapeDtypeStruct((rows, LANES), BF16)],
        scratch_shapes=[
            pltpu.VMEM((own, width, ff), BF16),
            pltpu.VMEM((own, width, ff), BF16),
            pltpu.SemaphoreType.DMA((2, own)),
        ],
        compiler_params=pltpu.CompilerParams(vmem_limit_bytes=56 * MIB),
        cost_estimate=pl.CostEstimate(
            flops=8 * rows * width * ff * own, bytes_accessed=40 * MIB, transcendentals=0
        ),
    )(x, d_hid, member, router_w, pick, w_gate, w_up)


def weight_kernel(n, x_ref, d_ref, *refs):
    out_ref = refs[-1]
    width = d_ref.shape[1]
    out_ref[:, :width] = t_mm(x_ref[...], d_ref[...]).astype(BF16)
    total = t_mm(refs[0][...], refs[n][...])
    for h in range(1, n):
        total = total + t_mm(refs[h][...], refs[n + h][...])
    out_ref[:, width:] = total.astype(BF16)


def attention_grads(xn, d_qkv, attended, dl, cols, earlier):
    seq, width = xn.shape
    n = len(attended)

    def by_column(a):
        return pl.BlockSpec((a.shape[0], cols), lambda i: (0, i))

    def fixed(a):
        return pl.BlockSpec(a.shape, lambda i: (0, 0))

    return pl.pallas_call(
        functools.partial(weight_kernel, n),
        grid=(width // cols,),
        in_specs=[by_column(xn), fixed(d_qkv)]
        + [fixed(a) for a in attended]
        + [by_column(a) for a in dl]
        + [pl.BlockSpec(memory_space=pl.ANY)] * len(earlier),
        out_specs=pl.BlockSpec((cols, 4 * cols), lambda i: (i, 0)),
        out_shape=jax.ShapeDtypeStruct((width, 4 * cols), BF16),
        compiler_params=pltpu.CompilerParams(vmem_limit_bytes=48 * MIB),
        cost_estimate=pl.CostEstimate(
            flops=8 * seq * width * cols, bytes_accessed=20 * MIB, transcendentals=0
        ),
    )(xn, d_qkv, *attended, *dl, *earlier)


def partial_kernel(n, part, d_ref, w_ref, *refs):
    out_ref = refs[-1]
    rows, halves = n * part, d_ref.shape[0] // (n * part)
    for h in range(halves):
        total = mm_t(d_ref[h * rows : (h + 1) * rows, :], w_ref[...]).astype(BF16)
        for c in range(n):
            out_ref[0, c, h * part : (h + 1) * part, :] = total[c * part : (c + 1) * part, :]


def input_partial(d_qkv, weights, part, earlier):
    n = lax.axis_size("ctx")
    seq, depth = d_qkv.shape
    width = weights.shape[0]
    rows = seq // n
    return pl.pallas_call(
        functools.partial(partial_kernel, n, part),
        grid=(2,),
        in_specs=[
            pl.BlockSpec((seq, depth), lambda i: (0, 0)),
            pl.BlockSpec((width // 2, depth), lambda i: (i, 0)),
        ]
        + [pl.BlockSpec(memory_space=pl.ANY)] * len(earlier),
        out_specs=pl.BlockSpec((1, n, rows, width // 2), lambda i: (i, 0, 0, 0)),
        out_shape=jax.ShapeDtypeStruct((2, n, rows, width // 2), BF16),
        compiler_params=pltpu.CompilerParams(vmem_limit_bytes=48 * MIB),
    )(d_qkv, weights, *earlier)


def give_kernel(n, count, table, *refs):
    for k in range(count):
        total = t_mm(refs[0][...], refs[(k + 1) * n][0])
        for h in range(1, n):
            total = total + t_mm(refs[h][...], refs[(k + 1) * n + h][0])
        refs[len(refs) - count + k][0] = total.astype(BF16)


def given_grads(table, lefts, rights, block, j, earlier):
    n, blocks = len(lefts), table.shape[0]
    flat = [a for right in rights for a in right]
    columns = flat[0].shape[2]
    return pl.pallas_call(
        functools.partial(give_kernel, n, len(rights)),
        grid_spec=pltpu.PrefetchScalarGridSpec(
            num_scalar_prefetch=1,
            grid=(blocks,),
            in_specs=[pl.BlockSpec((a.shape[0], block), lambda i, t: (0, t[i])) for a in lefts]
            + [pl.BlockSpec((1,) + a.shape[1:], lambda i, t: (j, 0, 0)) for a in flat]
            + [pl.BlockSpec(memory_space=pl.ANY)] * len(earlier),
            out_specs=[pl.BlockSpec((1, block, columns), lambda i, t: (i, 0, 0))] * len(rights),
        ),
        out_shape=[jax.ShapeDtypeStruct((blocks, block, columns), BF16)] * len(rights),
        compiler_params=pltpu.CompilerParams(vmem_limit_bytes=48 * MIB),
    )(table, *lefts, *flat, *earlier)


def mid_kernel(n, x_ref, own_ref, gain_ref, *refs):
    total = x_ref[...].astype(F32) + own_ref[...]
    for got in refs[: n - 1]:
        total = total + got[...].astype(F32)
    res_ref, scale_ref, low_ref = refs[-3:]
    scale = lax.rsqrt(jnp.mean(total * total, axis=1, keepdims=True) + EPSILON)
    res_ref[...] = total
    scale_ref[...] = scale
    low_ref[...] = (total * scale * gain_ref[...]).astype(BF16)


def middle(x, own_block, got, gain, earlier):
    rows, width = x.shape
    whole = pl.BlockSpec(memory_space=pltpu.VMEM)
    return pl.pallas_call(
        functools.partial(mid_kernel, len(got) + 1),
        in_specs=[whole] * (3 + len(got)) + [pl.BlockSpec(memory_space=pl.ANY)] * len(earlier),
        out_specs=[whole] * 3,
        out_shape=[
            jax.ShapeDtypeStruct((rows, width), F32),
            jax.ShapeDtypeStruct((rows, 1), F32),
            jax.ShapeDtypeStruct((rows, width), BF16),
        ],
        compiler_params=pltpu.CompilerParams(vmem_limit_bytes=32 * MIB),
    )(x, own_block, gain[None], *got, *earlier)


def res_kernel(res_ref, scale_ref, gain_ref, grad_ref, mid_ref, *refs):
    out_ref, low_ref, gain_out = refs[-3:]
    rows, scale = res_ref[...], scale_ref[...]
    grad_in = mid_ref[...].astype(F32)
    weighted = grad_in * gain_ref[...]
    inner = jnp.mean(weighted * rows, axis=1, keepdims=True)
    total = grad_ref[...] + scale * weighted - rows * (scale * scale * scale) * inner
    out_ref[...] = total
    low_ref[...] = total.astype(BF16)
    gain_out[...] = jnp.sum(grad_in * rows * scale, axis=0, keepdims=True)


def residual_back(residual, scale, gain, grad, d_mid, earlier):
    rows, width = residual.shape
    whole = pl.BlockSpec(memory_space=pltpu.VMEM)
    return pl.pallas_call(
        res_kernel,
        in_specs=[whole] * 5 + [pl.BlockSpec(memory_space=pl.ANY)] * len(earlier),
        out_specs=[whole] * 3,
        out_shape=[
            jax.ShapeDtypeStruct((rows, width), F32),
            jax.ShapeDtypeStruct((rows, width), BF16),
            jax.ShapeDtypeStruct((1, width), F32),
        ],
        compiler_params=pltpu.CompilerParams(vmem_limit_bytes=32 * MIB),
    )(residual, scale, gain[None], grad, d_mid, *earlier)


def meet(peers):
    barrier = pltpu.get_barrier_semaphore()
    for peer in peers:
        pl.semaphore_signal(barrier, inc=1, device_id=peer, device_id_type=pl.DeviceIdType.MESH)
    pl.semaphore_wait(barrier, len(peers))


def ctx_sum_kernel(n, x_ref, *refs):
    out_ref, slots, send, recv = refs[-4:]
    me = lax.axis_index("ctx")
    peers = [{"ctx": lax.rem(me + d, n)} for d in range(1, n)]
    meet(peers)
    slots[me] = x_ref[...]
    copies = [
        pltpu.make_async_remote_copy(
            src_ref=x_ref, dst_ref=slots.at[me], send_sem=send.at[d], recv_sem=recv.at[d],
            device_id=peer, device_id_type=pl.DeviceIdType.MESH,
        )
        for d, peer in enumerate(peers)
    ]
    for copy in copies:
        copy.start()
    for copy in copies:
        copy.wait()
    total = slots[0]
    for k in range(1, n):
        total = total + slots[k]
    out_ref[...] = total


def ctx_sum(x, number, earlier=()):
    n = lax.axis_size("ctx")
    whole = pl.BlockSpec(memory_space=pltpu.VMEM)
    return pl.pallas_call(
        functools.partial(ctx_sum_kernel, n),
        in_specs=[whole] + [pl.BlockSpec(memory_space=pl.ANY)] * len(earlier),
        out_specs=whole,
        out_shape=jax.ShapeDtypeStruct(x.shape, F32),
        scratch_shapes=[
            pltpu.VMEM((n,) + x.shape, F32),
            pltpu.SemaphoreType.DMA((n - 1,)),
            pltpu.SemaphoreType.DMA((n - 1,)),
        ],
        compiler_params=pltpu.CompilerParams(collective_id=number, has_side_effects=True),
    )(x, *earlier)


class SmallSum:
    def __init__(self, n_ctx, n_exp, x, first, second, sems):
        self.x, self.first, self.second, self.sems = x, first, second, sems
        self.c_at, self.e_at = lax.axis_index("ctx"), lax.axis_index("exp")
        self.across = [{"exp": lax.rem(self.e_at + d, n_exp)} for d in range(1, n_exp)]
        self.along = [{"ctx": lax.rem(self.c_at + d, n_ctx)} for d in range(1, n_ctx)]

    def copy(self, src, dst, step, d, peer):
        return pltpu.make_async_remote_copy(
            src_ref=src, dst_ref=dst, send_sem=self.sems.at[2 * step, d],
            recv_sem=self.sems.at[2 * step + 1, d], device_id=peer,
            device_id_type=pl.DeviceIdType.MESH,
        )

    def over_exp(self):
        return [
            self.copy(self.x.at[peer["exp"]], self.first.at[self.e_at], 0, d, peer)
            for d, peer in enumerate(self.across)
        ]

    def over_ctx(self):
        mine = self.second.at[self.c_at]
        return [self.copy(mine, mine, 1, d, peer) for d, peer in enumerate(self.along)]

    def begin(self):
        for copy in self.over_exp():
            copy.start()
        self.first[self.e_at] = self.x[self.e_at]

    def pass_on(self):
        for copy in self.over_exp():
            copy.wait()
        total = self.first[0]
        for k in range(1, self.first.shape[0]):
            total = total + self.first[k]
        self.second[self.c_at] = total
        for copy in self.over_ctx():
            copy.start()

    def finish(self, out):
        for copy in self.over_ctx():
            copy.wait()
        total = self.second[0]
        for k in range(1, self.second.shape[0]):
            total = total + self.second[k]
        out[...] = total

    @staticmethod
    def scratch(n_ctx, shape):
        return [
            pltpu.VMEM(shape, F32),
            pltpu.VMEM((n_ctx,) + shape[1:], F32),
            pltpu.SemaphoreType.DMA((4, max(n_ctx, shape[0]) - 1)),
        ]


def halving_masks(order):
    masks = [0]
    for bit in order[::-1]:
        masks = masks + [m | (1 << bit) for m in masks]
    return masks


def flip(value, mask):
    bit = 0
    while mask >> bit:
        if (mask >> bit) & 1:
            value = value + (1 << bit) * (1 - 2 * lax.rem(lax.div(value, 1 << bit), 2))
        bit += 1
    return value


class Halving:
    def __init__(self, n, me, source, blocks, got, send, recv, out, first=None):
        self.n, self.me, self.source, self.blocks, self.got = n, me, source, blocks, got
        self.send, self.recv, self.out = send, recv, out
        self.first = first
        bits = list(range(n.bit_length() - 1))
        self.own = out.shape[0]
        self.orders = [bits if j % 2 == 0 else bits[::-1] for j in range(self.own)]
        self.masks = [halving_masks(order) for order in self.orders]
        self.steps = len(bits)

    def target(self, j, k):
        return flip(self.me, self.masks[j][k])

    def slot(self, s, k):
        return self.n - (self.n >> s) + k - (self.n >> (s + 1))

    def copy(self, j, s, k):
        given = self.source is not None and s == 0
        at = self.slot(s, k)
        return pltpu.make_async_remote_copy(
            src_ref=self.source.at[j, self.target(j, k)] if given else self.blocks.at[j, k - 1],
            dst_ref=self.got.at[j, at],
            send_sem=self.send.at[j, at],
            recv_sem=self.recv.at[j, at],
            device_id={"ctx": flip(self.me, 1 << self.orders[j][s])},
            device_id_type=pl.DeviceIdType.MESH,
        )

    def going(self, s):
        return [
            (j, k)
            for k in range((self.n >> s) - 1, (self.n >> (s + 1)) - 1, -1)
            for j in range(self.own)
        ]

    def begin(self, value=None):
        for j, k in self.going(0) if self.first is None else []:
            if value is not None:
                self.blocks[j, k - 1] = value(j, self.target(j, k)).astype(BF16)
            self.copy(j, 0, k).start()
        for k in range(self.n // 2 - 1, 0, -1):
            for j in range(self.own):
                at = self.target(j, k)
                mine = self.source[j, at] if value is None else value(j, at)
                self.blocks[j, k - 1] = mine.astype(BF16)

    def rest(self, value=None):
        for j in range(self.own):
            self.out[j] = self.source[j, self.me].astype(F32) if value is None else value(j, self.me)

    def arrived(self, j, k, steps):
        total = None
        for s in range(steps):
            sent = k + (self.n >> (s + 1))
            if s == 0 and self.first is not None:
                part = self.first[j][k].astype(F32)
            else:
                self.copy(j, s, sent).wait_recv()
                part = self.got[j, self.slot(s, sent)].astype(F32)
            total = part if total is None else total + part
        return total

    def pass_on(self):
        for s in range(1, self.steps):
            for j, k in self.going(s):
                total = self.blocks[j, k - 1].astype(F32) + self.arrived(j, k, s)
                self.blocks[j, k - 1] = total.astype(BF16)
                self.copy(j, s, k).start()

    def finish(self):
        for j in range(self.own):
            self.out[j] += self.arrived(j, 0, self.steps)
        for s in range(0 if self.first is None else 1, self.steps):
            for j, k in self.going(s):
                self.copy(j, s, k).wait_send()

    @staticmethod
    def scratch(own, n, rows, columns):
        return [
            pltpu.VMEM((own, n - 1, rows, columns), BF16),
            pltpu.VMEM((own, n - 1, rows, columns), BF16),
            pltpu.SemaphoreType.DMA((own, n - 1)),
            pltpu.SemaphoreType.DMA((own, n - 1)),
        ]


def ctx_peers(n, me):
    return [{"ctx": lax.rem(me + d, n)} for d in range(1, n)]


def entry(ref, j):
    return ref.at[j] if len(ref.shape) == 3 else ref


def product(lefts, rights, block):
    def value(j, at):
        total = None
        for left, right in zip(lefts, rights):
            columns = pl.ds(pl.multiple_of(at * block, LANES), block)
            part = t_mm(entry(left, j)[:, columns], entry(right, j)[...])
            total = part if total is None else total + part
        return total

    return value


def down_kernel(n, halves, *refs):
    hid, grad, w_down = refs[:halves], refs[halves : 2 * halves], refs[2 * halves]
    refs = refs[2 * halves + 1 :]
    out, ys, scratch = refs[0], refs[1 : 1 + halves], refs[1 + halves :]
    me = lax.axis_index("ctx")
    meet(ctx_peers(n, me))
    sums = Halving(n, me, None, *scratch, out)
    value = product(hid, grad, hid[0].shape[2] // n)
    sums.begin(value)
    sums.rest(value)
    width = w_down.shape[2]
    for h in range(halves):
        for start in range(0, width, 512):
            cut = slice(start, start + 512)
            total = mm(hid[h][0], w_down[0, :, cut])
            for j in range(1, w_down.shape[0]):
                total = total + mm(hid[h][j], w_down[j, :, cut])
            ys[h][:, cut] = total.astype(BF16)
    sums.pass_on()
    sums.finish()


def gate_kernel(n, halves, *refs):
    mids, pres = refs[:halves], refs[halves : 2 * halves]
    partial, out, dxn = refs[2 * halves], refs[-10], refs[-9]
    first = refs[2 * halves + 1 : 2 * halves + 1 + out.shape[0]]
    me = lax.axis_index("ctx")
    meet(ctx_peers(n, me))
    rows = Halving(n, me, partial, *refs[-8:-4], dxn)
    rows.begin()
    sums = Halving(n, me, None, *refs[-4:], out, first)
    value = product(mids, pres, mids[0].shape[1] // n)
    sums.begin(value)
    sums.pass_on()
    rows.pass_on()
    sums.rest(value)
    rows.rest()
    rows.finish()
    sums.finish()


def up_kernel(n, halves, *refs):
    mids, pres = refs[:halves], refs[halves : 2 * halves]
    piece, x = refs[2 * halves], refs[2 * halves + 1]
    out, *whole = refs[-16:-11]
    small_out, slots, send, recv = refs[-11:-7]
    me = lax.axis_index("ctx")
    smalls = SmallSum(n, x.shape[0], x, *refs[-7:-4])
    meet(smalls.across + smalls.along)
    smalls.begin()
    bits = list(range(n.bit_length() - 1))
    half = piece.shape[0] // 2

    def doubling(i, s):
        order = bits if i == 0 else bits[::-1]
        lines = pl.ds(i * half, half)
        copies = []
        for m in halving_masks(order[:s]):
            at = flip(me, m)
            sem = i, (1 << s) - 1 + len(copies)
            copies.append(
                pltpu.make_async_remote_copy(
                    src_ref=slots.at[at, lines] if m else piece.at[lines],
                    dst_ref=slots.at[at, lines],
                    send_sem=send.at[sem],
                    recv_sem=recv.at[sem],
                    device_id={"ctx": flip(me, 1 << order[s])},
                    device_id_type=pl.DeviceIdType.MESH,
                )
            )
        return copies

    first = refs[2 * halves + 2 : 2 * halves + 2 + out.shape[0]]
    sums = Halving(n, me, None, *refs[-4:], out, first)
    for i in range(2):
        for copy in doubling(i, 0):
            copy.start()
    value = product(mids, pres, mids[0].shape[1] // n)
    sums.begin(value)
    sums.pass_on()
    smalls.pass_on()
    slots[me] = piece[...]
    for s in range(1, len(bits)):
        for i in range(2):
            for copy in doubling(i, s - 1):
                copy.wait_recv()
            for copy in doubling(i, s):
                copy.start()
    sums.rest(value)
    smalls.finish(small_out)
    sums.finish()
    for i in range(2):
        for copy in doubling(i, len(bits) - 1):
            copy.wait_recv()
        for s in range(len(bits)):
            for copy in doubling(i, s):
                copy.wait_send()
    cols = piece.shape[1] // len(whole)
    for c in range(n):
        for k, ref in enumerate(whole):
            ref[:, c * cols : (c + 1) * cols] = slots[c, :, k * cols : (k + 1) * cols].astype(F32)


VMEM = pl.BlockSpec(memory_space=pltpu.VMEM)
ANY = pl.BlockSpec(memory_space=pl.ANY)


def exchange(kernel, number, operands, earlier, outs, scratch):
    n = lax.axis_size("ctx")
    return pl.pallas_call(
        kernel,
        in_specs=[VMEM] * len(operands) + [ANY] * len(earlier),
        out_specs=[VMEM] * len(outs),
        out_shape=outs,
        scratch_shapes=scratch,
        compiler_params=pltpu.CompilerParams(
            collective_id=number, has_side_effects=True, vmem_limit_bytes=60 * MIB
        ),
    )(*operands, *earlier)


def down_sums(hid, grad, w_down):
    n, halves = lax.axis_size("ctx"), len(hid)
    own, ff, width = w_down.shape
    outs = [jax.ShapeDtypeStruct((own, ff // n, width), F32)]
    outs += [jax.ShapeDtypeStruct((h.shape[1], width), BF16) for h in hid]
    return exchange(
        functools.partial(down_kernel, n, halves), 3, [*hid, *grad, w_down], (), outs,
        Halving.scratch(own, n, ff // n, width),
    )


def gate_sums(mids, pres, partial, first, earlier):
    n, halves = lax.axis_size("ctx"), len(mids)
    own, _, ff = pres[0].shape
    rows = mids[0].shape[1] // n
    shape = partial.shape
    outs = [
        jax.ShapeDtypeStruct((own, rows, ff), F32),
        jax.ShapeDtypeStruct((shape[0],) + shape[2:], F32),
    ]
    return exchange(
        functools.partial(gate_kernel, n, halves), 4, [*mids, *pres, partial, *first], earlier, outs,
        Halving.scratch(shape[0], n, *shape[2:]) + Halving.scratch(own, n, rows, ff),
    )


def up_sums(mids, pres, piece, smalls, first, earlier):
    n, halves = lax.axis_size("ctx"), len(mids)
    own, _, ff = pres[0].shape
    rows = mids[0].shape[1] // n
    shard, width = piece.shape
    outs = [jax.ShapeDtypeStruct((own, rows, ff), F32)]
    outs += [jax.ShapeDtypeStruct((shard, n * width // 4), F32) for _ in range(4)]
    outs += [jax.ShapeDtypeStruct(smalls.shape[1:], F32)]
    return exchange(
        functools.partial(up_kernel, n, halves), 5, [*mids, *pres, piece, smalls, *first], earlier,
        outs,
        [
            pltpu.VMEM((n,) + piece.shape, BF16),
            pltpu.SemaphoreType.DMA((2, n - 1)),
            pltpu.SemaphoreType.DMA((2, n - 1)),
        ]
        + SmallSum.scratch(n, smalls.shape)
        + Halving.scratch(own, n, rows, ff),
    )


def gather(block, axis):
    return lax.all_gather(block, axis, axis=0, tiled=True)


def scatter_sum(block, axis, dimension=0):
    return lax.psum_scatter(block, axis, scatter_dimension=dimension, tiled=True)


def after(value, *earlier):
    return lax.optimization_barrier((value,) + earlier)[0]


def swap(block, bits):
    n = lax.axis_size("ctx")
    return lax.ppermute(block, "ctx", [(i, i ^ bits) for i in range(n)])


def take(block, at, size=1, axis=0):
    return lax.dynamic_slice_in_dim(block, at, size, axis)


def gather_ctx(block, axis):
    n, me = lax.axis_size("ctx"), lax.axis_index("ctx")
    parts = [block] + [swap(block, d) for d in range(1, n)]
    shape = block.shape[:axis] + (n,) + block.shape[axis:]
    out = jnp.zeros(shape, block.dtype)
    for d, piece in enumerate(parts):
        out = lax.dynamic_update_slice_in_dim(out, jnp.expand_dims(piece, axis), me ^ d, axis)
    return out


def local(
    tokens, cotangent, lengths, span_order, routes,
    w_query, w_key, w_value, w_output, w_router,
    gain_attn, gain_query, gain_key, gain_mlp,
    w_gate, w_up, w_down,
):
    n_ctx, n_exp = lax.axis_size("ctx"), lax.axis_size("exp")
    c_at, e_at = lax.axis_index("ctx"), lax.axis_index("exp")
    rows = tokens.shape[1]
    width = tokens.shape[2]
    seq = rows * n_ctx
    cols = width // n_ctx
    shard = width // n_exp
    own = w_gate.shape[0]
    ff = w_gate.shape[2]
    experts = w_router.shape[1]
    seq_length = lengths[0]
    halves = 2
    part = rows // halves
    half_seq = part * n_ctx

    ratio = n_exp // n_ctx
    moves = []
    for c in range(n_ctx):
        for e in range(n_exp):
            moves.append(((e // ratio) * n_exp + c * ratio + e % ratio, c * n_exp + e))
    out_piece = lax.ppermute(take(w_output, c_at * cols, cols, 1), ("ctx", "exp"), moves)

    x_low = gather_ctx(tokens[0].reshape(halves, part, width), 1).reshape(seq, width)
    storage = jnp.arange(seq, dtype=jnp.int32)
    storage = (storage % half_seq // part) * rows + storage // half_seq * part + storage % part
    positions = positions_of(span_order, storage, rows // 2)
    my_positions = positions_of(
        span_order, c_at * rows + jnp.arange(rows, dtype=jnp.int32), rows // 2
    )
    valid = (my_positions < seq_length).astype(F32)[:, None]
    member = jnp.sum(
        (routes[0][:, :, None] == jnp.arange(LANES, dtype=jnp.int32)[None, None, :]).astype(BF16),
        axis=1,
    )
    small = jnp.concatenate(
        [
            w_router.reshape(-1), gain_attn, gain_query, gain_key, gain_mlp,
            member[:, :experts].reshape(-1),
        ]
    )
    small_all = gather(small[None], "exp")
    at = shard * experts
    router_w = small_all[:, :at].reshape(width, experts)
    router_w = jnp.pad(router_w, ((0, 0), (0, LANES - experts)))
    gains = []
    for _ in range(4):
        gains.append(small_all[:, at : at + shard].reshape(width).astype(F32))
        at += shard
    attn_gain, query_gain_all, key_gain_all, mlp_gain = gains
    member_all = small_all[:, at:].reshape(n_exp, rows, experts)
    member_all = jnp.pad(member_all, ((0, 0), (0, 0), (0, LANES - experts)))
    query_gain = take(query_gain_all, c_at * cols, cols)
    key_gain = take(key_gain_all, c_at * cols, cols)

    pieces = [take(w, c_at * cols, cols, 1) for w in (w_query, w_key, w_value)]
    weights = gather(jnp.concatenate(pieces + [out_piece], axis=1), "exp")
    qkv_w = weights[:, : 3 * cols]
    out_w = weights[:, 3 * cols :].reshape(n_ctx, cols, cols).transpose(1, 0, 2).reshape(cols, width)
    x_all = x_low.astype(F32)

    grad_mine = cotangent[0].astype(F32) * valid
    grad_low = grad_mine.astype(BF16)
    grad_parts = [gather(grad_low[h * part : (h + 1) * part], "exp") for h in range(halves)]
    d_hid_parts = [
        jnp.stack([mm_t(g, w_down[j]).astype(BF16) for j in range(own)]) for g in grad_parts
    ]

    cosine, sine = rope_tables(positions)
    xn = (x_all * rms_scale(x_all) * attn_gain).astype(BF16)
    qkv = mm(xn, qkv_w)
    qp, kp = qkv[:, :cols], qkv[:, cols : 2 * cols]
    squares = jnp.stack([jnp.sum(qp * qp, axis=-1), jnp.sum(kp * kp, axis=-1)], axis=0)
    squares = ctx_sum(jnp.pad(squares, ((0, 6), (0, 0))), 0)[:2] / width
    q_scale = lax.rsqrt(squares[0] + EPSILON)[:, None]
    k_scale = lax.rsqrt(squares[1] + EPSILON)[:, None]
    key_positions = jnp.where(positions < seq_length, positions, jnp.int32(1 << 30))
    base = (
        qkv, qkv, qkv, q_scale, k_scale, query_gain[None], key_gain[None],
        cosine, sine, cosine, sine, positions[:, None], key_positions[None],
    )

    attended_parts, mids, residual_parts, scale_parts = [], [], [], []
    for h in range(halves):
        attended = attend(base, half_seq, h)
        attended_parts.append(attended)
        got = []
        for d in range(n_ctx - 1, -1, -1):
            block = mm(take(attended, (c_at ^ d) * part, part), out_w)
            if d:
                got.append(swap(block.astype(BF16), d))
        residual, scale, mid = middle(
            tokens[0, h * part : (h + 1) * part], block, got, mlp_gain, grad_parts[-1:]
        )
        residual_parts.append(residual)
        scale_parts.append(scale)
        mids.append(gather(mid, "exp"))

    lane = jnp.arange(LANES, dtype=jnp.int32)[None, :]
    pick = (lane == e_at * own + jnp.arange(max(own, 8), dtype=jnp.int32)[:, None]).astype(F32)
    hid_parts, da_parts, db_parts, coef_parts = [], [], [], []
    dxs = []
    for h in range(halves):
        member_h = member_all[:, h * part : (h + 1) * part].reshape(n_exp * part, LANES)
        hid, da, db, dx, coef = expert_pass(
            mids[h], d_hid_parts[h], member_h, router_w, pick, w_gate, w_up, experts
        )
        hid_parts.append(hid)
        da_parts.append(da)
        db_parts.append(db)
        coef_parts.append(coef)
        dxs.append(dx)
    d_mids = [scatter_sum(after(dx, mids[-1]), "exp") for dx in dxs]

    def back_to_rows(h, *earlier):
        d_residual, low, g_gain = residual_back(
            residual_parts[h], scale_parts[h], mlp_gain,
            grad_mine[h * part : (h + 1) * part], d_mids[h], earlier,
        )
        dl = gather_ctx(low, 0).reshape(half_seq, width)
        return d_residual, low, g_gain, dl

    g_router = sum(t_mm(c, m) for m, c in zip(mids, coef_parts))[:experts]

    g_down, *y_parts = down_sums(hid_parts, grad_parts, w_down)
    d_res0, low0, gain0, dl0 = back_to_rows(0, y_parts[0])
    d_res1, low1, gain1, dl1 = back_to_rows(1, y_parts[0])
    bits = list(range(n_ctx.bit_length() - 1))
    gives, first_gate, first_up = [], [], []
    for j in range(own):
        order = bits if j % 2 == 0 else bits[::-1]
        table = c_at ^ jnp.asarray(halving_masks(order)[n_ctx // 2 :], jnp.int32)
        give = given_grads(
            table, mids, [da_parts, db_parts], width // n_ctx, j, (low0, low1, *gives)
        )
        first_gate.append(swap(give[0], 1 << order[0]))
        first_up.append(swap(give[1], 1 << order[0]))
        gives.append(give[0])
    g_mid_gain = gain0 + gain1
    d_res_parts, dl_parts = [d_res0, d_res1], [dl0, dl1]
    d_att_parts = [mm_t(dl, out_w).astype(BF16) for dl in dl_parts]
    y_mine = [scatter_sum(y, "exp") for y in y_parts]
    mixed = jnp.concatenate(
        [(r + y.astype(F32)).astype(BF16) for r, y in zip(residual_parts, y_mine)], axis=0
    )

    dq_parts = []
    dk_n = jnp.zeros((seq, cols), F32)
    dv = jnp.zeros((seq, cols), F32)
    for h in range(halves):
        dq, dk_n, dv = attend_back(base, half_seq, h, d_att_parts[h], dk_n, dv, gives)
        dq_parts.append(dq)
    dq_n = jnp.concatenate(dq_parts, axis=0)
    inner = jnp.stack(
        [
            jnp.sum(dq_n * query_gain * qp, axis=-1),
            jnp.sum(dk_n * key_gain * kp, axis=-1),
        ],
        axis=0,
    )
    inner = ctx_sum(jnp.pad(inner, ((0, 6), (0, 0))), 1, first_gate)[:2] / width
    dqp = q_scale * dq_n * query_gain - qp * (q_scale**3) * inner[0][:, None]
    dkp = k_scale * dk_n * key_gain - kp * (k_scale**3) * inner[1][:, None]
    g_query_gain = jnp.sum(dq_n * qp * q_scale, axis=0)
    g_key_gain = jnp.sum(dk_n * kp * k_scale, axis=0)
    d_qkv = jnp.concatenate([dqp.astype(BF16), dkp.astype(BF16), dv.astype(BF16)], axis=1)
    g_mine = attention_grads(xn, d_qkv, attended_parts, dl_parts, cols, first_up)
    partial = input_partial(d_qkv, weights, part, ())
    g_gate, dxn = gate_sums(
        mids, da_parts, partial, first_gate, (g_mine,)
    )
    dxn = jnp.concatenate([dxn[0], dxn[1]], axis=1)
    block_input = tokens[0].astype(F32)
    in_scale = rms_scale(block_input)
    d_in_norm, g_attn_gain = rms_backward(block_input, in_scale, attn_gain, dxn)
    d_tokens = (jnp.concatenate(d_res_parts, axis=0) + d_in_norm).astype(BF16)

    g_mine = scatter_sum(g_mine, "exp")
    g_out = lax.ppermute(g_mine[:, 3 * cols :], ("ctx", "exp"), [(b, a) for a, b in moves])
    g_mine = jnp.concatenate([g_mine[:, : 3 * cols], g_out], axis=1)
    gain_grads = [g_attn_gain[None], g_mid_gain]
    for piece in (g_query_gain, g_key_gain):
        gain_grads.append(
            lax.dynamic_update_slice_in_dim(jnp.zeros((1, width), F32), piece[None], c_at * cols, 1)
        )
    spare = -(experts + 4) % 8
    smalls = jnp.concatenate([g_router] + gain_grads + [jnp.zeros((spare, width), F32)], axis=0)
    smalls = smalls.reshape(-1, n_exp, shard).transpose(1, 0, 2)
    g_up, *g_full, smalls = up_sums(mids, db_parts, g_mine, smalls, first_up, (g_gate,))
    return (
        mixed[None], d_tokens[None],
        *g_full,
        smalls[:experts].T,
        smalls[experts], smalls[experts + 2], smalls[experts + 3], smalls[experts + 1],
        g_gate, g_up, g_down,
    )


def solution(mesh):
    tok = P("exp", "ctx", None)
    two, three, one = P("exp", None), P("exp", None, None), P("exp")
    return jax.shard_map(
        local,
        mesh=mesh,
        in_specs=(tok, tok, one, P(), tok) + (two,) * 5 + (one,) * 4 + (three,) * 3,
        out_specs=(tok, tok) + (two,) * 5 + (one,) * 4 + (tok,) * 3,
        check_vma=False,
    )
```

```python
import functools
import math

import jax
import jax.numpy as jnp
from jax import lax
from jax.experimental import pallas as pl
from jax.experimental.pallas import tpu as pltpu
from jax.sharding import PartitionSpec as P

HEADS = 16
HEAD_DIM = 128
LANES = 128
EPSILON = 1e-05
ROPE_BASE = 10000.0
MASKED_SCORE = -1e30
FACTOR = HEAD_DIM ** (-0.5)
F32 = jnp.float32
BF16 = jnp.bfloat16
MIB = 1 << 20


def mm(left, right):
    return jnp.dot(left, right, preferred_element_type=F32)


def mm_t(left, right):
    return lax.dot_general(left, right, (((1,), (1,)), ((), ())), preferred_element_type=F32)


def t_mm(left, right):
    return lax.dot_general(left, right, (((0,), (0,)), ((), ())), preferred_element_type=F32)


def rms_scale(rows):
    return lax.rsqrt(jnp.mean(rows * rows, axis=-1, keepdims=True) + EPSILON)


def rms_backward(rows, inv_scale, gain_vec, grad_in):
    weighted = grad_in * gain_vec
    inner_mean = jnp.mean(weighted * rows, axis=-1, keepdims=True)
    d_rows = inv_scale * weighted - rows * (inv_scale * inv_scale * inv_scale) * inner_mean
    return d_rows, jnp.sum(grad_in * rows * inv_scale, axis=0)


def rope_tables(positions):
    half_dim = HEAD_DIM // 2
    frequency = jnp.exp(
        jnp.arange(half_dim, dtype=F32) * (-2.0 * math.log(ROPE_BASE) / HEAD_DIM)
    )
    angle = positions.astype(F32)[:, None] * frequency[None, :]
    cosine, sine = jnp.cos(angle), jnp.sin(angle)
    return (
        jnp.concatenate([cosine, cosine], axis=1),
        jnp.concatenate([-sine, sine], axis=1),
    )


def positions_of(span_order, storage, span_length):
    return jnp.take(span_order, storage // span_length) * span_length + storage % span_length


def rotated(rows, scale, gain, cosine, sine):
    normed = rows * scale * gain
    return (normed * cosine + pltpu.roll(normed, HEAD_DIM // 2, 1) * sine).astype(BF16)


def unrotated(rows, cosine, sine):
    return rows * cosine - pltpu.roll(rows, HEAD_DIM // 2, 1) * sine


def head_probs(query, key, q_pos, k_pos):
    scores = jnp.where(k_pos <= q_pos, mm_t(query, key) * FACTOR, MASKED_SCORE)
    expo = jnp.exp(scores - jnp.max(scores, axis=1, keepdims=True))
    return expo / jnp.sum(expo, axis=1, keepdims=True)


def attend_kernel(
    q_ref, k_ref, v_ref, qs_ref, ks_ref, qg_ref, kg_ref, qc_ref, qn_ref, kc_ref, kn_ref,
    qp_ref, kp_ref, out_ref,
):
    query = rotated(q_ref[...], qs_ref[...], qg_ref[...], qc_ref[...], qn_ref[...])
    key = rotated(k_ref[...], ks_ref[...], kg_ref[...], kc_ref[...], kn_ref[...])
    probs = head_probs(query, key, qp_ref[...], kp_ref[...])
    out_ref[...] = mm(probs.astype(BF16), v_ref[...].astype(BF16)).astype(BF16)


def attend_back_kernel(
    q_ref, k_ref, v_ref, qs_ref, ks_ref, qg_ref, kg_ref, qc_ref, qn_ref, kc_ref, kn_ref,
    qp_ref, kp_ref, da_ref, dk_in, dv_in, *refs,
):
    dq_ref, dk_ref, dv_ref = refs[-3:]
    query = rotated(q_ref[...], qs_ref[...], qg_ref[...], qc_ref[...], qn_ref[...])
    key = rotated(k_ref[...], ks_ref[...], kg_ref[...], kc_ref[...], kn_ref[...])
    probs = head_probs(query, key, qp_ref[...], kp_ref[...])
    d_att = da_ref[...]
    d_probs = mm_t(d_att, v_ref[...].astype(BF16))
    inner = jnp.sum(probs * d_probs, axis=1, keepdims=True)
    d_scores = (probs * (d_probs - inner)).astype(BF16)
    dq_ref[...] = unrotated(mm(d_scores, key) * FACTOR, qc_ref[...], qn_ref[...])
    dk = unrotated(t_mm(d_scores, query) * FACTOR, kc_ref[...], kn_ref[...])
    dk_ref[...] = dk_in[...] + dk
    dv_ref[...] = dv_in[...] + t_mm(probs.astype(BF16), d_att)


def attention_specs(rows, seq, heads, h):
    def head_rows(n, at, row=0):
        return pl.BlockSpec((n, HEAD_DIM), lambda i: (row, at + i))

    def fixed(shape, row=0):
        return pl.BlockSpec(shape, lambda i: (row, 0))

    return [
        head_rows(rows, 0, h), head_rows(seq, heads), head_rows(seq, 2 * heads),
        fixed((rows, 1), h), fixed((seq, 1)), head_rows(1, 0), head_rows(1, 0),
        fixed((rows, HEAD_DIM), h), fixed((rows, HEAD_DIM), h),
        fixed((seq, HEAD_DIM)), fixed((seq, HEAD_DIM)),
        fixed((rows, 1), h), fixed((1, seq)),
    ]


def attend(base, rows, h):
    seq, cols = base[0].shape[0], base[0].shape[1] // 3
    heads = cols // HEAD_DIM
    return pl.pallas_call(
        attend_kernel,
        grid=(heads,),
        in_specs=attention_specs(rows, seq, heads, h),
        out_specs=pl.BlockSpec((rows, HEAD_DIM), lambda i: (0, i)),
        out_shape=jax.ShapeDtypeStruct((rows, cols), BF16),
        compiler_params=pltpu.CompilerParams(vmem_limit_bytes=48 * MIB),
        cost_estimate=pl.CostEstimate(
            flops=4 * rows * seq * cols, bytes_accessed=8 * MIB, transcendentals=rows * seq * heads
        ),
    )(*base)


def attend_back(base, rows, h, d_att, dk, dv, earlier):
    seq, cols = base[0].shape[0], base[0].shape[1] // 3
    heads = cols // HEAD_DIM
    q_out = pl.BlockSpec((rows, HEAD_DIM), lambda i: (0, i))
    k_out = pl.BlockSpec((seq, HEAD_DIM), lambda i: (0, i))
    return pl.pallas_call(
        attend_back_kernel,
        grid=(heads,),
        in_specs=attention_specs(rows, seq, heads, h)
        + [q_out, k_out, k_out]
        + [pl.BlockSpec(memory_space=pl.ANY)] * len(earlier),
        out_specs=[q_out, k_out, k_out],
        out_shape=[
            jax.ShapeDtypeStruct((rows, cols), F32),
            jax.ShapeDtypeStruct((seq, cols), F32),
            jax.ShapeDtypeStruct((seq, cols), F32),
        ],
        compiler_params=pltpu.CompilerParams(vmem_limit_bytes=48 * MIB),
        cost_estimate=pl.CostEstimate(
            flops=10 * rows * seq * cols, bytes_accessed=16 * MIB, transcendentals=rows * seq * heads
        ),
    )(*base, d_att, dk, dv, *earlier)


def expert_kernel(
    experts, own, step, x_ref, dh_ref, member_ref, router_ref, pick_ref, wg_hbm, wu_hbm,
    hid_ref, da_ref, db_ref, dx_ref, coef_ref, wg, wu, sems,
):
    i = pl.program_id(0)

    def loads(j):
        return (
            pltpu.make_async_copy(wg_hbm.at[j], wg.at[j], sems.at[0, j]),
            pltpu.make_async_copy(wu_hbm.at[j], wu.at[j], sems.at[1, j]),
        )

    @pl.when(i == 0)
    def _():
        for j in range(own):
            for copy in loads(j):
                copy.start()

    logits = mm(x_ref[...], router_ref[...])
    lane = lax.broadcasted_iota(jnp.int32, logits.shape, 1)
    logits = jnp.where(lane < experts, logits, MASKED_SCORE)
    expo = jnp.exp(logits - jnp.max(logits, axis=1, keepdims=True))
    router = expo / jnp.sum(expo, axis=1, keepdims=True)
    chosen = router * member_ref[...].astype(F32)
    coef = jnp.zeros_like(router)
    ff = wg.shape[2]
    for j in range(own):

        @pl.when(i == 0)
        def _():
            for copy in loads(j):
                copy.wait()

        pick = pick_ref[j : j + 1, :]
        gate = jnp.sum(chosen * pick, axis=1, keepdims=True)
        flow = jnp.zeros_like(gate)
        for f in range(0, ff, step):
            cut = slice(f, f + step)
            a = mm(x_ref[...], wg[j, :, cut])
            b = mm(x_ref[...], wu[j, :, cut])
            d_hid = dh_ref[j, :, cut].astype(F32)
            sig = jax.nn.sigmoid(a)
            silu = a * sig
            hid = silu * b
            flow = flow + jnp.sum(hid * d_hid, axis=1, keepdims=True)
            hid_ref[j, :, cut] = (gate * hid).astype(BF16)
            d_hid = d_hid * gate
            da_ref[j, :, cut] = (d_hid * b * (sig + silu * (1.0 - sig))).astype(BF16)
            db_ref[j, :, cut] = (d_hid * silu).astype(BF16)
        coef = coef + flow * gate * (pick - router)
    low = coef.astype(BF16)
    coef_ref[...] = low
    width = x_ref.shape[1]
    for n in range(0, width, step):
        cut = slice(n, n + step)
        part = mm_t(low, router_ref[cut, :])
        for j in range(own):
            part = part + mm_t(da_ref[j], wg[j, cut, :]) + mm_t(db_ref[j], wu[j, cut, :])
        dx_ref[:, cut] = part.astype(BF16)


def expert_pass(x, d_hid, member, router_w, pick, w_gate, w_up, experts):
    rows, width = x.shape
    own, _, ff = w_gate.shape
    tile = 256
    by_row = pl.BlockSpec((tile, width), lambda i: (i, 0))
    by_lane = pl.BlockSpec((tile, LANES), lambda i: (i, 0))
    by_expert = pl.BlockSpec((own, tile, ff), lambda i: (0, i, 0))
    return pl.pallas_call(
        functools.partial(expert_kernel, experts, own, 512),
        grid=(rows // tile,),
        in_specs=[
            by_row, by_expert, by_lane,
            pl.BlockSpec((width, LANES), lambda i: (0, 0)),
            pl.BlockSpec(pick.shape, lambda i: (0, 0)),
            pl.BlockSpec(memory_space=pl.ANY),
            pl.BlockSpec(memory_space=pl.ANY),
        ],
        out_specs=[by_expert] * 3 + [by_row, by_lane],
        out_shape=[jax.ShapeDtypeStruct((own, rows, ff), BF16)] * 3
        + [jax.ShapeDtypeStruct((rows, width), BF16), jax.ShapeDtypeStruct((rows, LANES), BF16)],
        scratch_shapes=[
            pltpu.VMEM((own, width, ff), BF16),
            pltpu.VMEM((own, width, ff), BF16),
            pltpu.SemaphoreType.DMA((2, own)),
        ],
        compiler_params=pltpu.CompilerParams(vmem_limit_bytes=56 * MIB),
        cost_estimate=pl.CostEstimate(
            flops=8 * rows * width * ff * own, bytes_accessed=40 * MIB, transcendentals=0
        ),
    )(x, d_hid, member, router_w, pick, w_gate, w_up)


def weight_kernel(n, x_ref, d_ref, *refs):
    out_ref = refs[-1]
    width = d_ref.shape[1]
    out_ref[:, :width] = t_mm(x_ref[...], d_ref[...]).astype(BF16)
    total = t_mm(refs[0][...], refs[n][...])
    for h in range(1, n):
        total = total + t_mm(refs[h][...], refs[n + h][...])
    out_ref[:, width:] = total.astype(BF16)


def attention_grads(xn, d_qkv, attended, dl, cols, earlier):
    seq, width = xn.shape
    n = len(attended)

    def by_column(a):
        return pl.BlockSpec((a.shape[0], cols), lambda i: (0, i))

    def fixed(a):
        return pl.BlockSpec(a.shape, lambda i: (0, 0))

    return pl.pallas_call(
        functools.partial(weight_kernel, n),
        grid=(width // cols,),
        in_specs=[by_column(xn), fixed(d_qkv)]
        + [fixed(a) for a in attended]
        + [by_column(a) for a in dl]
        + [pl.BlockSpec(memory_space=pl.ANY)] * len(earlier),
        out_specs=pl.BlockSpec((cols, 4 * cols), lambda i: (i, 0)),
        out_shape=jax.ShapeDtypeStruct((width, 4 * cols), BF16),
        compiler_params=pltpu.CompilerParams(vmem_limit_bytes=48 * MIB),
        cost_estimate=pl.CostEstimate(
            flops=8 * seq * width * cols, bytes_accessed=20 * MIB, transcendentals=0
        ),
    )(xn, d_qkv, *attended, *dl, *earlier)


def partial_kernel(n, part, d_ref, w_ref, *refs):
    out_ref = refs[-1]
    rows, halves = n * part, d_ref.shape[0] // (n * part)
    for h in range(halves):
        total = mm_t(d_ref[h * rows : (h + 1) * rows, :], w_ref[...]).astype(BF16)
        for c in range(n):
            out_ref[0, c, h * part : (h + 1) * part, :] = total[c * part : (c + 1) * part, :]


def input_partial(d_qkv, weights, part, earlier):
    n = lax.axis_size("ctx")
    seq, depth = d_qkv.shape
    width = weights.shape[0]
    rows = seq // n
    return pl.pallas_call(
        functools.partial(partial_kernel, n, part),
        grid=(2,),
        in_specs=[
            pl.BlockSpec((seq, depth), lambda i: (0, 0)),
            pl.BlockSpec((width // 2, depth), lambda i: (i, 0)),
        ]
        + [pl.BlockSpec(memory_space=pl.ANY)] * len(earlier),
        out_specs=pl.BlockSpec((1, n, rows, width // 2), lambda i: (i, 0, 0, 0)),
        out_shape=jax.ShapeDtypeStruct((2, n, rows, width // 2), BF16),
        compiler_params=pltpu.CompilerParams(vmem_limit_bytes=48 * MIB),
    )(d_qkv, weights, *earlier)


def give_kernel(n, count, table, *refs):
    for k in range(count):
        total = t_mm(refs[0][...], refs[(k + 1) * n][0])
        for h in range(1, n):
            total = total + t_mm(refs[h][...], refs[(k + 1) * n + h][0])
        refs[len(refs) - count + k][0] = total.astype(BF16)


def given_grads(table, lefts, rights, block, j, earlier):
    n, blocks = len(lefts), table.shape[0]
    flat = [a for right in rights for a in right]
    columns = flat[0].shape[2]
    return pl.pallas_call(
        functools.partial(give_kernel, n, len(rights)),
        grid_spec=pltpu.PrefetchScalarGridSpec(
            num_scalar_prefetch=1,
            grid=(blocks,),
            in_specs=[pl.BlockSpec((a.shape[0], block), lambda i, t: (0, t[i])) for a in lefts]
            + [pl.BlockSpec((1,) + a.shape[1:], lambda i, t: (j, 0, 0)) for a in flat]
            + [pl.BlockSpec(memory_space=pl.ANY)] * len(earlier),
            out_specs=[pl.BlockSpec((1, block, columns), lambda i, t: (i, 0, 0))] * len(rights),
        ),
        out_shape=[jax.ShapeDtypeStruct((blocks, block, columns), BF16)] * len(rights),
        compiler_params=pltpu.CompilerParams(vmem_limit_bytes=48 * MIB),
    )(table, *lefts, *flat, *earlier)


def mid_kernel(n, x_ref, own_ref, gain_ref, *refs):
    total = x_ref[...].astype(F32) + own_ref[...]
    for got in refs[: n - 1]:
        total = total + got[...].astype(F32)
    res_ref, scale_ref, low_ref = refs[-3:]
    scale = lax.rsqrt(jnp.mean(total * total, axis=1, keepdims=True) + EPSILON)
    res_ref[...] = total
    scale_ref[...] = scale
    low_ref[...] = (total * scale * gain_ref[...]).astype(BF16)


def middle(x, own_block, got, gain, earlier):
    rows, width = x.shape
    whole = pl.BlockSpec(memory_space=pltpu.VMEM)
    return pl.pallas_call(
        functools.partial(mid_kernel, len(got) + 1),
        in_specs=[whole] * (3 + len(got)) + [pl.BlockSpec(memory_space=pl.ANY)] * len(earlier),
        out_specs=[whole] * 3,
        out_shape=[
            jax.ShapeDtypeStruct((rows, width), F32),
            jax.ShapeDtypeStruct((rows, 1), F32),
            jax.ShapeDtypeStruct((rows, width), BF16),
        ],
        compiler_params=pltpu.CompilerParams(vmem_limit_bytes=60 * MIB),
    )(x, own_block, gain[None], *got, *earlier)


def res_kernel(res_ref, scale_ref, gain_ref, grad_ref, mid_ref, *refs):
    out_ref, low_ref, gain_out = refs[-3:]
    rows, scale = res_ref[...], scale_ref[...]
    grad_in = mid_ref[...].astype(F32)
    weighted = grad_in * gain_ref[...]
    inner = jnp.mean(weighted * rows, axis=1, keepdims=True)
    total = grad_ref[...] + scale * weighted - rows * (scale * scale * scale) * inner
    out_ref[...] = total
    low_ref[...] = total.astype(BF16)
    gain_out[...] = jnp.sum(grad_in * rows * scale, axis=0, keepdims=True)


def residual_back(residual, scale, gain, grad, d_mid, earlier):
    rows, width = residual.shape
    whole = pl.BlockSpec(memory_space=pltpu.VMEM)
    return pl.pallas_call(
        res_kernel,
        in_specs=[whole] * 5 + [pl.BlockSpec(memory_space=pl.ANY)] * len(earlier),
        out_specs=[whole] * 3,
        out_shape=[
            jax.ShapeDtypeStruct((rows, width), F32),
            jax.ShapeDtypeStruct((rows, width), BF16),
            jax.ShapeDtypeStruct((1, width), F32),
        ],
        compiler_params=pltpu.CompilerParams(vmem_limit_bytes=60 * MIB),
    )(residual, scale, gain[None], grad, d_mid, *earlier)


def meet(peers):
    barrier = pltpu.get_barrier_semaphore()
    for peer in peers:
        pl.semaphore_signal(barrier, inc=1, device_id=peer, device_id_type=pl.DeviceIdType.MESH)
    pl.semaphore_wait(barrier, len(peers))


def ctx_sum_kernel(n, x_ref, *refs):
    out_ref, slots, send, recv = refs[-4:]
    me = lax.axis_index("ctx")
    peers = [{"ctx": lax.rem(me + d, n)} for d in range(1, n)]
    meet(peers)
    slots[me] = x_ref[...]
    copies = [
        pltpu.make_async_remote_copy(
            src_ref=x_ref, dst_ref=slots.at[me], send_sem=send.at[d], recv_sem=recv.at[d],
            device_id=peer, device_id_type=pl.DeviceIdType.MESH,
        )
        for d, peer in enumerate(peers)
    ]
    for copy in copies:
        copy.start()
    for copy in copies:
        copy.wait()
    total = slots[0]
    for k in range(1, n):
        total = total + slots[k]
    out_ref[...] = total


def ctx_sum(x, number, earlier=()):
    n = lax.axis_size("ctx")
    whole = pl.BlockSpec(memory_space=pltpu.VMEM)
    return pl.pallas_call(
        functools.partial(ctx_sum_kernel, n),
        in_specs=[whole] + [pl.BlockSpec(memory_space=pl.ANY)] * len(earlier),
        out_specs=whole,
        out_shape=jax.ShapeDtypeStruct(x.shape, F32),
        scratch_shapes=[
            pltpu.VMEM((n,) + x.shape, F32),
            pltpu.SemaphoreType.DMA((n - 1,)),
            pltpu.SemaphoreType.DMA((n - 1,)),
        ],
        compiler_params=pltpu.CompilerParams(collective_id=number, has_side_effects=True),
    )(x, *earlier)


class SmallSum:
    def __init__(self, n_ctx, n_exp, x, first, second, sems):
        self.x, self.first, self.second, self.sems = x, first, second, sems
        self.c_at, self.e_at = lax.axis_index("ctx"), lax.axis_index("exp")
        self.across = [{"exp": lax.rem(self.e_at + d, n_exp)} for d in range(1, n_exp)]
        self.along = [{"ctx": lax.rem(self.c_at + d, n_ctx)} for d in range(1, n_ctx)]

    def copy(self, src, dst, step, d, peer):
        return pltpu.make_async_remote_copy(
            src_ref=src, dst_ref=dst, send_sem=self.sems.at[2 * step, d],
            recv_sem=self.sems.at[2 * step + 1, d], device_id=peer,
            device_id_type=pl.DeviceIdType.MESH,
        )

    def over_exp(self):
        return [
            self.copy(self.x.at[peer["exp"]], self.first.at[self.e_at], 0, d, peer)
            for d, peer in enumerate(self.across)
        ]

    def over_ctx(self):
        mine = self.second.at[self.c_at]
        return [self.copy(mine, mine, 1, d, peer) for d, peer in enumerate(self.along)]

    def begin(self):
        for copy in self.over_exp():
            copy.start()
        self.first[self.e_at] = self.x[self.e_at]

    def pass_on(self):
        for copy in self.over_exp():
            copy.wait()
        total = self.first[0]
        for k in range(1, self.first.shape[0]):
            total = total + self.first[k]
        self.second[self.c_at] = total
        for copy in self.over_ctx():
            copy.start()

    def finish(self, out):
        for copy in self.over_ctx():
            copy.wait()
        total = self.second[0]
        for k in range(1, self.second.shape[0]):
            total = total + self.second[k]
        out[...] = total

    @staticmethod
    def scratch(n_ctx, shape):
        return [
            pltpu.VMEM(shape, F32),
            pltpu.VMEM((n_ctx,) + shape[1:], F32),
            pltpu.SemaphoreType.DMA((4, max(n_ctx, shape[0]) - 1)),
        ]


def halving_masks(order):
    masks = [0]
    for bit in order[::-1]:
        masks = masks + [m | (1 << bit) for m in masks]
    return masks


def flip(value, mask):
    bit = 0
    while mask >> bit:
        if (mask >> bit) & 1:
            value = value + (1 << bit) * (1 - 2 * lax.rem(lax.div(value, 1 << bit), 2))
        bit += 1
    return value


class Halving:
    def __init__(self, n, me, source, blocks, got, send, recv, out, first=None):
        self.n, self.me, self.source, self.blocks, self.got = n, me, source, blocks, got
        self.send, self.recv, self.out = send, recv, out
        self.first = first
        bits = list(range(n.bit_length() - 1))
        self.own = out.shape[0]
        self.orders = [bits if j % 2 == 0 else bits[::-1] for j in range(self.own)]
        self.masks = [halving_masks(order) for order in self.orders]
        self.steps = len(bits)

    def target(self, j, k):
        return flip(self.me, self.masks[j][k])

    def slot(self, s, k):
        return self.n - (self.n >> s) + k - (self.n >> (s + 1))

    def copy(self, j, s, k):
        given = self.source is not None and s == 0
        at = self.slot(s, k)
        return pltpu.make_async_remote_copy(
            src_ref=self.source.at[j, self.target(j, k)] if given else self.blocks.at[j, k - 1],
            dst_ref=self.got.at[j, at],
            send_sem=self.send.at[j, at],
            recv_sem=self.recv.at[j, at],
            device_id={"ctx": flip(self.me, 1 << self.orders[j][s])},
            device_id_type=pl.DeviceIdType.MESH,
        )

    def going(self, s):
        return [
            (j, k)
            for k in range((self.n >> s) - 1, (self.n >> (s + 1)) - 1, -1)
            for j in range(self.own)
        ]

    def begin(self, value=None):
        for j, k in self.going(0) if self.first is None else []:
            if value is not None:
                self.blocks[j, k - 1] = value(j, self.target(j, k)).astype(BF16)
            self.copy(j, 0, k).start()
        for k in range(self.n // 2 - 1, 0, -1):
            for j in range(self.own):
                at = self.target(j, k)
                mine = self.source[j, at] if value is None else value(j, at)
                self.blocks[j, k - 1] = mine.astype(BF16)

    def rest(self, value=None):
        for j in range(self.own):
            self.out[j] = self.source[j, self.me].astype(F32) if value is None else value(j, self.me)

    def arrived(self, j, k, steps):
        total = None
        for s in range(steps):
            sent = k + (self.n >> (s + 1))
            if s == 0 and self.first is not None:
                part = self.first[j][k].astype(F32)
            else:
                self.copy(j, s, sent).wait_recv()
                part = self.got[j, self.slot(s, sent)].astype(F32)
            total = part if total is None else total + part
        return total

    def pass_on(self):
        for s in range(1, self.steps):
            for j, k in self.going(s):
                total = self.blocks[j, k - 1].astype(F32) + self.arrived(j, k, s)
                self.blocks[j, k - 1] = total.astype(BF16)
                self.copy(j, s, k).start()

    def finish(self):
        for j in range(self.own):
            self.out[j] += self.arrived(j, 0, self.steps)
        for s in range(0 if self.first is None else 1, self.steps):
            for j, k in self.going(s):
                self.copy(j, s, k).wait_send()

    @staticmethod
    def scratch(own, n, rows, columns):
        return [
            pltpu.VMEM((own, n - 1, rows, columns), BF16),
            pltpu.VMEM((own, n - 1, rows, columns), BF16),
            pltpu.SemaphoreType.DMA((own, n - 1)),
            pltpu.SemaphoreType.DMA((own, n - 1)),
        ]


def ctx_peers(n, me):
    return [{"ctx": lax.rem(me + d, n)} for d in range(1, n)]


def entry(ref, j):
    return ref.at[j] if len(ref.shape) == 3 else ref


def product(lefts, rights, block):
    def value(j, at):
        total = None
        for left, right in zip(lefts, rights):
            columns = pl.ds(pl.multiple_of(at * block, LANES), block)
            part = t_mm(entry(left, j)[:, columns], entry(right, j)[...])
            total = part if total is None else total + part
        return total

    return value


def down_kernel(n, halves, *refs):
    hid, grad, w_down = refs[:halves], refs[halves : 2 * halves], refs[2 * halves]
    refs = refs[2 * halves + 1 :]
    out, ys, scratch = refs[0], refs[1 : 1 + halves], refs[1 + halves :]
    me = lax.axis_index("ctx")
    meet(ctx_peers(n, me))
    sums = Halving(n, me, None, *scratch, out)
    value = product(hid, grad, hid[0].shape[2] // n)
    sums.begin(value)
    sums.rest(value)
    width = w_down.shape[2]
    for h in range(halves):
        for start in range(0, width, 512):
            cut = slice(start, start + 512)
            total = mm(hid[h][0], w_down[0, :, cut])
            for j in range(1, w_down.shape[0]):
                total = total + mm(hid[h][j], w_down[j, :, cut])
            ys[h][:, cut] = total.astype(BF16)
    sums.pass_on()
    sums.finish()


def gate_kernel(n, halves, *refs):
    mids, pres = refs[:halves], refs[halves : 2 * halves]
    partial, out, dxn = refs[2 * halves], refs[-10], refs[-9]
    first = refs[2 * halves + 1 : 2 * halves + 1 + out.shape[0]]
    me = lax.axis_index("ctx")
    meet(ctx_peers(n, me))
    rows = Halving(n, me, partial, *refs[-8:-4], dxn)
    rows.begin()
    sums = Halving(n, me, None, *refs[-4:], out, first)
    value = product(mids, pres, mids[0].shape[1] // n)
    sums.begin(value)
    sums.pass_on()
    rows.pass_on()
    sums.rest(value)
    rows.rest()
    rows.finish()
    sums.finish()


def up_kernel(n, halves, *refs):
    mids, pres = refs[:halves], refs[halves : 2 * halves]
    piece, x = refs[2 * halves], refs[2 * halves + 1]
    out, *whole = refs[-16:-11]
    small_out, slots, send, recv = refs[-11:-7]
    me = lax.axis_index("ctx")
    smalls = SmallSum(n, x.shape[0], x, *refs[-7:-4])
    meet(smalls.across + smalls.along)
    smalls.begin()
    bits = list(range(n.bit_length() - 1))
    half = piece.shape[0] // 2

    def doubling(i, s):
        order = bits if i == 0 else bits[::-1]
        lines = pl.ds(i * half, half)
        copies = []
        for m in halving_masks(order[:s]):
            at = flip(me, m)
            sem = i, (1 << s) - 1 + len(copies)
            copies.append(
                pltpu.make_async_remote_copy(
                    src_ref=slots.at[at, lines] if m else piece.at[lines],
                    dst_ref=slots.at[at, lines],
                    send_sem=send.at[sem],
                    recv_sem=recv.at[sem],
                    device_id={"ctx": flip(me, 1 << order[s])},
                    device_id_type=pl.DeviceIdType.MESH,
                )
            )
        return copies

    first = refs[2 * halves + 2 : 2 * halves + 2 + out.shape[0]]
    sums = Halving(n, me, None, *refs[-4:], out, first)
    for i in range(2):
        for copy in doubling(i, 0):
            copy.start()
    value = product(mids, pres, mids[0].shape[1] // n)
    sums.begin(value)
    sums.pass_on()
    smalls.pass_on()
    slots[me] = piece[...]
    for s in range(1, len(bits)):
        for i in range(2):
            for copy in doubling(i, s - 1):
                copy.wait_recv()
            for copy in doubling(i, s):
                copy.start()
    sums.rest(value)
    smalls.finish(small_out)
    sums.finish()
    for i in range(2):
        for copy in doubling(i, len(bits) - 1):
            copy.wait_recv()
        for s in range(len(bits)):
            for copy in doubling(i, s):
                copy.wait_send()
    cols = piece.shape[1] // len(whole)
    for c in range(n):
        for k, ref in enumerate(whole):
            ref[:, c * cols : (c + 1) * cols] = slots[c, :, k * cols : (k + 1) * cols].astype(F32)


class Doubling:
    def __init__(self, axis, order, last, block, slot, sems, base):
        self.me, self.axis, self.order, self.last = lax.axis_index(axis), axis, order, last
        self.block, self.slot, self.sems, self.base = block, slot, sems, base
        self.steps = [halving_masks(order[:s]) for s in range(len(order) + 1)]
        self.keys = [(bit, m) for bit, ms in zip(order, self.steps) for m in ms]
        if last is not None:
            self.keys += [(last, m) for m in self.steps[-1]]

    def copy(self, bit, m):
        at = self.base + self.keys.index((bit, m))
        place = self.slot(flip(self.me, m))
        return pltpu.make_async_remote_copy(
            src_ref=place if m else self.block,
            dst_ref=place,
            send_sem=self.sems.at[0, at],
            recv_sem=self.sems.at[1, at],
            device_id={self.axis: flip(self.me, 1 << bit)},
            device_id_type=pl.DeviceIdType.MESH,
        )

    def step(self, s):
        fresh = [0]
        if s:
            fresh = [m | (1 << self.order[s - 1]) for m in self.steps[s - 1]]
            for m in self.steps[s - 1]:
                self.copy(self.order[s - 1], m).wait_recv()
        if s < len(self.order):
            for m in self.steps[s]:
                self.copy(self.order[s], m).start()
        if self.last is not None:
            for m in fresh:
                self.copy(self.last, m).start()

    def finish(self):
        if self.last is not None:
            for m in self.steps[-1]:
                self.copy(self.last, m).wait_recv()
        for key in self.keys:
            self.copy(*key).wait_send()


def start_kernel(n_ctx, n_exp, w_ref, x_ref, small_ref, w_out, x_out, small_out, sems, local_sems):
    c_at, e_at = lax.axis_index("ctx"), lax.axis_index("exp")
    c_bits, e_bits = n_ctx.bit_length() - 1, n_exp.bit_length() - 1
    meet(
        [{"ctx": flip(c_at, 1 << b)} for b in range(c_bits)]
        + [{"exp": flip(e_at, 1 << b)} for b in range(e_bits)]
    )
    far = list(range(1, e_bits))
    near = list(range(c_bits))
    half = w_ref.shape[0] // 2
    moves, base = [], 0

    def add(axis, order, last, block, slot):
        moves.append(Doubling(axis, order, last, block, slot, sems, base))
        return base + len(moves[-1].keys)

    base = add("exp", far, 0, small_ref, lambda at: small_out.at[at])
    for i, order in enumerate((far[::-1], far)):
        lines = pl.ds(i * half, half)
        base = add(
            "exp", order, 0, w_ref.at[lines], lambda at, lines=lines: w_out.at[at, lines]
        )
    for i, order in enumerate((near[::-1], near)):
        base = add("ctx", order, None, x_ref.at[i], lambda at, i=i: x_out.at[i, at])
    own = [
        pltpu.make_async_copy(w_ref, w_out.at[e_at], local_sems.at[0]),
        pltpu.make_async_copy(small_ref, small_out.at[e_at], local_sems.at[1]),
        pltpu.make_async_copy(x_ref.at[0], x_out.at[0, c_at], local_sems.at[2]),
        pltpu.make_async_copy(x_ref.at[1], x_out.at[1, c_at], local_sems.at[3]),
    ]
    for s in range(max(len(far), len(near)) + 1):
        for move in moves:
            if s <= len(move.order):
                move.step(s)
        if s == 0:
            for copy in own:
                copy.start()
    for move in moves:
        move.finish()
    for copy in own:
        copy.wait()


def gather_start(w, x, small):
    n_ctx, n_exp = lax.axis_size("ctx"), lax.axis_size("exp")
    count = 3 * (n_exp - 1) + 2 * (n_ctx - 1)
    return pl.pallas_call(
        functools.partial(start_kernel, n_ctx, n_exp),
        in_specs=[ANY] * 3,
        out_specs=[ANY] * 3,
        out_shape=[
            jax.ShapeDtypeStruct((n_exp,) + w.shape, BF16),
            jax.ShapeDtypeStruct((x.shape[0], n_ctx) + x.shape[1:], BF16),
            jax.ShapeDtypeStruct((n_exp,) + small.shape, BF16),
        ],
        scratch_shapes=[pltpu.SemaphoreType.DMA((2, count)), pltpu.SemaphoreType.DMA((4,))],
        compiler_params=pltpu.CompilerParams(collective_id=6, has_side_effects=True),
    )(w, x, small)


def hold_kernel(*refs):
    pass


def held(arrays, earlier):
    n = len(arrays)
    return pl.pallas_call(
        hold_kernel,
        in_specs=[ANY] * (n + len(earlier)),
        out_specs=[ANY] * n,
        out_shape=[jax.ShapeDtypeStruct(a.shape, a.dtype) for a in arrays],
        input_output_aliases={i: i for i in range(n)},
        compiler_params=pltpu.CompilerParams(vmem_limit_bytes=60 * MIB),
    )(*arrays, *earlier)


def mask_kernel(x_ref, valid_ref, *refs):
    refs[-1][...] = (x_ref[...].astype(F32) * valid_ref[...]).astype(BF16)


def masked(x, valid, earlier):
    blocks = [pl.BlockSpec(a.shape, lambda i: (0, 0)) for a in (x, valid)]
    return pl.pallas_call(
        mask_kernel,
        grid=(1,),
        in_specs=blocks + [ANY] * len(earlier),
        out_specs=blocks[0],
        out_shape=jax.ShapeDtypeStruct(x.shape, BF16),
    )(x, valid, *earlier)


VMEM = pl.BlockSpec(memory_space=pltpu.VMEM)
ANY = pl.BlockSpec(memory_space=pl.ANY)


def exchange(kernel, number, operands, earlier, outs, scratch):
    n = lax.axis_size("ctx")
    return pl.pallas_call(
        kernel,
        in_specs=[VMEM] * len(operands) + [ANY] * len(earlier),
        out_specs=[VMEM] * len(outs),
        out_shape=outs,
        scratch_shapes=scratch,
        compiler_params=pltpu.CompilerParams(
            collective_id=number, has_side_effects=True, vmem_limit_bytes=60 * MIB
        ),
    )(*operands, *earlier)


def down_sums(hid, grad, w_down):
    n, halves = lax.axis_size("ctx"), len(hid)
    own, ff, width = w_down.shape
    outs = [jax.ShapeDtypeStruct((own, ff // n, width), F32)]
    outs += [jax.ShapeDtypeStruct((h.shape[1], width), BF16) for h in hid]
    return exchange(
        functools.partial(down_kernel, n, halves), 3, [*hid, *grad, w_down], (), outs,
        Halving.scratch(own, n, ff // n, width),
    )


def gate_sums(mids, pres, partial, first, earlier):
    n, halves = lax.axis_size("ctx"), len(mids)
    own, _, ff = pres[0].shape
    rows = mids[0].shape[1] // n
    shape = partial.shape
    outs = [
        jax.ShapeDtypeStruct((own, rows, ff), F32),
        jax.ShapeDtypeStruct((shape[0],) + shape[2:], F32),
    ]
    return exchange(
        functools.partial(gate_kernel, n, halves), 4, [*mids, *pres, partial, *first], earlier, outs,
        Halving.scratch(shape[0], n, *shape[2:]) + Halving.scratch(own, n, rows, ff),
    )


def up_sums(mids, pres, piece, smalls, first, earlier):
    n, halves = lax.axis_size("ctx"), len(mids)
    own, _, ff = pres[0].shape
    rows = mids[0].shape[1] // n
    shard, width = piece.shape
    outs = [jax.ShapeDtypeStruct((own, rows, ff), F32)]
    outs += [jax.ShapeDtypeStruct((shard, n * width // 4), F32) for _ in range(4)]
    outs += [jax.ShapeDtypeStruct(smalls.shape[1:], F32)]
    return exchange(
        functools.partial(up_kernel, n, halves), 5, [*mids, *pres, piece, smalls, *first], earlier,
        outs,
        [
            pltpu.VMEM((n,) + piece.shape, BF16),
            pltpu.SemaphoreType.DMA((2, n - 1)),
            pltpu.SemaphoreType.DMA((2, n - 1)),
        ]
        + SmallSum.scratch(n, smalls.shape)
        + Halving.scratch(own, n, rows, ff),
    )


def gather(block, axis):
    return lax.all_gather(block, axis, axis=0, tiled=True)


def scatter_sum(block, axis, dimension=0):
    return lax.psum_scatter(block, axis, scatter_dimension=dimension, tiled=True)


def after(value, *earlier):
    return lax.optimization_barrier((value,) + earlier)[0]


def swap(block, bits):
    n = lax.axis_size("ctx")
    return lax.ppermute(block, "ctx", [(i, i ^ bits) for i in range(n)])


def take(block, at, size=1, axis=0):
    return lax.dynamic_slice_in_dim(block, at, size, axis)


def gather_ctx(block, axis):
    n, me = lax.axis_size("ctx"), lax.axis_index("ctx")
    parts = [block] + [swap(block, d) for d in range(1, n)]
    shape = block.shape[:axis] + (n,) + block.shape[axis:]
    out = jnp.zeros(shape, block.dtype)
    for d, piece in enumerate(parts):
        out = lax.dynamic_update_slice_in_dim(out, jnp.expand_dims(piece, axis), me ^ d, axis)
    return out


def local(
    tokens, cotangent, lengths, span_order, routes,
    w_query, w_key, w_value, w_output, w_router,
    gain_attn, gain_query, gain_key, gain_mlp,
    w_gate, w_up, w_down,
):
    n_ctx, n_exp = lax.axis_size("ctx"), lax.axis_size("exp")
    c_at, e_at = lax.axis_index("ctx"), lax.axis_index("exp")
    rows = tokens.shape[1]
    width = tokens.shape[2]
    seq = rows * n_ctx
    cols = width // n_ctx
    shard = width // n_exp
    own = w_gate.shape[0]
    ff = w_gate.shape[2]
    experts = w_router.shape[1]
    seq_length = lengths[0]
    halves = 2
    part = rows // halves
    half_seq = part * n_ctx

    ratio = n_exp // n_ctx
    moves = []
    for c in range(n_ctx):
        for e in range(n_exp):
            moves.append(((e // ratio) * n_exp + c * ratio + e % ratio, c * n_exp + e))
    out_piece = lax.ppermute(take(w_output, c_at * cols, cols, 1), ("ctx", "exp"), moves)

    storage = jnp.arange(seq, dtype=jnp.int32)
    storage = (storage % half_seq // part) * rows + storage // half_seq * part + storage % part
    positions = positions_of(span_order, storage, rows // 2)
    my_positions = positions_of(
        span_order, c_at * rows + jnp.arange(rows, dtype=jnp.int32), rows // 2
    )
    valid = (my_positions < seq_length).astype(F32)[:, None]
    member = jnp.sum(
        (routes[0][:, None, :] == jnp.arange(experts, dtype=jnp.int32)[None, :, None]).astype(BF16),
        axis=2,
    )
    small = jnp.concatenate(
        [
            w_router.reshape(-1), gain_attn, gain_query, gain_key, gain_mlp,
            member.reshape(-1),
        ]
    )
    used = small.shape[0]
    lines = -(-used // (16 * LANES)) * 16
    small = jnp.pad(small, (0, lines * LANES - used)).reshape(lines, LANES)
    pieces = [take(w, c_at * cols, cols, 1) for w in (w_query, w_key, w_value)]
    weights, x_low, small_all = gather_start(
        jnp.concatenate(pieces + [out_piece], axis=1), tokens[0].reshape(halves, part, width), small
    )
    weights = weights.reshape(width, 4 * cols)
    x_low = x_low.reshape(seq, width)
    small_all = small_all.reshape(n_exp, lines * LANES)[:, :used]
    at = shard * experts
    router_w = small_all[:, :at].reshape(width, experts)
    router_w = jnp.pad(router_w, ((0, 0), (0, LANES - experts)))
    gains = []
    for _ in range(4):
        gains.append(small_all[:, at : at + shard].reshape(width).astype(F32))
        at += shard
    attn_gain, query_gain_all, key_gain_all, mlp_gain = gains
    member_all = small_all[:, at:].reshape(n_exp, rows, experts)
    member_all = jnp.pad(member_all, ((0, 0), (0, 0), (0, LANES - experts)))
    query_gain = take(query_gain_all, c_at * cols, cols)
    key_gain = take(key_gain_all, c_at * cols, cols)

    qkv_w = weights[:, : 3 * cols]
    out_w = weights[:, 3 * cols :].reshape(n_ctx, cols, cols).transpose(1, 0, 2).reshape(cols, width)
    x_all = x_low.astype(F32)

    grad_low = masked(cotangent[0], valid, (weights,))
    grad_mine = grad_low.astype(F32)
    grad_parts = [gather(grad_low[h * part : (h + 1) * part], "exp") for h in range(halves)]
    d_hid_parts = [
        jnp.stack([mm_t(g, w_down[j]).astype(BF16) for j in range(own)]) for g in grad_parts
    ]

    cosine, sine = rope_tables(positions)
    xn = (x_all * rms_scale(x_all) * attn_gain).astype(BF16)
    qkv = mm(xn, qkv_w)
    qp, kp = qkv[:, :cols], qkv[:, cols : 2 * cols]
    squares = jnp.stack([jnp.sum(qp * qp, axis=-1), jnp.sum(kp * kp, axis=-1)], axis=0)
    squares = ctx_sum(jnp.pad(squares, ((0, 6), (0, 0))), 0)[:2] / width
    q_scale = lax.rsqrt(squares[0] + EPSILON)[:, None]
    k_scale = lax.rsqrt(squares[1] + EPSILON)[:, None]
    key_positions = jnp.where(positions < seq_length, positions, jnp.int32(1 << 30))
    base = (
        qkv, qkv, qkv, q_scale, k_scale, query_gain[None], key_gain[None],
        cosine, sine, cosine, sine, positions[:, None], key_positions[None],
    )

    attended_parts, mids, residual_parts, scale_parts = [], [], [], []
    for h in range(halves):
        attended = attend(base, half_seq, h)
        attended_parts.append(attended)
        got = []
        for d in range(n_ctx - 1, -1, -1):
            block = mm(take(attended, (c_at ^ d) * part, part), out_w)
            if d:
                got.append(swap(block.astype(BF16), d))
        residual, scale, mid = middle(
            tokens[0, h * part : (h + 1) * part], block, got, mlp_gain,
            (d_hid_parts[h],),
        )
        residual_parts.append(residual)
        scale_parts.append(scale)
        mids.append(gather(mid, "exp"))

    lane = jnp.arange(LANES, dtype=jnp.int32)[None, :]
    pick = (lane == e_at * own + jnp.arange(max(own, 8), dtype=jnp.int32)[:, None]).astype(F32)
    hid_parts, da_parts, db_parts, coef_parts = [], [], [], []
    dxs = []
    for h in range(halves):
        member_h = member_all[:, h * part : (h + 1) * part].reshape(n_exp * part, LANES)
        hid, da, db, dx, coef = expert_pass(
            mids[h], d_hid_parts[h], member_h, router_w, pick, w_gate, w_up, experts
        )
        hid_parts.append(hid)
        da_parts.append(da)
        db_parts.append(db)
        coef_parts.append(coef)
        dxs.append(dx)
    d_mids = [scatter_sum(after(dx, mids[-1]), "exp") for dx in dxs]

    def back_to_rows(h, *earlier):
        d_residual, low, g_gain = residual_back(
            residual_parts[h], scale_parts[h], mlp_gain,
            grad_mine[h * part : (h + 1) * part], d_mids[h], earlier,
        )
        dl = gather_ctx(low, 0).reshape(half_seq, width)
        return d_residual, low, g_gain, dl

    g_router = sum(t_mm(c, m) for m, c in zip(mids, coef_parts))[:experts]

    g_down, *y_parts = down_sums(hid_parts, grad_parts, w_down)
    d_res0, low0, gain0, dl0 = back_to_rows(0, y_parts[0])
    d_res1, low1, gain1, dl1 = back_to_rows(1, y_parts[0])
    bits = list(range(n_ctx.bit_length() - 1))
    gives, first_gate, give_up = [], [], []
    for j in range(own):
        order = bits if j % 2 == 0 else bits[::-1]
        table = c_at ^ jnp.asarray(halving_masks(order)[n_ctx // 2 :], jnp.int32)
        give = given_grads(
            table, mids, [da_parts, db_parts], width // n_ctx, j, (low0, low1, *gives)
        )
        first_gate.append(swap(give[0], 1 << order[0]))
        give_up.append(give[1])
        gives.append(give[0])
    g_mid_gain = gain0 + gain1
    d_res_parts, dl_parts = [d_res0, d_res1], [dl0, dl1]
    d_att_parts = [mm_t(dl, out_w).astype(BF16) for dl in dl_parts]
    y_mine = [scatter_sum(y, "exp") for y in y_parts]
    mixed = jnp.concatenate(
        [(r + y.astype(F32)).astype(BF16) for r, y in zip(residual_parts, y_mine)], axis=0
    )

    dq_parts = []
    dk_n = jnp.zeros((seq, cols), F32)
    dv = jnp.zeros((seq, cols), F32)
    for h in range(halves):
        dq, dk_n, dv = attend_back(base, half_seq, h, d_att_parts[h], dk_n, dv, gives)
        dq_parts.append(dq)
    dq_n = jnp.concatenate(dq_parts, axis=0)
    inner = jnp.stack(
        [
            jnp.sum(dq_n * query_gain * qp, axis=-1),
            jnp.sum(dk_n * key_gain * kp, axis=-1),
        ],
        axis=0,
    )
    inner = ctx_sum(jnp.pad(inner, ((0, 6), (0, 0))), 1, first_gate)
    give_up = held(give_up, (inner,))
    first_up = [swap(g, 1 << (bits[0] if j % 2 == 0 else bits[-1])) for j, g in enumerate(give_up)]
    inner = inner[:2] / width
    dqp = q_scale * dq_n * query_gain - qp * (q_scale**3) * inner[0][:, None]
    dkp = k_scale * dk_n * key_gain - kp * (k_scale**3) * inner[1][:, None]
    g_query_gain = jnp.sum(dq_n * qp * q_scale, axis=0)
    g_key_gain = jnp.sum(dk_n * kp * k_scale, axis=0)
    d_qkv = jnp.concatenate([dqp.astype(BF16), dkp.astype(BF16), dv.astype(BF16)], axis=1)
    g_mine = attention_grads(xn, d_qkv, attended_parts, dl_parts, cols, ())
    partial = input_partial(d_qkv, weights, part, first_up)
    g_gate, dxn = gate_sums(
        mids, da_parts, partial, first_gate, (g_mine,)
    )
    dxn = jnp.concatenate([dxn[0], dxn[1]], axis=1)
    block_input = tokens[0].astype(F32)
    in_scale = rms_scale(block_input)
    d_in_norm, g_attn_gain = rms_backward(block_input, in_scale, attn_gain, dxn)
    d_tokens = (jnp.concatenate(d_res_parts, axis=0) + d_in_norm).astype(BF16)

    g_mine = scatter_sum(g_mine, "exp")
    g_out = lax.ppermute(g_mine[:, 3 * cols :], ("ctx", "exp"), [(b, a) for a, b in moves])
    g_mine = jnp.concatenate([g_mine[:, : 3 * cols], g_out], axis=1)
    gain_grads = [g_attn_gain[None], g_mid_gain]
    for piece in (g_query_gain, g_key_gain):
        gain_grads.append(
            lax.dynamic_update_slice_in_dim(jnp.zeros((1, width), F32), piece[None], c_at * cols, 1)
        )
    spare = -(experts + 4) % 8
    smalls = jnp.concatenate([g_router] + gain_grads + [jnp.zeros((spare, width), F32)], axis=0)
    smalls = smalls.reshape(-1, n_exp, shard).transpose(1, 0, 2)
    g_up, *g_full, smalls = up_sums(mids, db_parts, g_mine, smalls, first_up, (g_gate,))
    return (
        mixed[None], d_tokens[None],
        *g_full,
        smalls[:experts].T,
        smalls[experts], smalls[experts + 2], smalls[experts + 3], smalls[experts + 1],
        g_gate, g_up, g_down,
    )


def solution(mesh):
    tok = P("exp", "ctx", None)
    two, three, one = P("exp", None), P("exp", None, None), P("exp")
    return jax.shard_map(
        local,
        mesh=mesh,
        in_specs=(tok, tok, one, P(), tok) + (two,) * 5 + (one,) * 4 + (three,) * 3,
        out_specs=(tok, tok) + (two,) * 5 + (one,) * 4 + (tok,) * 3,
        check_vma=False,
    )
```

```python
import functools
import math

import jax
import jax.numpy as jnp
from jax import lax
from jax.experimental import pallas as pl
from jax.experimental.pallas import tpu as pltpu
from jax.sharding import PartitionSpec as P

HEADS = 16
HEAD_DIM = 128
LANES = 128
EPSILON = 1e-05
ROPE_BASE = 10000.0
MASKED_SCORE = -1e30
FACTOR = HEAD_DIM ** (-0.5)
F32 = jnp.float32
BF16 = jnp.bfloat16
MIB = 1 << 20


def mm(left, right):
    return jnp.dot(left, right, preferred_element_type=F32)


def mm_t(left, right):
    return lax.dot_general(left, right, (((1,), (1,)), ((), ())), preferred_element_type=F32)


def t_mm(left, right):
    return lax.dot_general(left, right, (((0,), (0,)), ((), ())), preferred_element_type=F32)


def rms_scale(rows):
    return lax.rsqrt(jnp.mean(rows * rows, axis=-1, keepdims=True) + EPSILON)


def rms_backward(rows, inv_scale, gain_vec, grad_in):
    weighted = grad_in * gain_vec
    inner_mean = jnp.mean(weighted * rows, axis=-1, keepdims=True)
    d_rows = inv_scale * weighted - rows * (inv_scale * inv_scale * inv_scale) * inner_mean
    return d_rows, jnp.sum(grad_in * rows * inv_scale, axis=0)


def rope_tables(positions):
    half_dim = HEAD_DIM // 2
    frequency = jnp.exp(
        jnp.arange(half_dim, dtype=F32) * (-2.0 * math.log(ROPE_BASE) / HEAD_DIM)
    )
    angle = positions.astype(F32)[:, None] * frequency[None, :]
    cosine, sine = jnp.cos(angle), jnp.sin(angle)
    return (
        jnp.concatenate([cosine, cosine], axis=1),
        jnp.concatenate([-sine, sine], axis=1),
    )


def positions_of(span_order, storage, span_length):
    return jnp.take(span_order, storage // span_length) * span_length + storage % span_length


def rotated(rows, scale, gain, cosine, sine):
    normed = rows * scale * gain
    return (normed * cosine + pltpu.roll(normed, HEAD_DIM // 2, 1) * sine).astype(BF16)


def unrotated(rows, cosine, sine):
    return rows * cosine - pltpu.roll(rows, HEAD_DIM // 2, 1) * sine


def head_probs(query, key, q_pos, k_pos):
    scores = jnp.where(k_pos <= q_pos, mm_t(query, key) * FACTOR, MASKED_SCORE)
    expo = jnp.exp(scores - jnp.max(scores, axis=1, keepdims=True))
    return expo / jnp.sum(expo, axis=1, keepdims=True)


def attend_kernel(
    q_ref, k_ref, v_ref, qs_ref, ks_ref, qg_ref, kg_ref, qc_ref, qn_ref, kc_ref, kn_ref,
    qp_ref, kp_ref, out_ref,
):
    query = rotated(q_ref[...], qs_ref[...], qg_ref[...], qc_ref[...], qn_ref[...])
    key = rotated(k_ref[...], ks_ref[...], kg_ref[...], kc_ref[...], kn_ref[...])
    probs = head_probs(query, key, qp_ref[...], kp_ref[...])
    out_ref[...] = mm(probs.astype(BF16), v_ref[...].astype(BF16)).astype(BF16)


def attend_back_kernel(
    q_ref, k_ref, v_ref, qs_ref, ks_ref, qg_ref, kg_ref, qc_ref, qn_ref, kc_ref, kn_ref,
    qp_ref, kp_ref, da_ref, dk_in, dv_in, *refs,
):
    dq_ref, dk_ref, dv_ref = refs[-3:]
    query = rotated(q_ref[...], qs_ref[...], qg_ref[...], qc_ref[...], qn_ref[...])
    key = rotated(k_ref[...], ks_ref[...], kg_ref[...], kc_ref[...], kn_ref[...])
    probs = head_probs(query, key, qp_ref[...], kp_ref[...])
    d_att = da_ref[...]
    d_probs = mm_t(d_att, v_ref[...].astype(BF16))
    inner = jnp.sum(probs * d_probs, axis=1, keepdims=True)
    d_scores = (probs * (d_probs - inner)).astype(BF16)
    dq_ref[...] = unrotated(mm(d_scores, key) * FACTOR, qc_ref[...], qn_ref[...])
    dk = unrotated(t_mm(d_scores, query) * FACTOR, kc_ref[...], kn_ref[...])
    dk_ref[...] = dk_in[...] + dk
    dv_ref[...] = dv_in[...] + t_mm(probs.astype(BF16), d_att)


def attention_specs(rows, seq, heads, h):
    def head_rows(n, at, row=0):
        return pl.BlockSpec((n, HEAD_DIM), lambda i: (row, at + i))

    def fixed(shape, row=0):
        return pl.BlockSpec(shape, lambda i: (row, 0))

    return [
        head_rows(rows, 0, h), head_rows(seq, heads), head_rows(seq, 2 * heads),
        fixed((rows, 1), h), fixed((seq, 1)), head_rows(1, 0), head_rows(1, 0),
        fixed((rows, HEAD_DIM), h), fixed((rows, HEAD_DIM), h),
        fixed((seq, HEAD_DIM)), fixed((seq, HEAD_DIM)),
        fixed((rows, 1), h), fixed((1, seq)),
    ]


def attend(base, rows, h):
    seq, cols = base[0].shape[0], base[0].shape[1] // 3
    heads = cols // HEAD_DIM
    return pl.pallas_call(
        attend_kernel,
        grid=(heads,),
        in_specs=attention_specs(rows, seq, heads, h),
        out_specs=pl.BlockSpec((rows, HEAD_DIM), lambda i: (0, i)),
        out_shape=jax.ShapeDtypeStruct((rows, cols), BF16),
        compiler_params=pltpu.CompilerParams(vmem_limit_bytes=48 * MIB),
        cost_estimate=pl.CostEstimate(
            flops=4 * rows * seq * cols, bytes_accessed=8 * MIB, transcendentals=rows * seq * heads
        ),
    )(*base)


def attend_back(base, rows, h, d_att, dk, dv, earlier):
    seq, cols = base[0].shape[0], base[0].shape[1] // 3
    heads = cols // HEAD_DIM
    q_out = pl.BlockSpec((rows, HEAD_DIM), lambda i: (0, i))
    k_out = pl.BlockSpec((seq, HEAD_DIM), lambda i: (0, i))
    return pl.pallas_call(
        attend_back_kernel,
        grid=(heads,),
        in_specs=attention_specs(rows, seq, heads, h)
        + [q_out, k_out, k_out]
        + [pl.BlockSpec(memory_space=pl.ANY)] * len(earlier),
        out_specs=[q_out, k_out, k_out],
        out_shape=[
            jax.ShapeDtypeStruct((rows, cols), F32),
            jax.ShapeDtypeStruct((seq, cols), F32),
            jax.ShapeDtypeStruct((seq, cols), F32),
        ],
        compiler_params=pltpu.CompilerParams(vmem_limit_bytes=48 * MIB),
        cost_estimate=pl.CostEstimate(
            flops=10 * rows * seq * cols, bytes_accessed=16 * MIB, transcendentals=rows * seq * heads
        ),
    )(*base, d_att, dk, dv, *earlier)


def expert_kernel(
    experts, own, step, x_ref, dh_ref, member_ref, router_ref, pick_ref, wg_hbm, wu_hbm,
    hid_ref, da_ref, db_ref, dx_ref, coef_ref, wg, wu, sems,
):
    i = pl.program_id(0)

    def loads(j):
        return (
            pltpu.make_async_copy(wg_hbm.at[j], wg.at[j], sems.at[0, j]),
            pltpu.make_async_copy(wu_hbm.at[j], wu.at[j], sems.at[1, j]),
        )

    @pl.when(i == 0)
    def _():
        for j in range(own):
            for copy in loads(j):
                copy.start()

    logits = mm(x_ref[...], router_ref[...])
    lane = lax.broadcasted_iota(jnp.int32, logits.shape, 1)
    logits = jnp.where(lane < experts, logits, MASKED_SCORE)
    expo = jnp.exp(logits - jnp.max(logits, axis=1, keepdims=True))
    router = expo / jnp.sum(expo, axis=1, keepdims=True)
    chosen = router * member_ref[...].astype(F32)
    coef = jnp.zeros_like(router)
    ff = wg.shape[2]
    for j in range(own):

        @pl.when(i == 0)
        def _():
            for copy in loads(j):
                copy.wait()

        pick = pick_ref[j : j + 1, :]
        gate = jnp.sum(chosen * pick, axis=1, keepdims=True)
        flow = jnp.zeros_like(gate)
        for f in range(0, ff, step):
            cut = slice(f, f + step)
            a = mm(x_ref[...], wg[j, :, cut])
            b = mm(x_ref[...], wu[j, :, cut])
            d_hid = dh_ref[j, :, cut].astype(F32)
            sig = jax.nn.sigmoid(a)
            silu = a * sig
            hid = silu * b
            flow = flow + jnp.sum(hid * d_hid, axis=1, keepdims=True)
            hid_ref[j, :, cut] = (gate * hid).astype(BF16)
            d_hid = d_hid * gate
            da_ref[j, :, cut] = (d_hid * b * (sig + silu * (1.0 - sig))).astype(BF16)
            db_ref[j, :, cut] = (d_hid * silu).astype(BF16)
        coef = coef + flow * gate * (pick - router)
    low = coef.astype(BF16)
    coef_ref[...] = low
    width = x_ref.shape[1]
    for n in range(0, width, step):
        cut = slice(n, n + step)
        part = mm_t(low, router_ref[cut, :])
        for j in range(own):
            part = part + mm_t(da_ref[j], wg[j, cut, :]) + mm_t(db_ref[j], wu[j, cut, :])
        dx_ref[:, cut] = part.astype(BF16)


def expert_pass(x, d_hid, member, router_w, pick, w_gate, w_up, experts):
    rows, width = x.shape
    own, _, ff = w_gate.shape
    tile = 256
    by_row = pl.BlockSpec((tile, width), lambda i: (i, 0))
    by_lane = pl.BlockSpec((tile, LANES), lambda i: (i, 0))
    by_expert = pl.BlockSpec((own, tile, ff), lambda i: (0, i, 0))
    return pl.pallas_call(
        functools.partial(expert_kernel, experts, own, 512),
        grid=(rows // tile,),
        in_specs=[
            by_row, by_expert, by_lane,
            pl.BlockSpec((width, LANES), lambda i: (0, 0)),
            pl.BlockSpec(pick.shape, lambda i: (0, 0)),
            pl.BlockSpec(memory_space=pl.ANY),
            pl.BlockSpec(memory_space=pl.ANY),
        ],
        out_specs=[by_expert] * 3 + [by_row, by_lane],
        out_shape=[jax.ShapeDtypeStruct((own, rows, ff), BF16)] * 3
        + [jax.ShapeDtypeStruct((rows, width), BF16), jax.ShapeDtypeStruct((rows, LANES), BF16)],
        scratch_shapes=[
            pltpu.VMEM((own, width, ff), BF16),
            pltpu.VMEM((own, width, ff), BF16),
            pltpu.SemaphoreType.DMA((2, own)),
        ],
        compiler_params=pltpu.CompilerParams(vmem_limit_bytes=56 * MIB),
        cost_estimate=pl.CostEstimate(
            flops=8 * rows * width * ff * own, bytes_accessed=40 * MIB, transcendentals=0
        ),
    )(x, d_hid, member, router_w, pick, w_gate, w_up)


def weight_kernel(n, x_ref, d_ref, *refs):
    out_ref = refs[-1]
    width = d_ref.shape[1]
    out_ref[:, :width] = t_mm(x_ref[...], d_ref[...]).astype(BF16)
    total = t_mm(refs[0][...], refs[n][...])
    for h in range(1, n):
        total = total + t_mm(refs[h][...], refs[n + h][...])
    out_ref[:, width:] = total.astype(BF16)


def attention_grads(xn, d_qkv, attended, dl, cols, earlier):
    seq, width = xn.shape
    n = len(attended)

    def by_column(a):
        return pl.BlockSpec((a.shape[0], cols), lambda i: (0, i))

    def fixed(a):
        return pl.BlockSpec(a.shape, lambda i: (0, 0))

    return pl.pallas_call(
        functools.partial(weight_kernel, n),
        grid=(width // cols,),
        in_specs=[by_column(xn), fixed(d_qkv)]
        + [fixed(a) for a in attended]
        + [by_column(a) for a in dl]
        + [pl.BlockSpec(memory_space=pl.ANY)] * len(earlier),
        out_specs=pl.BlockSpec((cols, 4 * cols), lambda i: (i, 0)),
        out_shape=jax.ShapeDtypeStruct((width, 4 * cols), BF16),
        compiler_params=pltpu.CompilerParams(vmem_limit_bytes=48 * MIB),
        cost_estimate=pl.CostEstimate(
            flops=8 * seq * width * cols, bytes_accessed=20 * MIB, transcendentals=0
        ),
    )(xn, d_qkv, *attended, *dl, *earlier)


def partial_kernel(n, part, d_ref, w_ref, *refs):
    out_ref = refs[-1]
    rows, halves = n * part, d_ref.shape[0] // (n * part)
    for h in range(halves):
        total = mm_t(d_ref[h * rows : (h + 1) * rows, :], w_ref[...]).astype(BF16)
        for c in range(n):
            out_ref[0, c, h * part : (h + 1) * part, :] = total[c * part : (c + 1) * part, :]


def input_partial(d_qkv, weights, part, earlier):
    n = lax.axis_size("ctx")
    seq, depth = d_qkv.shape
    width = weights.shape[0]
    rows = seq // n
    return pl.pallas_call(
        functools.partial(partial_kernel, n, part),
        grid=(2,),
        in_specs=[
            pl.BlockSpec((seq, depth), lambda i: (0, 0)),
            pl.BlockSpec((width // 2, depth), lambda i: (i, 0)),
        ]
        + [pl.BlockSpec(memory_space=pl.ANY)] * len(earlier),
        out_specs=pl.BlockSpec((1, n, rows, width // 2), lambda i: (i, 0, 0, 0)),
        out_shape=jax.ShapeDtypeStruct((2, n, rows, width // 2), BF16),
        compiler_params=pltpu.CompilerParams(vmem_limit_bytes=48 * MIB),
    )(d_qkv, weights, *earlier)


def give_kernel(n, count, table, *refs):
    for k in range(count):
        total = t_mm(refs[0][...], refs[(k + 1) * n][0])
        for h in range(1, n):
            total = total + t_mm(refs[h][...], refs[(k + 1) * n + h][0])
        refs[len(refs) - count + k][0] = total.astype(BF16)


def given_grads(table, lefts, rights, block, j, earlier):
    n, blocks = len(lefts), table.shape[0]
    flat = [a for right in rights for a in right]
    columns = flat[0].shape[2]
    return pl.pallas_call(
        functools.partial(give_kernel, n, len(rights)),
        grid_spec=pltpu.PrefetchScalarGridSpec(
            num_scalar_prefetch=1,
            grid=(blocks,),
            in_specs=[pl.BlockSpec((a.shape[0], block), lambda i, t: (0, t[i])) for a in lefts]
            + [pl.BlockSpec((1,) + a.shape[1:], lambda i, t: (j, 0, 0)) for a in flat]
            + [pl.BlockSpec(memory_space=pl.ANY)] * len(earlier),
            out_specs=[pl.BlockSpec((1, block, columns), lambda i, t: (i, 0, 0))] * len(rights),
        ),
        out_shape=[jax.ShapeDtypeStruct((blocks, block, columns), BF16)] * len(rights),
        compiler_params=pltpu.CompilerParams(vmem_limit_bytes=48 * MIB),
    )(table, *lefts, *flat, *earlier)


def mid_kernel(n, x_ref, own_ref, gain_ref, *refs):
    total = x_ref[...].astype(F32) + own_ref[...]
    for got in refs[: n - 1]:
        total = total + got[...].astype(F32)
    res_ref, scale_ref, low_ref = refs[-3:]
    scale = lax.rsqrt(jnp.mean(total * total, axis=1, keepdims=True) + EPSILON)
    res_ref[...] = total
    scale_ref[...] = scale
    low_ref[...] = (total * scale * gain_ref[...]).astype(BF16)


def middle(x, own_block, got, gain, earlier):
    rows, width = x.shape
    whole = pl.BlockSpec(memory_space=pltpu.VMEM)
    return pl.pallas_call(
        functools.partial(mid_kernel, len(got) + 1),
        in_specs=[whole] * (3 + len(got)) + [pl.BlockSpec(memory_space=pl.ANY)] * len(earlier),
        out_specs=[whole] * 3,
        out_shape=[
            jax.ShapeDtypeStruct((rows, width), F32),
            jax.ShapeDtypeStruct((rows, 1), F32),
            jax.ShapeDtypeStruct((rows, width), BF16),
        ],
        compiler_params=pltpu.CompilerParams(vmem_limit_bytes=60 * MIB),
    )(x, own_block, gain[None], *got, *earlier)


def res_kernel(res_ref, scale_ref, gain_ref, grad_ref, mid_ref, *refs):
    out_ref, low_ref, gain_out = refs[-3:]
    rows, scale = res_ref[...], scale_ref[...]
    grad_in = mid_ref[...].astype(F32)
    weighted = grad_in * gain_ref[...]
    inner = jnp.mean(weighted * rows, axis=1, keepdims=True)
    total = grad_ref[...] + scale * weighted - rows * (scale * scale * scale) * inner
    out_ref[...] = total
    low_ref[...] = total.astype(BF16)
    gain_out[...] = jnp.sum(grad_in * rows * scale, axis=0, keepdims=True)


def residual_back(residual, scale, gain, grad, d_mid, earlier):
    rows, width = residual.shape
    whole = pl.BlockSpec(memory_space=pltpu.VMEM)
    return pl.pallas_call(
        res_kernel,
        in_specs=[whole] * 5 + [pl.BlockSpec(memory_space=pl.ANY)] * len(earlier),
        out_specs=[whole] * 3,
        out_shape=[
            jax.ShapeDtypeStruct((rows, width), F32),
            jax.ShapeDtypeStruct((rows, width), BF16),
            jax.ShapeDtypeStruct((1, width), F32),
        ],
        compiler_params=pltpu.CompilerParams(vmem_limit_bytes=60 * MIB),
    )(residual, scale, gain[None], grad, d_mid, *earlier)


def meet(peers):
    barrier = pltpu.get_barrier_semaphore()
    for peer in peers:
        pl.semaphore_signal(barrier, inc=1, device_id=peer, device_id_type=pl.DeviceIdType.MESH)
    pl.semaphore_wait(barrier, len(peers))


def ctx_sum_kernel(n, x_ref, *refs):
    out_ref, slots, send, recv = refs[-4:]
    me = lax.axis_index("ctx")
    peers = [{"ctx": lax.rem(me + d, n)} for d in range(1, n)]
    meet(peers)
    slots[me] = x_ref[...]
    copies = [
        pltpu.make_async_remote_copy(
            src_ref=x_ref, dst_ref=slots.at[me], send_sem=send.at[d], recv_sem=recv.at[d],
            device_id=peer, device_id_type=pl.DeviceIdType.MESH,
        )
        for d, peer in enumerate(peers)
    ]
    for copy in copies:
        copy.start()
    for copy in copies:
        copy.wait()
    total = slots[0]
    for k in range(1, n):
        total = total + slots[k]
    out_ref[...] = total


def ctx_sum(x, number, earlier=()):
    n = lax.axis_size("ctx")
    whole = pl.BlockSpec(memory_space=pltpu.VMEM)
    return pl.pallas_call(
        functools.partial(ctx_sum_kernel, n),
        in_specs=[whole] + [pl.BlockSpec(memory_space=pl.ANY)] * len(earlier),
        out_specs=whole,
        out_shape=jax.ShapeDtypeStruct(x.shape, F32),
        scratch_shapes=[
            pltpu.VMEM((n,) + x.shape, F32),
            pltpu.SemaphoreType.DMA((n - 1,)),
            pltpu.SemaphoreType.DMA((n - 1,)),
        ],
        compiler_params=pltpu.CompilerParams(collective_id=number, has_side_effects=True),
    )(x, *earlier)


class SmallSum:
    def __init__(self, n_ctx, n_exp, x, first, second, sems):
        self.x, self.first, self.second, self.sems = x, first, second, sems
        self.c_at, self.e_at = lax.axis_index("ctx"), lax.axis_index("exp")
        self.across = [{"exp": lax.rem(self.e_at + d, n_exp)} for d in range(1, n_exp)]
        self.along = [{"ctx": lax.rem(self.c_at + d, n_ctx)} for d in range(1, n_ctx)]

    def copy(self, src, dst, step, d, peer):
        return pltpu.make_async_remote_copy(
            src_ref=src, dst_ref=dst, send_sem=self.sems.at[2 * step, d],
            recv_sem=self.sems.at[2 * step + 1, d], device_id=peer,
            device_id_type=pl.DeviceIdType.MESH,
        )

    def over_exp(self):
        return [
            self.copy(self.x.at[peer["exp"]], self.first.at[self.e_at], 0, d, peer)
            for d, peer in enumerate(self.across)
        ]

    def over_ctx(self):
        mine = self.second.at[self.c_at]
        return [self.copy(mine, mine, 1, d, peer) for d, peer in enumerate(self.along)]

    def begin(self):
        for copy in self.over_exp():
            copy.start()
        self.first[self.e_at] = self.x[self.e_at]

    def pass_on(self):
        for copy in self.over_exp():
            copy.wait()
        total = self.first[0]
        for k in range(1, self.first.shape[0]):
            total = total + self.first[k]
        self.second[self.c_at] = total
        for copy in self.over_ctx():
            copy.start()

    def finish(self, out):
        for copy in self.over_ctx():
            copy.wait()
        total = self.second[0]
        for k in range(1, self.second.shape[0]):
            total = total + self.second[k]
        out[...] = total

    @staticmethod
    def scratch(n_ctx, shape):
        return [
            pltpu.VMEM(shape, F32),
            pltpu.VMEM((n_ctx,) + shape[1:], F32),
            pltpu.SemaphoreType.DMA((4, max(n_ctx, shape[0]) - 1)),
        ]


def halving_masks(order):
    masks = [0]
    for bit in order[::-1]:
        masks = masks + [m | (1 << bit) for m in masks]
    return masks


def flip(value, mask):
    bit = 0
    while mask >> bit:
        if (mask >> bit) & 1:
            value = value + (1 << bit) * (1 - 2 * lax.rem(lax.div(value, 1 << bit), 2))
        bit += 1
    return value


class Halving:
    def __init__(
        self, n, me, source, blocks, got, send, recv, out, first=None, acc=None, kept=None
    ):
        self.n, self.me, self.source, self.blocks, self.got = n, me, source, blocks, got
        self.send, self.recv, self.out = send, recv, out
        self.first, self.acc, self.kept = first, out if acc is None else acc, kept
        bits = list(range(n.bit_length() - 1))
        self.own = out.shape[0]
        self.orders = [bits if j % 2 == 0 else bits[::-1] for j in range(self.own)]
        self.masks = [halving_masks(order) for order in self.orders]
        self.steps = len(bits)

    def target(self, j, k):
        return flip(self.me, self.masks[j][k])

    def slot(self, s, k):
        made = 0 if self.first is None else self.n >> 1
        return self.n - (self.n >> s) + k - (self.n >> (s + 1)) - made

    def copy(self, j, s, k):
        given = self.source is not None and s == 0
        at = self.slot(s, k)
        return pltpu.make_async_remote_copy(
            src_ref=self.source.at[j, self.target(j, k)] if given else self.blocks.at[j, k - 1],
            dst_ref=self.got.at[j, at],
            send_sem=self.send.at[j, at],
            recv_sem=self.recv.at[j, at],
            device_id={"ctx": flip(self.me, 1 << self.orders[j][s])},
            device_id_type=pl.DeviceIdType.MESH,
        )

    def going(self, s):
        return [
            (j, k)
            for k in range((self.n >> s) - 1, (self.n >> (s + 1)) - 1, -1)
            for j in range(self.own)
        ]

    def begin(self, value=None):
        for j, k in self.going(0) if self.first is None else []:
            if value is not None:
                self.blocks[j, k - 1] = value(j, self.target(j, k)).astype(BF16)
            self.copy(j, 0, k).start()
        for k in range(self.n // 2 - 1, 0, -1):
            for j in range(self.own):
                at = self.target(j, k)
                mine = self.source[j, at] if value is None else value(j, at)
                self.blocks[j, k - 1] = mine.astype(BF16)

    def rest(self, value=None):
        for j in range(self.own):
            self.acc[j] = self.source[j, self.me].astype(F32) if value is None else value(j, self.me)

    def arrived(self, j, k, steps):
        total = None
        for s in range(steps):
            sent = k + (self.n >> (s + 1))
            if s == 0 and self.first is not None:
                part = self.first[j][k].astype(F32)
            else:
                self.copy(j, s, sent).wait_recv()
                part = self.got[j, self.slot(s, sent)].astype(F32)
            total = part if total is None else total + part
        return total

    def pass_on(self):
        for s in range(1, self.steps):
            for j, k in self.going(s):
                mine = self.blocks[j, k - 1] if self.kept is None else self.kept[j, k]
                total = mine.astype(F32) + self.arrived(j, k, s)
                self.blocks[j, k - 1] = total.astype(BF16)
                self.copy(j, s, k).start()

    def finish(self):
        for j in range(self.own):
            mine = self.acc[j] if self.kept is None else self.kept[j, 0].astype(F32)
            self.out[j] = (mine + self.arrived(j, 0, self.steps)).astype(self.out.dtype)
        for s in range(0 if self.first is None else 1, self.steps):
            for j, k in self.going(s):
                self.copy(j, s, k).wait_send()

    @staticmethod
    def scratch(own, n, rows, columns):
        return [
            pltpu.VMEM((own, n - 1, rows, columns), BF16),
            pltpu.VMEM((own, n - 1, rows, columns), BF16),
            pltpu.SemaphoreType.DMA((own, n - 1)),
            pltpu.SemaphoreType.DMA((own, n - 1)),
        ]


def ctx_peers(n, me):
    return [{"ctx": lax.rem(me + d, n)} for d in range(1, n)]


def entry(ref, j):
    return ref.at[j] if len(ref.shape) == 3 else ref


def product(lefts, rights, block):
    def value(j, at):
        total = None
        for left, right in zip(lefts, rights):
            columns = pl.ds(pl.multiple_of(at * block, LANES), block)
            part = t_mm(entry(left, j)[:, columns], entry(right, j)[...])
            total = part if total is None else total + part
        return total

    return value


def down_kernel(n, halves, *refs):
    hid, grad, w_down = refs[:halves], refs[halves : 2 * halves], refs[2 * halves]
    refs = refs[2 * halves + 1 :]
    out, ys, scratch = refs[0], refs[1 : 1 + halves], refs[1 + halves :]
    me = lax.axis_index("ctx")
    meet(ctx_peers(n, me))
    sums = Halving(n, me, None, *scratch[:4], out, acc=scratch[4])
    value = product(hid, grad, hid[0].shape[2] // n)
    sums.begin(value)
    sums.rest(value)
    width = w_down.shape[2]
    for h in range(halves):
        for start in range(0, width, 512):
            cut = slice(start, start + 512)
            total = mm(hid[h][0], w_down[0, :, cut])
            for j in range(1, w_down.shape[0]):
                total = total + mm(hid[h][j], w_down[j, :, cut])
            ys[h][:, cut] = total.astype(BF16)
    sums.pass_on()
    sums.finish()


def gate_kernel(n, halves, *refs):
    mids, gate_pres, up_pres = [refs[k * halves : (k + 1) * halves] for k in range(3)]
    own = gate_pres[0].shape[0]
    partial, first = refs[3 * halves], refs[3 * halves + 1 : 3 * halves + 1 + own]
    out, dxn, kept = refs[-12:-9]
    me = lax.axis_index("ctx")
    meet(ctx_peers(n, me))
    rows = Halving(n, me, partial, *refs[-9:-5], dxn)
    rows.begin()
    block = mids[0].shape[1] // n
    sums = Halving(n, me, None, *refs[-5:-1], out, first, refs[-1])
    value = product(mids, gate_pres, block)
    sums.begin(value)
    sums.pass_on()
    rows.pass_on()
    sums.rest(value)
    rows.rest()
    value = product(mids, up_pres, block)
    for k in range(n // 2):
        for j in range(own):
            kept[j, k] = value(j, sums.target(j, k)).astype(BF16)
    rows.finish()
    sums.finish()


def up_kernel(n, *refs):
    piece, x, kept = refs[:3]
    out, *whole = refs[-16:-11]
    small_out, slots, send, recv = refs[-11:-7]
    me = lax.axis_index("ctx")
    smalls = SmallSum(n, x.shape[0], x, *refs[-7:-4])
    meet(smalls.across + smalls.along)
    smalls.begin()
    bits = list(range(n.bit_length() - 1))
    half = piece.shape[0] // 2

    def doubling(i, s):
        order = bits if i == 0 else bits[::-1]
        lines = pl.ds(i * half, half)
        copies = []
        for m in halving_masks(order[:s]):
            at = flip(me, m)
            sem = i, (1 << s) - 1 + len(copies)
            copies.append(
                pltpu.make_async_remote_copy(
                    src_ref=slots.at[at, lines] if m else piece.at[lines],
                    dst_ref=slots.at[at, lines],
                    send_sem=send.at[sem],
                    recv_sem=recv.at[sem],
                    device_id={"ctx": flip(me, 1 << order[s])},
                    device_id_type=pl.DeviceIdType.MESH,
                )
            )
        return copies

    first = refs[3 : 3 + kept.shape[0]]
    sums = Halving(n, me, None, *refs[-4:], out, first, kept=kept)
    for i in range(2):
        for copy in doubling(i, 0):
            copy.start()
    sums.pass_on()
    smalls.pass_on()
    slots[me] = piece[...]
    for s in range(1, len(bits)):
        for i in range(2):
            for copy in doubling(i, s - 1):
                copy.wait_recv()
            for copy in doubling(i, s):
                copy.start()
    smalls.finish(small_out)
    sums.finish()
    for i in range(2):
        for copy in doubling(i, len(bits) - 1):
            copy.wait_recv()
        for s in range(len(bits)):
            for copy in doubling(i, s):
                copy.wait_send()
    cols = piece.shape[1] // len(whole)
    for c in range(n):
        for k, ref in enumerate(whole):
            ref[:, c * cols : (c + 1) * cols] = slots[c, :, k * cols : (k + 1) * cols]


class Doubling:
    def __init__(self, axis, order, last, block, slot, sems, base):
        self.me, self.axis, self.order, self.last = lax.axis_index(axis), axis, order, last
        self.block, self.slot, self.sems, self.base = block, slot, sems, base
        self.steps = [halving_masks(order[:s]) for s in range(len(order) + 1)]
        self.keys = [(bit, m) for bit, ms in zip(order, self.steps) for m in ms]
        if last is not None:
            self.keys += [(last, m) for m in self.steps[-1]]

    def copy(self, bit, m):
        at = self.base + self.keys.index((bit, m))
        place = self.slot(flip(self.me, m))
        return pltpu.make_async_remote_copy(
            src_ref=place if m else self.block,
            dst_ref=place,
            send_sem=self.sems.at[0, at],
            recv_sem=self.sems.at[1, at],
            device_id={self.axis: flip(self.me, 1 << bit)},
            device_id_type=pl.DeviceIdType.MESH,
        )

    def step(self, s):
        fresh = [0]
        if s:
            fresh = [m | (1 << self.order[s - 1]) for m in self.steps[s - 1]]
            for m in self.steps[s - 1]:
                self.copy(self.order[s - 1], m).wait_recv()
        if s < len(self.order):
            for m in self.steps[s]:
                self.copy(self.order[s], m).start()
        if self.last is not None:
            for m in fresh:
                self.copy(self.last, m).start()

    def finish(self):
        if self.last is not None:
            for m in self.steps[-1]:
                self.copy(self.last, m).wait_recv()
        for key in self.keys:
            self.copy(*key).wait_send()


def start_kernel(n_ctx, n_exp, w_ref, x_ref, small_ref, w_out, x_out, small_out, sems, local_sems):
    c_at, e_at = lax.axis_index("ctx"), lax.axis_index("exp")
    c_bits, e_bits = n_ctx.bit_length() - 1, n_exp.bit_length() - 1
    meet(
        [{"ctx": flip(c_at, 1 << b)} for b in range(c_bits)]
        + [{"exp": flip(e_at, 1 << b)} for b in range(e_bits)]
    )
    far = list(range(1, e_bits))
    near = list(range(c_bits))
    half = w_ref.shape[0] // 2
    moves, base = [], 0

    def add(axis, order, last, block, slot):
        moves.append(Doubling(axis, order, last, block, slot, sems, base))
        return base + len(moves[-1].keys)

    base = add("exp", far, 0, small_ref, lambda at: small_out.at[at])
    for i, order in enumerate((far[::-1], far)):
        lines = pl.ds(i * half, half)
        base = add(
            "exp", order, 0, w_ref.at[lines], lambda at, lines=lines: w_out.at[at, lines]
        )
    for i, order in enumerate((near[::-1], near)):
        base = add("ctx", order, None, x_ref.at[i], lambda at, i=i: x_out.at[i, at])
    own = [
        pltpu.make_async_copy(w_ref, w_out.at[e_at], local_sems.at[0]),
        pltpu.make_async_copy(small_ref, small_out.at[e_at], local_sems.at[1]),
        pltpu.make_async_copy(x_ref.at[0], x_out.at[0, c_at], local_sems.at[2]),
        pltpu.make_async_copy(x_ref.at[1], x_out.at[1, c_at], local_sems.at[3]),
    ]
    for s in range(max(len(far), len(near)) + 1):
        for move in moves:
            if s <= len(move.order):
                move.step(s)
        if s == 0:
            for copy in own:
                copy.start()
    for move in moves:
        move.finish()
    for copy in own:
        copy.wait()


def gather_start(w, x, small):
    n_ctx, n_exp = lax.axis_size("ctx"), lax.axis_size("exp")
    count = 3 * (n_exp - 1) + 2 * (n_ctx - 1)
    return pl.pallas_call(
        functools.partial(start_kernel, n_ctx, n_exp),
        in_specs=[ANY] * 3,
        out_specs=[ANY] * 3,
        out_shape=[
            jax.ShapeDtypeStruct((n_exp,) + w.shape, BF16),
            jax.ShapeDtypeStruct((x.shape[0], n_ctx) + x.shape[1:], BF16),
            jax.ShapeDtypeStruct((n_exp,) + small.shape, BF16),
        ],
        scratch_shapes=[pltpu.SemaphoreType.DMA((2, count)), pltpu.SemaphoreType.DMA((4,))],
        compiler_params=pltpu.CompilerParams(collective_id=6, has_side_effects=True),
    )(w, x, small)


def hold_kernel(*refs):
    pass


def held(arrays, earlier):
    n = len(arrays)
    return pl.pallas_call(
        hold_kernel,
        in_specs=[ANY] * (n + len(earlier)),
        out_specs=[ANY] * n,
        out_shape=[jax.ShapeDtypeStruct(a.shape, a.dtype) for a in arrays],
        input_output_aliases={i: i for i in range(n)},
        compiler_params=pltpu.CompilerParams(vmem_limit_bytes=60 * MIB),
    )(*arrays, *earlier)


def mask_kernel(x_ref, valid_ref, *refs):
    refs[-1][...] = (x_ref[...].astype(F32) * valid_ref[...]).astype(BF16)


def masked(x, valid, earlier):
    blocks = [pl.BlockSpec(a.shape, lambda i: (0, 0)) for a in (x, valid)]
    return pl.pallas_call(
        mask_kernel,
        grid=(1,),
        in_specs=blocks + [ANY] * len(earlier),
        out_specs=blocks[0],
        out_shape=jax.ShapeDtypeStruct(x.shape, BF16),
    )(x, valid, *earlier)


VMEM = pl.BlockSpec(memory_space=pltpu.VMEM)
ANY = pl.BlockSpec(memory_space=pl.ANY)


def exchange(kernel, number, operands, earlier, outs, scratch):
    n = lax.axis_size("ctx")
    return pl.pallas_call(
        kernel,
        in_specs=[VMEM] * len(operands) + [ANY] * len(earlier),
        out_specs=[VMEM] * len(outs),
        out_shape=outs,
        scratch_shapes=scratch,
        compiler_params=pltpu.CompilerParams(
            collective_id=number, has_side_effects=True, vmem_limit_bytes=60 * MIB
        ),
    )(*operands, *earlier)


def down_sums(hid, grad, w_down):
    n, halves = lax.axis_size("ctx"), len(hid)
    own, ff, width = w_down.shape
    outs = [jax.ShapeDtypeStruct((own, ff // n, width), BF16)]
    outs += [jax.ShapeDtypeStruct((h.shape[1], width), BF16) for h in hid]
    return exchange(
        functools.partial(down_kernel, n, halves), 3, [*hid, *grad, w_down], (), outs,
        Halving.scratch(own, n, ff // n, width) + [pltpu.VMEM((own, ff // n, width), F32)],
    )


def gate_sums(mids, gate_pres, up_pres, partial, first, earlier):
    n, halves = lax.axis_size("ctx"), len(mids)
    own, _, ff = gate_pres[0].shape
    rows = mids[0].shape[1] // n
    shape = partial.shape
    outs = [
        jax.ShapeDtypeStruct((own, rows, ff), BF16),
        jax.ShapeDtypeStruct((shape[0],) + shape[2:], F32),
        jax.ShapeDtypeStruct((own, n // 2, rows, ff), BF16),
    ]
    return exchange(
        functools.partial(gate_kernel, n, halves), 4,
        [*mids, *gate_pres, *up_pres, partial, *first], earlier, outs,
        Halving.scratch(shape[0], n, *shape[2:])
        + Halving.scratch(own, n // 2, rows, ff)
        + [pltpu.VMEM((own, rows, ff), F32)],
    )


def up_sums(kept, first, piece, smalls):
    n = lax.axis_size("ctx")
    own, _, rows, ff = kept.shape
    shard, width = piece.shape
    outs = [jax.ShapeDtypeStruct((own, rows, ff), BF16)]
    outs += [jax.ShapeDtypeStruct((shard, n * width // 4), BF16) for _ in range(4)]
    outs += [jax.ShapeDtypeStruct(smalls.shape[1:], F32)]
    return exchange(
        functools.partial(up_kernel, n), 5, [piece, smalls, kept, *first], (), outs,
        [
            pltpu.VMEM((n,) + piece.shape, BF16),
            pltpu.SemaphoreType.DMA((2, n - 1)),
            pltpu.SemaphoreType.DMA((2, n - 1)),
        ]
        + SmallSum.scratch(n, smalls.shape)
        + Halving.scratch(own, n // 2, rows, ff),
    )


def gather(block, axis):
    return lax.all_gather(block, axis, axis=0, tiled=True)


def scatter_sum(block, axis, dimension=0):
    return lax.psum_scatter(block, axis, scatter_dimension=dimension, tiled=True)


def after(value, *earlier):
    return lax.optimization_barrier((value,) + earlier)[0]


def swap(block, bits):
    n = lax.axis_size("ctx")
    return lax.ppermute(block, "ctx", [(i, i ^ bits) for i in range(n)])


def take(block, at, size=1, axis=0):
    return lax.dynamic_slice_in_dim(block, at, size, axis)


def gather_ctx(block, axis):
    n, me = lax.axis_size("ctx"), lax.axis_index("ctx")
    parts = [block] + [swap(block, d) for d in range(1, n)]
    shape = block.shape[:axis] + (n,) + block.shape[axis:]
    out = jnp.zeros(shape, block.dtype)
    for d, piece in enumerate(parts):
        out = lax.dynamic_update_slice_in_dim(out, jnp.expand_dims(piece, axis), me ^ d, axis)
    return out


def local(
    tokens, cotangent, lengths, span_order, routes,
    w_query, w_key, w_value, w_output, w_router,
    gain_attn, gain_query, gain_key, gain_mlp,
    w_gate, w_up, w_down,
):
    n_ctx, n_exp = lax.axis_size("ctx"), lax.axis_size("exp")
    c_at, e_at = lax.axis_index("ctx"), lax.axis_index("exp")
    rows = tokens.shape[1]
    width = tokens.shape[2]
    seq = rows * n_ctx
    cols = width // n_ctx
    shard = width // n_exp
    own = w_gate.shape[0]
    ff = w_gate.shape[2]
    experts = w_router.shape[1]
    seq_length = lengths[0]
    halves = 2
    part = rows // halves
    half_seq = part * n_ctx

    ratio = n_exp // n_ctx
    moves = []
    for c in range(n_ctx):
        for e in range(n_exp):
            moves.append(((e // ratio) * n_exp + c * ratio + e % ratio, c * n_exp + e))
    out_piece = lax.ppermute(take(w_output, c_at * cols, cols, 1), ("ctx", "exp"), moves)

    storage = jnp.arange(seq, dtype=jnp.int32)
    storage = (storage % half_seq // part) * rows + storage // half_seq * part + storage % part
    positions = positions_of(span_order, storage, rows // 2)
    my_positions = positions_of(
        span_order, c_at * rows + jnp.arange(rows, dtype=jnp.int32), rows // 2
    )
    valid = (my_positions < seq_length).astype(F32)[:, None]
    small = jnp.concatenate(
        [
            w_router.reshape(-1), gain_attn, gain_query, gain_key, gain_mlp,
            routes[0].astype(BF16).reshape(-1),
        ]
    )
    used = small.shape[0]
    lines = -(-used // (16 * LANES)) * 16
    small = jnp.pad(small, (0, lines * LANES - used)).reshape(lines, LANES)
    pieces = [take(w, c_at * cols, cols, 1) for w in (w_query, w_key, w_value)]
    weights, x_low, small_all = gather_start(
        jnp.concatenate(pieces + [out_piece], axis=1), tokens[0].reshape(halves, part, width), small
    )
    weights = weights.reshape(width, 4 * cols)
    x_low = x_low.reshape(seq, width)
    small_all = small_all.reshape(n_exp, lines * LANES)[:, :used]
    at = shard * experts
    router_w = small_all[:, :at].reshape(width, experts)
    router_w = jnp.pad(router_w, ((0, 0), (0, LANES - experts)))
    gains = []
    for _ in range(4):
        gains.append(small_all[:, at : at + shard].reshape(width).astype(F32))
        at += shard
    attn_gain, query_gain_all, key_gain_all, mlp_gain = gains
    routes_all = small_all[:, at:].reshape(n_exp, rows, routes.shape[2])
    lane = jnp.arange(LANES, dtype=jnp.int32)[None, :]
    query_gain = take(query_gain_all, c_at * cols, cols)
    key_gain = take(key_gain_all, c_at * cols, cols)

    qkv_w = weights[:, : 3 * cols]
    out_w = weights[:, 3 * cols :].reshape(n_ctx, cols, cols).transpose(1, 0, 2).reshape(cols, width)
    x_all = x_low.astype(F32)

    grad_low = masked(cotangent[0], valid, (weights,))
    grad_mine = grad_low.astype(F32)
    grad_parts = [gather(grad_low[h * part : (h + 1) * part], "exp") for h in range(halves)]
    d_hid_parts = [
        jnp.stack([mm_t(g, w_down[j]).astype(BF16) for j in range(own)]) for g in grad_parts
    ]

    cosine, sine = rope_tables(positions)
    xn = (x_all * rms_scale(x_all) * attn_gain).astype(BF16)
    qkv = mm(xn, qkv_w)
    qp, kp = qkv[:, :cols], qkv[:, cols : 2 * cols]
    squares = jnp.stack([jnp.sum(qp * qp, axis=-1), jnp.sum(kp * kp, axis=-1)], axis=0)
    squares = ctx_sum(jnp.pad(squares, ((0, 6), (0, 0))), 0)[:2] / width
    q_scale = lax.rsqrt(squares[0] + EPSILON)[:, None]
    k_scale = lax.rsqrt(squares[1] + EPSILON)[:, None]
    key_positions = jnp.where(positions < seq_length, positions, jnp.int32(1 << 30))
    base = (
        qkv, qkv, qkv, q_scale, k_scale, query_gain[None], key_gain[None],
        cosine, sine, cosine, sine, positions[:, None], key_positions[None],
    )

    attended_parts, mids, residual_parts, scale_parts = [], [], [], []
    for h in range(halves):
        attended = attend(base, half_seq, h)
        attended_parts.append(attended)
        got = []
        for d in range(n_ctx - 1, -1, -1):
            block = mm(take(attended, (c_at ^ d) * part, part), out_w)
            if d:
                got.append(swap(block.astype(BF16), d))
        residual, scale, mid = middle(
            tokens[0, h * part : (h + 1) * part], block, got, mlp_gain,
            (d_hid_parts[h],),
        )
        residual_parts.append(residual)
        scale_parts.append(scale)
        mids.append(gather(mid, "exp"))

    pick = (lane == e_at * own + jnp.arange(max(own, 8), dtype=jnp.int32)[:, None]).astype(F32)
    hid_parts, da_parts, db_parts, coef_parts = [], [], [], []
    dxs = []
    for h in range(halves):
        named = routes_all[:, h * part : (h + 1) * part].reshape(n_exp * part, -1)
        member_h = sum(
            (named[:, k : k + 1] == lane.astype(BF16)).astype(BF16) for k in range(named.shape[1])
        )
        hid, da, db, dx, coef = expert_pass(
            mids[h], d_hid_parts[h], member_h, router_w, pick, w_gate, w_up, experts
        )
        hid_parts.append(hid)
        da_parts.append(da)
        db_parts.append(db)
        coef_parts.append(coef)
        dxs.append(dx)
    d_mids = [scatter_sum(after(dx, mids[-1]), "exp") for dx in dxs]

    def back_to_rows(h, *earlier):
        d_residual, low, g_gain = residual_back(
            residual_parts[h], scale_parts[h], mlp_gain,
            grad_mine[h * part : (h + 1) * part], d_mids[h], earlier,
        )
        dl = gather_ctx(low, 0).reshape(half_seq, width)
        return d_residual, low, g_gain, dl

    g_router = sum(t_mm(c, m) for m, c in zip(mids, coef_parts))[:experts]

    g_down, *y_parts = down_sums(hid_parts, grad_parts, w_down)
    d_res0, low0, gain0, dl0 = back_to_rows(0, y_parts[0])
    d_res1, low1, gain1, dl1 = back_to_rows(1, y_parts[0])
    bits = list(range(n_ctx.bit_length() - 1))
    gives, first_gate, give_up = [], [], []
    for j in range(own):
        order = bits if j % 2 == 0 else bits[::-1]
        table = c_at ^ jnp.asarray(halving_masks(order)[n_ctx // 2 :], jnp.int32)
        give = given_grads(
            table, mids, [da_parts, db_parts], width // n_ctx, j, (low0, low1, *gives)
        )
        first_gate.append(swap(give[0], 1 << order[0]))
        give_up.append(give[1])
        gives.append(give[0])
    g_mid_gain = gain0 + gain1
    d_res_parts, dl_parts = [d_res0, d_res1], [dl0, dl1]
    d_att_parts = [mm_t(dl, out_w).astype(BF16) for dl in dl_parts]
    y_mine = [scatter_sum(y, "exp") for y in y_parts]
    mixed = jnp.concatenate(
        [(r + y.astype(F32)).astype(BF16) for r, y in zip(residual_parts, y_mine)], axis=0
    )

    dq_parts = []
    dk_n = jnp.zeros((seq, cols), F32)
    dv = jnp.zeros((seq, cols), F32)
    for h in range(halves):
        dq, dk_n, dv = attend_back(base, half_seq, h, d_att_parts[h], dk_n, dv, gives)
        dq_parts.append(dq)
    dq_n = jnp.concatenate(dq_parts, axis=0)
    inner = jnp.stack(
        [
            jnp.sum(dq_n * query_gain * qp, axis=-1),
            jnp.sum(dk_n * key_gain * kp, axis=-1),
        ],
        axis=0,
    )
    inner = ctx_sum(jnp.pad(inner, ((0, 6), (0, 0))), 1, first_gate)
    give_up = held(give_up, (inner,))
    first_up = [swap(g, 1 << (bits[0] if j % 2 == 0 else bits[-1])) for j, g in enumerate(give_up)]
    inner = inner[:2] / width
    dqp = q_scale * dq_n * query_gain - qp * (q_scale**3) * inner[0][:, None]
    dkp = k_scale * dk_n * key_gain - kp * (k_scale**3) * inner[1][:, None]
    g_query_gain = jnp.sum(dq_n * qp * q_scale, axis=0)
    g_key_gain = jnp.sum(dk_n * kp * k_scale, axis=0)
    d_qkv = jnp.concatenate([dqp.astype(BF16), dkp.astype(BF16), dv.astype(BF16)], axis=1)
    partial = input_partial(d_qkv, weights, part, ())
    g_mine = attention_grads(xn, d_qkv, attended_parts, dl_parts, cols, (partial, *first_up))
    g_gate, dxn, kept_up = gate_sums(mids, da_parts, db_parts, partial, first_gate, (g_mine,))
    dxn = jnp.concatenate([dxn[0], dxn[1]], axis=1)
    block_input = tokens[0].astype(F32)
    in_scale = rms_scale(block_input)
    d_in_norm, g_attn_gain = rms_backward(block_input, in_scale, attn_gain, dxn)
    d_tokens = (jnp.concatenate(d_res_parts, axis=0) + d_in_norm).astype(BF16)

    g_mine = scatter_sum(g_mine, "exp")
    g_out = lax.ppermute(g_mine[:, 3 * cols :], ("ctx", "exp"), [(b, a) for a, b in moves])
    g_mine = jnp.concatenate([g_mine[:, : 3 * cols], g_out], axis=1)
    gain_grads = [g_attn_gain[None], g_mid_gain]
    for piece in (g_query_gain, g_key_gain):
        gain_grads.append(
            lax.dynamic_update_slice_in_dim(jnp.zeros((1, width), F32), piece[None], c_at * cols, 1)
        )
    spare = -(experts + 4) % 8
    smalls = jnp.concatenate([g_router] + gain_grads + [jnp.zeros((spare, width), F32)], axis=0)
    smalls = smalls.reshape(-1, n_exp, shard).transpose(1, 0, 2)
    g_up, *g_full, smalls = up_sums(kept_up, first_up, g_mine, smalls)
    return (
        mixed[None], d_tokens[None],
        *[g.astype(F32) for g in g_full],
        smalls[:experts].T,
        smalls[experts], smalls[experts + 2], smalls[experts + 3], smalls[experts + 1],
        g_gate.astype(F32), g_up.astype(F32), g_down.astype(F32),
    )


def solution(mesh):
    tok = P("exp", "ctx", None)
    two, three, one = P("exp", None), P("exp", None, None), P("exp")
    return jax.shard_map(
        local,
        mesh=mesh,
        in_specs=(tok, tok, one, P(), tok) + (two,) * 5 + (one,) * 4 + (three,) * 3,
        out_specs=(tok, tok) + (two,) * 5 + (one,) * 4 + (tok,) * 3,
        check_vma=False,
    )
```

```python
import functools
import math

import jax
import jax.numpy as jnp
from jax import lax
from jax.experimental import pallas as pl
from jax.experimental.pallas import tpu as pltpu
from jax.sharding import PartitionSpec as P

HEADS = 16
HEAD_DIM = 128
LANES = 128
EPSILON = 1e-05
ROPE_BASE = 10000.0
MASKED_SCORE = -1e30
FACTOR = HEAD_DIM ** (-0.5)
F32 = jnp.float32
BF16 = jnp.bfloat16
MIB = 1 << 20


def mm(left, right):
    return jnp.dot(left, right, preferred_element_type=F32)


def mm_t(left, right):
    return lax.dot_general(left, right, (((1,), (1,)), ((), ())), preferred_element_type=F32)


def t_mm(left, right):
    return lax.dot_general(left, right, (((0,), (0,)), ((), ())), preferred_element_type=F32)


def rms_scale(rows):
    return lax.rsqrt(jnp.mean(rows * rows, axis=-1, keepdims=True) + EPSILON)


def rms_backward(rows, inv_scale, gain_vec, grad_in):
    weighted = grad_in * gain_vec
    inner_mean = jnp.mean(weighted * rows, axis=-1, keepdims=True)
    d_rows = inv_scale * weighted - rows * (inv_scale * inv_scale * inv_scale) * inner_mean
    return d_rows, jnp.sum(grad_in * rows * inv_scale, axis=0)


def rope_tables(positions):
    half_dim = HEAD_DIM // 2
    frequency = jnp.exp(
        jnp.arange(half_dim, dtype=F32) * (-2.0 * math.log(ROPE_BASE) / HEAD_DIM)
    )
    angle = positions.astype(F32)[:, None] * frequency[None, :]
    cosine, sine = jnp.cos(angle), jnp.sin(angle)
    return (
        jnp.concatenate([cosine, cosine], axis=1),
        jnp.concatenate([-sine, sine], axis=1),
    )


def positions_of(span_order, storage, span_length):
    return jnp.take(span_order, storage // span_length) * span_length + storage % span_length


def rotated(rows, scale, gain, cosine, sine):
    normed = rows * scale * gain
    return (normed * cosine + pltpu.roll(normed, HEAD_DIM // 2, 1) * sine).astype(BF16)


def unrotated(rows, cosine, sine):
    return rows * cosine - pltpu.roll(rows, HEAD_DIM // 2, 1) * sine


def head_probs(query, key, q_pos, k_pos):
    scores = jnp.where(k_pos <= q_pos, mm_t(query, key) * FACTOR, MASKED_SCORE)
    expo = jnp.exp(scores - jnp.max(scores, axis=1, keepdims=True))
    return expo / jnp.sum(expo, axis=1, keepdims=True)


def attend_kernel(
    q_ref, k_ref, v_ref, qs_ref, ks_ref, qg_ref, kg_ref, qc_ref, qn_ref, kc_ref, kn_ref,
    qp_ref, kp_ref, out_ref,
):
    query = rotated(q_ref[...], qs_ref[...], qg_ref[...], qc_ref[...], qn_ref[...])
    key = rotated(k_ref[...], ks_ref[...], kg_ref[...], kc_ref[...], kn_ref[...])
    probs = head_probs(query, key, qp_ref[...], kp_ref[...])
    out_ref[...] = mm(probs.astype(BF16), v_ref[...].astype(BF16)).astype(BF16)


def attend_back_kernel(
    q_ref, k_ref, v_ref, qs_ref, ks_ref, qg_ref, kg_ref, qc_ref, qn_ref, kc_ref, kn_ref,
    qp_ref, kp_ref, da_ref, dk_in, dv_in, *refs,
):
    dq_ref, dk_ref, dv_ref = refs[-3:]
    query = rotated(q_ref[...], qs_ref[...], qg_ref[...], qc_ref[...], qn_ref[...])
    key = rotated(k_ref[...], ks_ref[...], kg_ref[...], kc_ref[...], kn_ref[...])
    probs = head_probs(query, key, qp_ref[...], kp_ref[...])
    d_att = da_ref[...]
    d_probs = mm_t(d_att, v_ref[...].astype(BF16))
    inner = jnp.sum(probs * d_probs, axis=1, keepdims=True)
    d_scores = (probs * (d_probs - inner)).astype(BF16)
    dq_ref[...] = unrotated(mm(d_scores, key) * FACTOR, qc_ref[...], qn_ref[...])
    dk = unrotated(t_mm(d_scores, query) * FACTOR, kc_ref[...], kn_ref[...])
    dk_ref[...] = dk_in[...] + dk
    dv_ref[...] = dv_in[...] + t_mm(probs.astype(BF16), d_att)


def attention_specs(rows, seq, heads, h):
    def head_rows(n, at, row=0):
        return pl.BlockSpec((n, HEAD_DIM), lambda i: (row, at + i))

    def fixed(shape, row=0):
        return pl.BlockSpec(shape, lambda i: (row, 0))

    return [
        head_rows(rows, 0, h), head_rows(seq, heads), head_rows(seq, 2 * heads),
        fixed((rows, 1), h), fixed((seq, 1)), head_rows(1, 0), head_rows(1, 0),
        fixed((rows, HEAD_DIM), h), fixed((rows, HEAD_DIM), h),
        fixed((seq, HEAD_DIM)), fixed((seq, HEAD_DIM)),
        fixed((rows, 1), h), fixed((1, seq)),
    ]


def attend(base, rows, h):
    seq, cols = base[0].shape[0], base[0].shape[1] // 3
    heads = cols // HEAD_DIM
    return pl.pallas_call(
        attend_kernel,
        grid=(heads,),
        in_specs=attention_specs(rows, seq, heads, h),
        out_specs=pl.BlockSpec((rows, HEAD_DIM), lambda i: (0, i)),
        out_shape=jax.ShapeDtypeStruct((rows, cols), BF16),
        compiler_params=pltpu.CompilerParams(vmem_limit_bytes=48 * MIB),
        cost_estimate=pl.CostEstimate(
            flops=4 * rows * seq * cols, bytes_accessed=8 * MIB, transcendentals=rows * seq * heads
        ),
    )(*base)


def attend_back(base, rows, h, d_att, dk, dv, earlier):
    seq, cols = base[0].shape[0], base[0].shape[1] // 3
    heads = cols // HEAD_DIM
    q_out = pl.BlockSpec((rows, HEAD_DIM), lambda i: (0, i))
    k_out = pl.BlockSpec((seq, HEAD_DIM), lambda i: (0, i))
    return pl.pallas_call(
        attend_back_kernel,
        grid=(heads,),
        in_specs=attention_specs(rows, seq, heads, h)
        + [q_out, k_out, k_out]
        + [pl.BlockSpec(memory_space=pl.ANY)] * len(earlier),
        out_specs=[q_out, k_out, k_out],
        out_shape=[
            jax.ShapeDtypeStruct((rows, cols), F32),
            jax.ShapeDtypeStruct((seq, cols), F32),
            jax.ShapeDtypeStruct((seq, cols), F32),
        ],
        compiler_params=pltpu.CompilerParams(vmem_limit_bytes=48 * MIB),
        cost_estimate=pl.CostEstimate(
            flops=10 * rows * seq * cols, bytes_accessed=16 * MIB, transcendentals=rows * seq * heads
        ),
    )(*base, d_att, dk, dv, *earlier)


def expert_kernel(
    experts, own, step, x_ref, dh_ref, member_ref, router_ref, pick_ref, wg_hbm, wu_hbm,
    hid_ref, da_ref, db_ref, dx_ref, coef_ref, wg, wu, sems,
):
    i = pl.program_id(0)

    def loads(j):
        return (
            pltpu.make_async_copy(wg_hbm.at[j], wg.at[j], sems.at[0, j]),
            pltpu.make_async_copy(wu_hbm.at[j], wu.at[j], sems.at[1, j]),
        )

    @pl.when(i == 0)
    def _():
        for j in range(own):
            for copy in loads(j):
                copy.start()

    logits = mm(x_ref[...], router_ref[...])
    lane = lax.broadcasted_iota(jnp.int32, logits.shape, 1)
    logits = jnp.where(lane < experts, logits, MASKED_SCORE)
    expo = jnp.exp(logits - jnp.max(logits, axis=1, keepdims=True))
    router = expo / jnp.sum(expo, axis=1, keepdims=True)
    chosen = router * member_ref[...].astype(F32)
    coef = jnp.zeros_like(router)
    ff = wg.shape[2]
    for j in range(own):

        @pl.when(i == 0)
        def _():
            for copy in loads(j):
                copy.wait()

        pick = pick_ref[j : j + 1, :]
        gate = jnp.sum(chosen * pick, axis=1, keepdims=True)
        flow = jnp.zeros_like(gate)
        for f in range(0, ff, step):
            cut = slice(f, f + step)
            a = mm(x_ref[...], wg[j, :, cut])
            b = mm(x_ref[...], wu[j, :, cut])
            d_hid = dh_ref[j, :, cut].astype(F32)
            sig = jax.nn.sigmoid(a)
            silu = a * sig
            hid = silu * b
            flow = flow + jnp.sum(hid * d_hid, axis=1, keepdims=True)
            hid_ref[j, :, cut] = (gate * hid).astype(BF16)
            d_hid = d_hid * gate
            da_ref[j, :, cut] = (d_hid * b * (sig + silu * (1.0 - sig))).astype(BF16)
            db_ref[j, :, cut] = (d_hid * silu).astype(BF16)
        coef = coef + flow * gate * (pick - router)
    low = coef.astype(BF16)
    coef_ref[...] = low
    width = x_ref.shape[1]
    for n in range(0, width, step):
        cut = slice(n, n + step)
        part = mm_t(low, router_ref[cut, :])
        for j in range(own):
            part = part + mm_t(da_ref[j], wg[j, cut, :]) + mm_t(db_ref[j], wu[j, cut, :])
        dx_ref[:, cut] = part.astype(BF16)


def expert_pass(x, d_hid, member, router_w, pick, w_gate, w_up, experts):
    rows, width = x.shape
    own, _, ff = w_gate.shape
    tile = 256
    by_row = pl.BlockSpec((tile, width), lambda i: (i, 0))
    by_lane = pl.BlockSpec((tile, LANES), lambda i: (i, 0))
    by_expert = pl.BlockSpec((own, tile, ff), lambda i: (0, i, 0))
    return pl.pallas_call(
        functools.partial(expert_kernel, experts, own, 512),
        grid=(rows // tile,),
        in_specs=[
            by_row, by_expert, by_lane,
            pl.BlockSpec((width, LANES), lambda i: (0, 0)),
            pl.BlockSpec(pick.shape, lambda i: (0, 0)),
            pl.BlockSpec(memory_space=pl.ANY),
            pl.BlockSpec(memory_space=pl.ANY),
        ],
        out_specs=[by_expert] * 3 + [by_row, by_lane],
        out_shape=[jax.ShapeDtypeStruct((own, rows, ff), BF16)] * 3
        + [jax.ShapeDtypeStruct((rows, width), BF16), jax.ShapeDtypeStruct((rows, LANES), BF16)],
        scratch_shapes=[
            pltpu.VMEM((own, width, ff), BF16),
            pltpu.VMEM((own, width, ff), BF16),
            pltpu.SemaphoreType.DMA((2, own)),
        ],
        compiler_params=pltpu.CompilerParams(vmem_limit_bytes=56 * MIB),
        cost_estimate=pl.CostEstimate(
            flops=8 * rows * width * ff * own, bytes_accessed=40 * MIB, transcendentals=0
        ),
    )(x, d_hid, member, router_w, pick, w_gate, w_up)


def weight_kernel(n, *refs):
    total = t_mm(refs[0][...], refs[n][...])
    for h in range(1, n):
        total = total + t_mm(refs[h][...], refs[n + h][...])
    refs[-1][...] = total.astype(BF16)


def weight_grad(lefts, rights, block, tall, earlier):
    n = len(lefts)

    def by_column(a):
        return pl.BlockSpec((a.shape[0], block), lambda i: (0, i))

    def fixed(a):
        return pl.BlockSpec(a.shape, lambda i: (0, 0))

    columns = rights[0].shape[1] if tall else block
    rows = block if tall else lefts[0].shape[1]
    count = (lefts if tall else rights)[0].shape[1] // block
    return pl.pallas_call(
        functools.partial(weight_kernel, n),
        grid=(count,),
        in_specs=[(by_column if tall else fixed)(a) for a in lefts]
        + [(fixed if tall else by_column)(a) for a in rights]
        + [pl.BlockSpec(memory_space=pl.ANY)] * len(earlier),
        out_specs=pl.BlockSpec((rows, columns), lambda i: (i, 0)),
        out_shape=jax.ShapeDtypeStruct((count * rows, columns), BF16),
        compiler_params=pltpu.CompilerParams(vmem_limit_bytes=48 * MIB),
    )(*lefts, *rights, *earlier)


def partial_kernel(n, part, d_ref, w_ref, *refs):
    out_ref = refs[-1]
    rows, halves = n * part, d_ref.shape[0] // (n * part)
    for h in range(halves):
        total = mm_t(d_ref[h * rows : (h + 1) * rows, :], w_ref[...]).astype(BF16)
        for c in range(n):
            out_ref[0, c, h * part : (h + 1) * part, :] = total[c * part : (c + 1) * part, :]


def input_partial(d_qkv, weights, part, earlier):
    n = lax.axis_size("ctx")
    seq, depth = d_qkv.shape
    width = weights.shape[0]
    rows = seq // n
    return pl.pallas_call(
        functools.partial(partial_kernel, n, part),
        grid=(2,),
        in_specs=[
            pl.BlockSpec((seq, depth), lambda i: (0, 0)),
            pl.BlockSpec((width // 2, depth), lambda i: (i, 0)),
        ]
        + [pl.BlockSpec(memory_space=pl.ANY)] * len(earlier),
        out_specs=pl.BlockSpec((1, n, rows, width // 2), lambda i: (i, 0, 0, 0)),
        out_shape=jax.ShapeDtypeStruct((2, n, rows, width // 2), BF16),
        compiler_params=pltpu.CompilerParams(vmem_limit_bytes=48 * MIB),
    )(d_qkv, weights, *earlier)


def give_kernel(n, count, table, *refs):
    for k in range(count):
        total = t_mm(refs[0][...], refs[(k + 1) * n][0])
        for h in range(1, n):
            total = total + t_mm(refs[h][...], refs[(k + 1) * n + h][0])
        refs[len(refs) - count + k][0] = total.astype(BF16)


def given_grads(table, lefts, rights, block, j, earlier):
    n, blocks = len(lefts), table.shape[0]
    flat = [a for right in rights for a in right]
    columns = flat[0].shape[2]
    return pl.pallas_call(
        functools.partial(give_kernel, n, len(rights)),
        grid_spec=pltpu.PrefetchScalarGridSpec(
            num_scalar_prefetch=1,
            grid=(blocks,),
            in_specs=[pl.BlockSpec((a.shape[0], block), lambda i, t: (0, t[i])) for a in lefts]
            + [pl.BlockSpec((1,) + a.shape[1:], lambda i, t: (j, 0, 0)) for a in flat]
            + [pl.BlockSpec(memory_space=pl.ANY)] * len(earlier),
            out_specs=[pl.BlockSpec((1, block, columns), lambda i, t: (i, 0, 0))] * len(rights),
        ),
        out_shape=[jax.ShapeDtypeStruct((blocks, block, columns), BF16)] * len(rights),
        compiler_params=pltpu.CompilerParams(vmem_limit_bytes=48 * MIB),
    )(table, *lefts, *flat, *earlier)


def mid_kernel(n, x_ref, own_ref, gain_ref, *refs):
    total = x_ref[...].astype(F32) + own_ref[...]
    for got in refs[: n - 1]:
        total = total + got[...].astype(F32)
    res_ref, scale_ref, low_ref = refs[-3:]
    scale = lax.rsqrt(jnp.mean(total * total, axis=1, keepdims=True) + EPSILON)
    res_ref[...] = total
    scale_ref[...] = scale
    low_ref[...] = (total * scale * gain_ref[...]).astype(BF16)


def middle(x, own_block, got, gain, earlier):
    rows, width = x.shape
    whole = pl.BlockSpec(memory_space=pltpu.VMEM)
    return pl.pallas_call(
        functools.partial(mid_kernel, len(got) + 1),
        in_specs=[whole] * (3 + len(got)) + [pl.BlockSpec(memory_space=pl.ANY)] * len(earlier),
        out_specs=[whole] * 3,
        out_shape=[
            jax.ShapeDtypeStruct((rows, width), F32),
            jax.ShapeDtypeStruct((rows, 1), F32),
            jax.ShapeDtypeStruct((rows, width), BF16),
        ],
        compiler_params=pltpu.CompilerParams(vmem_limit_bytes=60 * MIB),
    )(x, own_block, gain[None], *got, *earlier)


def res_kernel(res_ref, scale_ref, gain_ref, grad_ref, mid_ref, *refs):
    out_ref, low_ref, gain_out = refs[-3:]
    rows, scale = res_ref[...], scale_ref[...]
    grad_in = mid_ref[...].astype(F32)
    weighted = grad_in * gain_ref[...]
    inner = jnp.mean(weighted * rows, axis=1, keepdims=True)
    total = grad_ref[...] + scale * weighted - rows * (scale * scale * scale) * inner
    out_ref[...] = total
    low_ref[...] = total.astype(BF16)
    gain_out[...] = jnp.sum(grad_in * rows * scale, axis=0, keepdims=True)


def residual_back(residual, scale, gain, grad, d_mid, earlier):
    rows, width = residual.shape
    whole = pl.BlockSpec(memory_space=pltpu.VMEM)
    return pl.pallas_call(
        res_kernel,
        in_specs=[whole] * 5 + [pl.BlockSpec(memory_space=pl.ANY)] * len(earlier),
        out_specs=[whole] * 3,
        out_shape=[
            jax.ShapeDtypeStruct((rows, width), F32),
            jax.ShapeDtypeStruct((rows, width), BF16),
            jax.ShapeDtypeStruct((1, width), F32),
        ],
        compiler_params=pltpu.CompilerParams(vmem_limit_bytes=60 * MIB),
    )(residual, scale, gain[None], grad, d_mid, *earlier)


def meet(peers):
    barrier = pltpu.get_barrier_semaphore()
    for peer in peers:
        pl.semaphore_signal(barrier, inc=1, device_id=peer, device_id_type=pl.DeviceIdType.MESH)
    pl.semaphore_wait(barrier, len(peers))


def ctx_sum_kernel(n, x_ref, *refs):
    out_ref, slots, send, recv = refs[-4:]
    me = lax.axis_index("ctx")
    peers = [{"ctx": lax.rem(me + d, n)} for d in range(1, n)]
    meet(peers)
    slots[me] = x_ref[...]
    copies = [
        pltpu.make_async_remote_copy(
            src_ref=x_ref, dst_ref=slots.at[me], send_sem=send.at[d], recv_sem=recv.at[d],
            device_id=peer, device_id_type=pl.DeviceIdType.MESH,
        )
        for d, peer in enumerate(peers)
    ]
    for copy in copies:
        copy.start()
    for copy in copies:
        copy.wait()
    total = slots[0]
    for k in range(1, n):
        total = total + slots[k]
    out_ref[...] = total


def ctx_sum(x, number, earlier=()):
    n = lax.axis_size("ctx")
    whole = pl.BlockSpec(memory_space=pltpu.VMEM)
    return pl.pallas_call(
        functools.partial(ctx_sum_kernel, n),
        in_specs=[whole] + [pl.BlockSpec(memory_space=pl.ANY)] * len(earlier),
        out_specs=whole,
        out_shape=jax.ShapeDtypeStruct(x.shape, F32),
        scratch_shapes=[
            pltpu.VMEM((n,) + x.shape, F32),
            pltpu.SemaphoreType.DMA((n - 1,)),
            pltpu.SemaphoreType.DMA((n - 1,)),
        ],
        compiler_params=pltpu.CompilerParams(collective_id=number, has_side_effects=True),
    )(x, *earlier)


class SmallSum:
    def __init__(self, n_ctx, n_exp, x, first, second, sems):
        self.x, self.first, self.second, self.sems = x, first, second, sems
        self.c_at, self.e_at = lax.axis_index("ctx"), lax.axis_index("exp")
        self.across = [{"exp": lax.rem(self.e_at + d, n_exp)} for d in range(1, n_exp)]
        self.along = [{"ctx": lax.rem(self.c_at + d, n_ctx)} for d in range(1, n_ctx)]

    def copy(self, src, dst, step, d, peer):
        return pltpu.make_async_remote_copy(
            src_ref=src, dst_ref=dst, send_sem=self.sems.at[2 * step, d],
            recv_sem=self.sems.at[2 * step + 1, d], device_id=peer,
            device_id_type=pl.DeviceIdType.MESH,
        )

    def over_exp(self):
        return [
            self.copy(self.x.at[peer["exp"]], self.first.at[self.e_at], 0, d, peer)
            for d, peer in enumerate(self.across)
        ]

    def over_ctx(self):
        mine = self.second.at[self.c_at]
        return [self.copy(mine, mine, 1, d, peer) for d, peer in enumerate(self.along)]

    def begin(self):
        for copy in self.over_exp():
            copy.start()
        self.first[self.e_at] = self.x[self.e_at]

    def pass_on(self):
        for copy in self.over_exp():
            copy.wait()
        total = self.first[0]
        for k in range(1, self.first.shape[0]):
            total = total + self.first[k]
        self.second[self.c_at] = total
        for copy in self.over_ctx():
            copy.start()

    def finish(self, out):
        for copy in self.over_ctx():
            copy.wait()
        total = self.second[0]
        for k in range(1, self.second.shape[0]):
            total = total + self.second[k]
        out[...] = total

    @staticmethod
    def scratch(n_ctx, shape):
        return [
            pltpu.VMEM(shape, F32),
            pltpu.VMEM((n_ctx,) + shape[1:], F32),
            pltpu.SemaphoreType.DMA((4, max(n_ctx, shape[0]) - 1)),
        ]


def halving_masks(order):
    masks = [0]
    for bit in order[::-1]:
        masks = masks + [m | (1 << bit) for m in masks]
    return masks


def flip(value, mask):
    bit = 0
    while mask >> bit:
        if (mask >> bit) & 1:
            value = value + (1 << bit) * (1 - 2 * lax.rem(lax.div(value, 1 << bit), 2))
        bit += 1
    return value


class Halving:
    def __init__(
        self, n, me, source, blocks, got, send, recv, out, first=None, acc=None, kept=None
    ):
        self.n, self.me, self.source, self.blocks, self.got = n, me, source, blocks, got
        self.send, self.recv, self.out = send, recv, out
        self.first, self.acc, self.kept = first, out if acc is None else acc, kept
        bits = list(range(n.bit_length() - 1))
        self.own = out.shape[0]
        self.orders = [bits if j % 2 == 0 else bits[::-1] for j in range(self.own)]
        self.masks = [halving_masks(order) for order in self.orders]
        self.steps = len(bits)

    def target(self, j, k):
        return flip(self.me, self.masks[j][k])

    def slot(self, s, k):
        made = 0 if self.first is None else self.n >> 1
        return self.n - (self.n >> s) + k - (self.n >> (s + 1)) - made

    def copy(self, j, s, k):
        given = self.source is not None and s == 0
        at = self.slot(s, k)
        return pltpu.make_async_remote_copy(
            src_ref=self.source.at[j, self.target(j, k)] if given else self.blocks.at[j, k - 1],
            dst_ref=self.got.at[j, at],
            send_sem=self.send.at[j, at],
            recv_sem=self.recv.at[j, at],
            device_id={"ctx": flip(self.me, 1 << self.orders[j][s])},
            device_id_type=pl.DeviceIdType.MESH,
        )

    def going(self, s):
        return [
            (j, k)
            for k in range((self.n >> s) - 1, (self.n >> (s + 1)) - 1, -1)
            for j in range(self.own)
        ]

    def begin(self, value=None):
        for j, k in self.going(0) if self.first is None else []:
            if value is not None:
                self.blocks[j, k - 1] = value(j, self.target(j, k)).astype(BF16)
            self.copy(j, 0, k).start()
        for k in range(self.n // 2 - 1, 0, -1):
            for j in range(self.own):
                at = self.target(j, k)
                mine = self.source[j, at] if value is None else value(j, at)
                self.blocks[j, k - 1] = mine.astype(BF16)

    def rest(self, value=None):
        for j in range(self.own):
            self.acc[j] = self.source[j, self.me].astype(F32) if value is None else value(j, self.me)

    def arrived(self, j, k, steps):
        total = None
        for s in range(steps):
            sent = k + (self.n >> (s + 1))
            if s == 0 and self.first is not None:
                part = self.first[j][k].astype(F32)
            else:
                self.copy(j, s, sent).wait_recv()
                part = self.got[j, self.slot(s, sent)].astype(F32)
            total = part if total is None else total + part
        return total

    def pass_on(self):
        for s in range(1, self.steps):
            for j, k in self.going(s):
                mine = self.blocks[j, k - 1] if self.kept is None else self.kept[j, k]
                total = mine.astype(F32) + self.arrived(j, k, s)
                self.blocks[j, k - 1] = total.astype(BF16)
                self.copy(j, s, k).start()

    def finish(self):
        for j in range(self.own):
            mine = self.acc[j] if self.kept is None else self.kept[j, 0].astype(F32)
            self.out[j] = (mine + self.arrived(j, 0, self.steps)).astype(self.out.dtype)
        for s in range(0 if self.first is None else 1, self.steps):
            for j, k in self.going(s):
                self.copy(j, s, k).wait_send()

    @staticmethod
    def scratch(own, n, rows, columns):
        return [
            pltpu.VMEM((own, n - 1, rows, columns), BF16),
            pltpu.VMEM((own, n - 1, rows, columns), BF16),
            pltpu.SemaphoreType.DMA((own, n - 1)),
            pltpu.SemaphoreType.DMA((own, n - 1)),
        ]


def ctx_peers(n, me):
    return [{"ctx": lax.rem(me + d, n)} for d in range(1, n)]


def entry(ref, j):
    return ref.at[j] if len(ref.shape) == 3 else ref


def product(lefts, rights, block):
    def value(j, at):
        total = None
        for left, right in zip(lefts, rights):
            columns = pl.ds(pl.multiple_of(at * block, LANES), block)
            part = t_mm(entry(left, j)[:, columns], entry(right, j)[...])
            total = part if total is None else total + part
        return total

    return value


def down_kernel(n, halves, *refs):
    hid, grad, w_down = refs[:halves], refs[halves : 2 * halves], refs[2 * halves]
    refs = refs[2 * halves + 1 :]
    out, ys, scratch = refs[0], refs[1 : 1 + halves], refs[1 + halves :]
    me = lax.axis_index("ctx")
    meet(ctx_peers(n, me))
    sums = Halving(n, me, None, *scratch[:4], out, acc=scratch[4])
    value = product(hid, grad, hid[0].shape[2] // n)
    sums.begin(value)
    sums.rest(value)
    width = w_down.shape[2]
    for h in range(halves):
        for start in range(0, width, 512):
            cut = slice(start, start + 512)
            total = mm(hid[h][0], w_down[0, :, cut])
            for j in range(1, w_down.shape[0]):
                total = total + mm(hid[h][j], w_down[j, :, cut])
            ys[h][:, cut] = total.astype(BF16)
    sums.pass_on()
    sums.finish()


def gate_kernel(n, halves, *refs):
    mids, gate_pres, up_pres = [refs[k * halves : (k + 1) * halves] for k in range(3)]
    own = gate_pres[0].shape[0]
    partial, first = refs[3 * halves], refs[3 * halves + 1 : 3 * halves + 1 + own]
    out, dxn, kept = refs[-12:-9]
    me = lax.axis_index("ctx")
    meet(ctx_peers(n, me))
    rows = Halving(n, me, partial, *refs[-9:-5], dxn)
    rows.begin()
    block = mids[0].shape[1] // n
    sums = Halving(n, me, None, *refs[-5:-1], out, first, refs[-1])
    value = product(mids, gate_pres, block)
    sums.begin(value)
    sums.pass_on()
    rows.pass_on()
    sums.rest(value)
    rows.rest()
    value = product(mids, up_pres, block)
    for k in range(n // 2):
        for j in range(own):
            kept[j, k] = value(j, sums.target(j, k)).astype(BF16)
    rows.finish()
    sums.finish()


def up_kernel(n, *refs):
    piece, x, kept = refs[:3]
    out, *whole = refs[-16:-11]
    small_out, slots, send, recv = refs[-11:-7]
    me = lax.axis_index("ctx")
    smalls = SmallSum(n, x.shape[0], x, *refs[-7:-4])
    meet(smalls.across + smalls.along)
    smalls.begin()
    bits = list(range(n.bit_length() - 1))
    half = piece.shape[0] // 2

    def doubling(i, s):
        order = bits if i == 0 else bits[::-1]
        lines = pl.ds(i * half, half)
        copies = []
        for m in halving_masks(order[:s]):
            at = flip(me, m)
            sem = i, (1 << s) - 1 + len(copies)
            copies.append(
                pltpu.make_async_remote_copy(
                    src_ref=slots.at[at, lines] if m else piece.at[lines],
                    dst_ref=slots.at[at, lines],
                    send_sem=send.at[sem],
                    recv_sem=recv.at[sem],
                    device_id={"ctx": flip(me, 1 << order[s])},
                    device_id_type=pl.DeviceIdType.MESH,
                )
            )
        return copies

    first = refs[3 : 3 + kept.shape[0]]
    sums = Halving(n, me, None, *refs[-4:], out, first, kept=kept)
    for i in range(2):
        for copy in doubling(i, 0):
            copy.start()
    sums.pass_on()
    smalls.pass_on()
    slots[me] = piece[...]
    for s in range(1, len(bits)):
        for i in range(2):
            for copy in doubling(i, s - 1):
                copy.wait_recv()
            for copy in doubling(i, s):
                copy.start()
    smalls.finish(small_out)
    sums.finish()
    for i in range(2):
        for copy in doubling(i, len(bits) - 1):
            copy.wait_recv()
        for s in range(len(bits)):
            for copy in doubling(i, s):
                copy.wait_send()
    cols = piece.shape[1] // len(whole)
    for c in range(n):
        for k, ref in enumerate(whole):
            ref[:, c * cols : (c + 1) * cols] = slots[c, :, k * cols : (k + 1) * cols]


class Doubling:
    def __init__(self, axis, order, last, block, slot, sems, base):
        self.me, self.axis, self.order, self.last = lax.axis_index(axis), axis, order, last
        self.block, self.slot, self.sems, self.base = block, slot, sems, base
        self.steps = [halving_masks(order[:s]) for s in range(len(order) + 1)]
        self.keys = [(bit, m) for bit, ms in zip(order, self.steps) for m in ms]
        if last is not None:
            self.keys += [(last, m) for m in self.steps[-1]]

    def copy(self, bit, m):
        at = self.base + self.keys.index((bit, m))
        place = self.slot(flip(self.me, m))
        return pltpu.make_async_remote_copy(
            src_ref=place if m else self.block,
            dst_ref=place,
            send_sem=self.sems.at[0, at],
            recv_sem=self.sems.at[1, at],
            device_id={self.axis: flip(self.me, 1 << bit)},
            device_id_type=pl.DeviceIdType.MESH,
        )

    def step(self, s):
        fresh = [0]
        if s:
            fresh = [m | (1 << self.order[s - 1]) for m in self.steps[s - 1]]
            for m in self.steps[s - 1]:
                self.copy(self.order[s - 1], m).wait_recv()
        if s < len(self.order):
            for m in self.steps[s]:
                self.copy(self.order[s], m).start()
        if self.last is not None:
            for m in fresh:
                self.copy(self.last, m).start()

    def finish(self):
        if self.last is not None:
            for m in self.steps[-1]:
                self.copy(self.last, m).wait_recv()
        for key in self.keys:
            self.copy(*key).wait_send()


def start_kernel(n_ctx, n_exp, w_ref, x_ref, small_ref, w_out, x_out, small_out, sems, local_sems):
    c_at, e_at = lax.axis_index("ctx"), lax.axis_index("exp")
    c_bits, e_bits = n_ctx.bit_length() - 1, n_exp.bit_length() - 1
    meet(
        [{"ctx": flip(c_at, 1 << b)} for b in range(c_bits)]
        + [{"exp": flip(e_at, 1 << b)} for b in range(e_bits)]
    )
    far = list(range(1, e_bits))
    near = list(range(c_bits))
    half = w_ref.shape[0] // 2
    moves, base = [], 0

    def add(axis, order, last, block, slot):
        moves.append(Doubling(axis, order, last, block, slot, sems, base))
        return base + len(moves[-1].keys)

    base = add("exp", far, 0, small_ref, lambda at: small_out.at[at])
    for i, order in enumerate((far[::-1], far)):
        lines = pl.ds(i * half, half)
        base = add(
            "exp", order, 0, w_ref.at[lines], lambda at, lines=lines: w_out.at[at, lines]
        )
    for i, order in enumerate((near[::-1], near)):
        base = add("ctx", order, None, x_ref.at[i], lambda at, i=i: x_out.at[i, at])
    own = [
        pltpu.make_async_copy(w_ref, w_out.at[e_at], local_sems.at[0]),
        pltpu.make_async_copy(small_ref, small_out.at[e_at], local_sems.at[1]),
        pltpu.make_async_copy(x_ref.at[0], x_out.at[0, c_at], local_sems.at[2]),
        pltpu.make_async_copy(x_ref.at[1], x_out.at[1, c_at], local_sems.at[3]),
    ]
    for s in range(max(len(far), len(near)) + 1):
        for move in moves:
            if s <= len(move.order):
                move.step(s)
        if s == 0:
            for copy in own:
                copy.start()
    for move in moves:
        move.finish()
    for copy in own:
        copy.wait()


def gather_start(w, x, small):
    n_ctx, n_exp = lax.axis_size("ctx"), lax.axis_size("exp")
    count = 3 * (n_exp - 1) + 2 * (n_ctx - 1)
    return pl.pallas_call(
        functools.partial(start_kernel, n_ctx, n_exp),
        in_specs=[ANY] * 3,
        out_specs=[ANY] * 3,
        out_shape=[
            jax.ShapeDtypeStruct((n_exp,) + w.shape, BF16),
            jax.ShapeDtypeStruct((x.shape[0], n_ctx) + x.shape[1:], BF16),
            jax.ShapeDtypeStruct((n_exp,) + small.shape, BF16),
        ],
        scratch_shapes=[pltpu.SemaphoreType.DMA((2, count)), pltpu.SemaphoreType.DMA((4,))],
        compiler_params=pltpu.CompilerParams(collective_id=6, has_side_effects=True),
    )(w, x, small)


def hold_kernel(*refs):
    pass


def held(arrays, earlier):
    n = len(arrays)
    return pl.pallas_call(
        hold_kernel,
        in_specs=[ANY] * (n + len(earlier)),
        out_specs=[ANY] * n,
        out_shape=[jax.ShapeDtypeStruct(a.shape, a.dtype) for a in arrays],
        input_output_aliases={i: i for i in range(n)},
        compiler_params=pltpu.CompilerParams(vmem_limit_bytes=60 * MIB),
    )(*arrays, *earlier)


def mask_kernel(x_ref, valid_ref, *refs):
    refs[-1][...] = (x_ref[...].astype(F32) * valid_ref[...]).astype(BF16)


def masked(x, valid, earlier):
    blocks = [pl.BlockSpec(a.shape, lambda i: (0, 0)) for a in (x, valid)]
    return pl.pallas_call(
        mask_kernel,
        grid=(1,),
        in_specs=blocks + [ANY] * len(earlier),
        out_specs=blocks[0],
        out_shape=jax.ShapeDtypeStruct(x.shape, BF16),
    )(x, valid, *earlier)


VMEM = pl.BlockSpec(memory_space=pltpu.VMEM)
ANY = pl.BlockSpec(memory_space=pl.ANY)


def exchange(kernel, number, operands, earlier, outs, scratch):
    n = lax.axis_size("ctx")
    return pl.pallas_call(
        kernel,
        in_specs=[VMEM] * len(operands) + [ANY] * len(earlier),
        out_specs=[VMEM] * len(outs),
        out_shape=outs,
        scratch_shapes=scratch,
        compiler_params=pltpu.CompilerParams(
            collective_id=number, has_side_effects=True, vmem_limit_bytes=60 * MIB
        ),
    )(*operands, *earlier)


def down_sums(hid, grad, w_down):
    n, halves = lax.axis_size("ctx"), len(hid)
    own, ff, width = w_down.shape
    outs = [jax.ShapeDtypeStruct((own, ff // n, width), BF16)]
    outs += [jax.ShapeDtypeStruct((h.shape[1], width), BF16) for h in hid]
    return exchange(
        functools.partial(down_kernel, n, halves), 3, [*hid, *grad, w_down], (), outs,
        Halving.scratch(own, n, ff // n, width) + [pltpu.VMEM((own, ff // n, width), F32)],
    )


def gate_sums(mids, gate_pres, up_pres, partial, first, earlier):
    n, halves = lax.axis_size("ctx"), len(mids)
    own, _, ff = gate_pres[0].shape
    rows = mids[0].shape[1] // n
    shape = partial.shape
    outs = [
        jax.ShapeDtypeStruct((own, rows, ff), BF16),
        jax.ShapeDtypeStruct((shape[0],) + shape[2:], F32),
        jax.ShapeDtypeStruct((own, n // 2, rows, ff), BF16),
    ]
    return exchange(
        functools.partial(gate_kernel, n, halves), 4,
        [*mids, *gate_pres, *up_pres, partial, *first], earlier, outs,
        Halving.scratch(shape[0], n, *shape[2:])
        + Halving.scratch(own, n // 2, rows, ff)
        + [pltpu.VMEM((own, rows, ff), F32)],
    )


def up_sums(kept, first, piece, smalls):
    n = lax.axis_size("ctx")
    own, _, rows, ff = kept.shape
    shard, width = piece.shape
    outs = [jax.ShapeDtypeStruct((own, rows, ff), BF16)]
    outs += [jax.ShapeDtypeStruct((shard, n * width // 4), BF16) for _ in range(4)]
    outs += [jax.ShapeDtypeStruct(smalls.shape[1:], F32)]
    return exchange(
        functools.partial(up_kernel, n), 5, [piece, smalls, kept, *first], (), outs,
        [
            pltpu.VMEM((n,) + piece.shape, BF16),
            pltpu.SemaphoreType.DMA((2, n - 1)),
            pltpu.SemaphoreType.DMA((2, n - 1)),
        ]
        + SmallSum.scratch(n, smalls.shape)
        + Halving.scratch(own, n // 2, rows, ff),
    )


def gather(block, axis):
    return lax.all_gather(block, axis, axis=0, tiled=True)


def scatter_sum(block, axis, dimension=0):
    return lax.psum_scatter(block, axis, scatter_dimension=dimension, tiled=True)


def after(value, *earlier):
    return lax.optimization_barrier((value,) + earlier)[0]


def swap(block, bits):
    n = lax.axis_size("ctx")
    return lax.ppermute(block, "ctx", [(i, i ^ bits) for i in range(n)])


def take(block, at, size=1, axis=0):
    return lax.dynamic_slice_in_dim(block, at, size, axis)


def gather_ctx(block, axis):
    n, me = lax.axis_size("ctx"), lax.axis_index("ctx")
    parts = [block] + [swap(block, d) for d in range(1, n)]
    shape = block.shape[:axis] + (n,) + block.shape[axis:]
    out = jnp.zeros(shape, block.dtype)
    for d, piece in enumerate(parts):
        out = lax.dynamic_update_slice_in_dim(out, jnp.expand_dims(piece, axis), me ^ d, axis)
    return out


def local(
    tokens, cotangent, lengths, span_order, routes,
    w_query, w_key, w_value, w_output, w_router,
    gain_attn, gain_query, gain_key, gain_mlp,
    w_gate, w_up, w_down,
):
    n_ctx, n_exp = lax.axis_size("ctx"), lax.axis_size("exp")
    c_at, e_at = lax.axis_index("ctx"), lax.axis_index("exp")
    rows = tokens.shape[1]
    width = tokens.shape[2]
    seq = rows * n_ctx
    cols = width // n_ctx
    shard = width // n_exp
    own = w_gate.shape[0]
    ff = w_gate.shape[2]
    experts = w_router.shape[1]
    seq_length = lengths[0]
    halves = 2
    part = rows // halves
    half_seq = part * n_ctx

    ratio = n_exp // n_ctx
    moves = []
    for c in range(n_ctx):
        for e in range(n_exp):
            moves.append(((e // ratio) * n_exp + c * ratio + e % ratio, c * n_exp + e))
    out_piece = lax.ppermute(take(w_output, c_at * cols, cols, 1), ("ctx", "exp"), moves)

    storage = jnp.arange(seq, dtype=jnp.int32)
    storage = (storage % half_seq // part) * rows + storage // half_seq * part + storage % part
    positions = positions_of(span_order, storage, rows // 2)
    my_positions = positions_of(
        span_order, c_at * rows + jnp.arange(rows, dtype=jnp.int32), rows // 2
    )
    valid = (my_positions < seq_length).astype(F32)[:, None]
    small = jnp.concatenate(
        [
            w_router.reshape(-1), gain_attn, gain_query, gain_key, gain_mlp,
            routes[0].astype(BF16).reshape(-1),
        ]
    )
    used = small.shape[0]
    lines = -(-used // (16 * LANES)) * 16
    small = jnp.pad(small, (0, lines * LANES - used)).reshape(lines, LANES)
    pieces = [take(w, c_at * cols, cols, 1) for w in (w_query, w_key, w_value)]
    weights, x_low, small_all = gather_start(
        jnp.concatenate(pieces + [out_piece], axis=1), tokens[0].reshape(halves, part, width), small
    )
    weights = weights.reshape(width, 4 * cols)
    x_low = x_low.reshape(seq, width)
    small_all = small_all.reshape(n_exp, lines * LANES)[:, :used]
    at = shard * experts
    router_w = small_all[:, :at].reshape(width, experts)
    router_w = jnp.pad(router_w, ((0, 0), (0, LANES - experts)))
    gains = []
    for _ in range(4):
        gains.append(small_all[:, at : at + shard].reshape(width).astype(F32))
        at += shard
    attn_gain, query_gain_all, key_gain_all, mlp_gain = gains
    routes_all = small_all[:, at:].reshape(n_exp, rows, routes.shape[2])
    lane = jnp.arange(LANES, dtype=jnp.int32)[None, :]
    query_gain = take(query_gain_all, c_at * cols, cols)
    key_gain = take(key_gain_all, c_at * cols, cols)

    qkv_w = weights[:, : 3 * cols]
    out_w = weights[:, 3 * cols :].reshape(n_ctx, cols, cols).transpose(1, 0, 2).reshape(cols, width)
    x_all = x_low.astype(F32)

    grad_low = masked(cotangent[0], valid, (weights,))
    grad_mine = grad_low.astype(F32)
    grad_parts = [gather(grad_low[h * part : (h + 1) * part], "exp") for h in range(halves)]
    d_hid_parts = [
        jnp.stack([mm_t(g, w_down[j]).astype(BF16) for j in range(own)]) for g in grad_parts
    ]

    cosine, sine = rope_tables(positions)
    xn = (x_all * rms_scale(x_all) * attn_gain).astype(BF16)
    qkv = mm(xn, qkv_w)
    qp, kp = qkv[:, :cols], qkv[:, cols : 2 * cols]
    squares = jnp.stack([jnp.sum(qp * qp, axis=-1), jnp.sum(kp * kp, axis=-1)], axis=0)
    squares = ctx_sum(jnp.pad(squares, ((0, 6), (0, 0))), 0)[:2] / width
    q_scale = lax.rsqrt(squares[0] + EPSILON)[:, None]
    k_scale = lax.rsqrt(squares[1] + EPSILON)[:, None]
    key_positions = jnp.where(positions < seq_length, positions, jnp.int32(1 << 30))
    base = (
        qkv, qkv, qkv, q_scale, k_scale, query_gain[None], key_gain[None],
        cosine, sine, cosine, sine, positions[:, None], key_positions[None],
    )

    attended_parts, mids, residual_parts, scale_parts = [], [], [], []
    for h in range(halves):
        attended = attend(base, half_seq, h)
        attended_parts.append(attended)
        got = []
        for d in range(n_ctx - 1, -1, -1):
            block = mm(take(attended, (c_at ^ d) * part, part), out_w)
            if d:
                got.append(swap(block.astype(BF16), d))
        residual, scale, mid = middle(
            tokens[0, h * part : (h + 1) * part], block, got, mlp_gain,
            (d_hid_parts[h],),
        )
        residual_parts.append(residual)
        scale_parts.append(scale)
        mids.append(gather(mid, "exp"))

    pick = (lane == e_at * own + jnp.arange(max(own, 8), dtype=jnp.int32)[:, None]).astype(F32)
    hid_parts, da_parts, db_parts, coef_parts = [], [], [], []
    dxs = []
    for h in range(halves):
        named = routes_all[:, h * part : (h + 1) * part].reshape(n_exp * part, -1)
        member_h = sum(
            (named[:, k : k + 1] == lane.astype(BF16)).astype(BF16) for k in range(named.shape[1])
        )
        hid, da, db, dx, coef = expert_pass(
            mids[h], d_hid_parts[h], member_h, router_w, pick, w_gate, w_up, experts
        )
        hid_parts.append(hid)
        da_parts.append(da)
        db_parts.append(db)
        coef_parts.append(coef)
        dxs.append(dx)
    d_mids = [scatter_sum(after(dx, mids[-1]), "exp") for dx in dxs]

    def back_to_rows(h, *earlier):
        d_residual, low, g_gain = residual_back(
            residual_parts[h], scale_parts[h], mlp_gain,
            grad_mine[h * part : (h + 1) * part], d_mids[h], earlier,
        )
        dl = gather_ctx(low, 0).reshape(half_seq, width)
        return d_residual, low, g_gain, dl

    g_router = sum(t_mm(c, m) for m, c in zip(mids, coef_parts))[:experts]

    g_down, *y_parts = down_sums(hid_parts, grad_parts, w_down)
    d_res0, low0, gain0, dl0 = back_to_rows(0, y_parts[0])
    d_res1, low1, gain1, dl1 = back_to_rows(1, y_parts[0])
    bits = list(range(n_ctx.bit_length() - 1))
    gives, first_gate, give_up = [], [], []
    for j in range(own):
        order = bits if j % 2 == 0 else bits[::-1]
        table = c_at ^ jnp.asarray(halving_masks(order)[n_ctx // 2 :], jnp.int32)
        give = given_grads(
            table, mids, [da_parts, db_parts], width // n_ctx, j, (low0, low1, *gives)
        )
        first_gate.append(swap(give[0], 1 << order[0]))
        give_up.append(give[1])
        gives.append(give[0])
    g_mid_gain = gain0 + gain1
    d_res_parts, dl_parts = [d_res0, d_res1], [dl0, dl1]
    d_att_parts = [mm_t(dl, out_w).astype(BF16) for dl in dl_parts]
    y_mine = [scatter_sum(y, "exp") for y in y_parts]
    mixed = jnp.concatenate(
        [(r + y.astype(F32)).astype(BF16) for r, y in zip(residual_parts, y_mine)], axis=0
    )

    dq_parts = []
    dk_n = jnp.zeros((seq, cols), F32)
    dv = jnp.zeros((seq, cols), F32)
    g_out = weight_grad(attended_parts, dl_parts, cols, False, (*gives, y_mine[0]))
    for h in range(halves):
        dq, dk_n, dv = attend_back(base, half_seq, h, d_att_parts[h], dk_n, dv, (g_out,))
        dq_parts.append(dq)
    g_out = lax.ppermute(scatter_sum(g_out, "exp"), ("ctx", "exp"), [(b, a) for a, b in moves])
    dq_n = jnp.concatenate(dq_parts, axis=0)
    inner = jnp.stack(
        [
            jnp.sum(dq_n * query_gain * qp, axis=-1),
            jnp.sum(dk_n * key_gain * kp, axis=-1),
        ],
        axis=0,
    )
    inner = ctx_sum(jnp.pad(inner, ((0, 6), (0, 0))), 1, first_gate)
    give_up = held(give_up, (inner,))
    first_up = [swap(g, 1 << (bits[0] if j % 2 == 0 else bits[-1])) for j, g in enumerate(give_up)]
    inner = inner[:2] / width
    dqp = q_scale * dq_n * query_gain - qp * (q_scale**3) * inner[0][:, None]
    dkp = k_scale * dk_n * key_gain - kp * (k_scale**3) * inner[1][:, None]
    g_query_gain = jnp.sum(dq_n * qp * q_scale, axis=0)
    g_key_gain = jnp.sum(dk_n * kp * k_scale, axis=0)
    d_qkv = jnp.concatenate([dqp.astype(BF16), dkp.astype(BF16), dv.astype(BF16)], axis=1)
    partial = input_partial(d_qkv, weights, part, ())
    g_mine = weight_grad([xn], [d_qkv], cols, True, (partial, g_out, y_mine[1], *first_up))
    g_gate, dxn, kept_up = gate_sums(mids, da_parts, db_parts, partial, first_gate, (g_mine,))
    dxn = jnp.concatenate([dxn[0], dxn[1]], axis=1)
    block_input = tokens[0].astype(F32)
    in_scale = rms_scale(block_input)
    d_in_norm, g_attn_gain = rms_backward(block_input, in_scale, attn_gain, dxn)
    d_tokens = (jnp.concatenate(d_res_parts, axis=0) + d_in_norm).astype(BF16)

    g_mine = scatter_sum(g_mine, "exp")
    g_mine = jnp.concatenate([g_mine, g_out], axis=1)
    gain_grads = [g_attn_gain[None], g_mid_gain]
    for piece in (g_query_gain, g_key_gain):
        gain_grads.append(
            lax.dynamic_update_slice_in_dim(jnp.zeros((1, width), F32), piece[None], c_at * cols, 1)
        )
    spare = -(experts + 4) % 8
    smalls = jnp.concatenate([g_router] + gain_grads + [jnp.zeros((spare, width), F32)], axis=0)
    smalls = smalls.reshape(-1, n_exp, shard).transpose(1, 0, 2)
    g_up, *g_full, smalls = up_sums(kept_up, first_up, g_mine, smalls)
    return (
        mixed[None], d_tokens[None],
        *[g.astype(F32) for g in g_full],
        smalls[:experts].T,
        smalls[experts], smalls[experts + 2], smalls[experts + 3], smalls[experts + 1],
        g_gate.astype(F32), g_up.astype(F32), g_down.astype(F32),
    )


def solution(mesh):
    tok = P("exp", "ctx", None)
    two, three, one = P("exp", None), P("exp", None, None), P("exp")
    return jax.shard_map(
        local,
        mesh=mesh,
        in_specs=(tok, tok, one, P(), tok) + (two,) * 5 + (one,) * 4 + (three,) * 3,
        out_specs=(tok, tok) + (two,) * 5 + (one,) * 4 + (tok,) * 3,
        check_vma=False,
    )
```

```python
import functools
import math

import jax
import jax.numpy as jnp
from jax import lax
from jax.experimental import pallas as pl
from jax.experimental.pallas import tpu as pltpu
from jax.sharding import PartitionSpec as P

HEADS = 16
HEAD_DIM = 128
LANES = 128
EPSILON = 1e-05
ROPE_BASE = 10000.0
MASKED_SCORE = -1e30
FACTOR = HEAD_DIM ** (-0.5)
F32 = jnp.float32
BF16 = jnp.bfloat16
MIB = 1 << 20


def mm(left, right):
    return jnp.dot(left, right, preferred_element_type=F32)


def mm_t(left, right):
    return lax.dot_general(left, right, (((1,), (1,)), ((), ())), preferred_element_type=F32)


def t_mm(left, right):
    return lax.dot_general(left, right, (((0,), (0,)), ((), ())), preferred_element_type=F32)


def rms_scale(rows):
    return lax.rsqrt(jnp.mean(rows * rows, axis=-1, keepdims=True) + EPSILON)


def rms_backward(rows, inv_scale, gain_vec, grad_in):
    weighted = grad_in * gain_vec
    inner_mean = jnp.mean(weighted * rows, axis=-1, keepdims=True)
    d_rows = inv_scale * weighted - rows * (inv_scale * inv_scale * inv_scale) * inner_mean
    return d_rows, jnp.sum(grad_in * rows * inv_scale, axis=0)


def rope_tables(positions):
    half_dim = HEAD_DIM // 2
    frequency = jnp.exp(
        jnp.arange(half_dim, dtype=F32) * (-2.0 * math.log(ROPE_BASE) / HEAD_DIM)
    )
    angle = positions.astype(F32)[:, None] * frequency[None, :]
    cosine, sine = jnp.cos(angle), jnp.sin(angle)
    return (
        jnp.concatenate([cosine, cosine], axis=1),
        jnp.concatenate([-sine, sine], axis=1),
    )


def positions_of(span_order, storage, span_length):
    return jnp.take(span_order, storage // span_length) * span_length + storage % span_length


def rotated(rows, scale, gain, cosine, sine):
    normed = rows * scale * gain
    return (normed * cosine + pltpu.roll(normed, HEAD_DIM // 2, 1) * sine).astype(BF16)


def unrotated(rows, cosine, sine):
    return rows * cosine - pltpu.roll(rows, HEAD_DIM // 2, 1) * sine


def head_probs(query, key, q_pos, k_pos):
    scores = jnp.where(k_pos <= q_pos, mm_t(query, key) * FACTOR, MASKED_SCORE)
    expo = jnp.exp(scores - jnp.max(scores, axis=1, keepdims=True))
    return expo / jnp.sum(expo, axis=1, keepdims=True)


def attend_kernel(
    q_ref, k_ref, v_ref, qs_ref, ks_ref, qg_ref, kg_ref, qc_ref, qn_ref, kc_ref, kn_ref,
    qp_ref, kp_ref, out_ref,
):
    query = rotated(q_ref[...], qs_ref[...], qg_ref[...], qc_ref[...], qn_ref[...])
    key = rotated(k_ref[...], ks_ref[...], kg_ref[...], kc_ref[...], kn_ref[...])
    probs = head_probs(query, key, qp_ref[...], kp_ref[...])
    out_ref[...] = mm(probs.astype(BF16), v_ref[...].astype(BF16)).astype(BF16)


def attend_back_kernel(
    q_ref, k_ref, v_ref, qs_ref, ks_ref, qg_ref, kg_ref, qc_ref, qn_ref, kc_ref, kn_ref,
    qp_ref, kp_ref, da_ref, dk_in, dv_in, *refs,
):
    dq_ref, dk_ref, dv_ref = refs[-3:]
    query = rotated(q_ref[...], qs_ref[...], qg_ref[...], qc_ref[...], qn_ref[...])
    key = rotated(k_ref[...], ks_ref[...], kg_ref[...], kc_ref[...], kn_ref[...])
    probs = head_probs(query, key, qp_ref[...], kp_ref[...])
    d_att = da_ref[...]
    d_probs = mm_t(d_att, v_ref[...].astype(BF16))
    inner = jnp.sum(probs * d_probs, axis=1, keepdims=True)
    d_scores = (probs * (d_probs - inner)).astype(BF16)
    dq_ref[...] = unrotated(mm(d_scores, key) * FACTOR, qc_ref[...], qn_ref[...])
    dk = unrotated(t_mm(d_scores, query) * FACTOR, kc_ref[...], kn_ref[...])
    dk_ref[...] = dk_in[...] + dk
    dv_ref[...] = dv_in[...] + t_mm(probs.astype(BF16), d_att)


def attention_specs(rows, seq, heads, h):
    def head_rows(n, at, row=0):
        return pl.BlockSpec((n, HEAD_DIM), lambda i: (row, at + i))

    def fixed(shape, row=0):
        return pl.BlockSpec(shape, lambda i: (row, 0))

    return [
        head_rows(rows, 0, h), head_rows(seq, heads), head_rows(seq, 2 * heads),
        fixed((rows, 1), h), fixed((seq, 1)), head_rows(1, 0), head_rows(1, 0),
        fixed((rows, HEAD_DIM), h), fixed((rows, HEAD_DIM), h),
        fixed((seq, HEAD_DIM)), fixed((seq, HEAD_DIM)),
        fixed((rows, 1), h), fixed((1, seq)),
    ]


def attend(base, rows, h):
    seq, cols = base[0].shape[0], base[0].shape[1] // 3
    heads = cols // HEAD_DIM
    return pl.pallas_call(
        attend_kernel,
        grid=(heads,),
        in_specs=attention_specs(rows, seq, heads, h),
        out_specs=pl.BlockSpec((rows, HEAD_DIM), lambda i: (0, i)),
        out_shape=jax.ShapeDtypeStruct((rows, cols), BF16),
        compiler_params=pltpu.CompilerParams(vmem_limit_bytes=48 * MIB),
        cost_estimate=pl.CostEstimate(
            flops=4 * rows * seq * cols, bytes_accessed=8 * MIB, transcendentals=rows * seq * heads
        ),
    )(*base)


def attend_back(base, rows, h, d_att, dk, dv, earlier):
    seq, cols = base[0].shape[0], base[0].shape[1] // 3
    heads = cols // HEAD_DIM
    q_out = pl.BlockSpec((rows, HEAD_DIM), lambda i: (0, i))
    k_out = pl.BlockSpec((seq, HEAD_DIM), lambda i: (0, i))
    return pl.pallas_call(
        attend_back_kernel,
        grid=(heads,),
        in_specs=attention_specs(rows, seq, heads, h)
        + [q_out, k_out, k_out]
        + [pl.BlockSpec(memory_space=pl.ANY)] * len(earlier),
        out_specs=[q_out, k_out, k_out],
        out_shape=[
            jax.ShapeDtypeStruct((rows, cols), F32),
            jax.ShapeDtypeStruct((seq, cols), F32),
            jax.ShapeDtypeStruct((seq, cols), F32),
        ],
        compiler_params=pltpu.CompilerParams(vmem_limit_bytes=48 * MIB),
        cost_estimate=pl.CostEstimate(
            flops=10 * rows * seq * cols, bytes_accessed=16 * MIB, transcendentals=rows * seq * heads
        ),
    )(*base, d_att, dk, dv, *earlier)


def expert_kernel(
    experts, own, step, x_ref, dh_ref, member_ref, router_ref, pick_ref, wg_hbm, wu_hbm,
    hid_ref, da_ref, db_ref, dx_ref, coef_ref, wg, wu, sems,
):
    i = pl.program_id(0)

    def loads(j):
        return (
            pltpu.make_async_copy(wg_hbm.at[j], wg.at[j], sems.at[0, j]),
            pltpu.make_async_copy(wu_hbm.at[j], wu.at[j], sems.at[1, j]),
        )

    @pl.when(i == 0)
    def _():
        for j in range(own):
            for copy in loads(j):
                copy.start()

    logits = mm(x_ref[...], router_ref[...])
    lane = lax.broadcasted_iota(jnp.int32, logits.shape, 1)
    logits = jnp.where(lane < experts, logits, MASKED_SCORE)
    expo = jnp.exp(logits - jnp.max(logits, axis=1, keepdims=True))
    router = expo / jnp.sum(expo, axis=1, keepdims=True)
    chosen = router * member_ref[...].astype(F32)
    coef = jnp.zeros_like(router)
    ff = wg.shape[2]
    for j in range(own):

        @pl.when(i == 0)
        def _():
            for copy in loads(j):
                copy.wait()

        pick = pick_ref[j : j + 1, :]
        gate = jnp.sum(chosen * pick, axis=1, keepdims=True)
        flow = jnp.zeros_like(gate)
        for f in range(0, ff, step):
            cut = slice(f, f + step)
            a = mm(x_ref[...], wg[j, :, cut])
            b = mm(x_ref[...], wu[j, :, cut])
            d_hid = dh_ref[j, :, cut].astype(F32)
            sig = jax.nn.sigmoid(a)
            silu = a * sig
            hid = silu * b
            flow = flow + jnp.sum(hid * d_hid, axis=1, keepdims=True)
            hid_ref[j, :, cut] = (gate * hid).astype(BF16)
            d_hid = d_hid * gate
            da_ref[j, :, cut] = (d_hid * b * (sig + silu * (1.0 - sig))).astype(BF16)
            db_ref[j, :, cut] = (d_hid * silu).astype(BF16)
        coef = coef + flow * gate * (pick - router)
    low = coef.astype(BF16)
    coef_ref[...] = low
    width = x_ref.shape[1]
    for n in range(0, width, step):
        cut = slice(n, n + step)
        part = mm_t(low, router_ref[cut, :])
        for j in range(own):
            part = part + mm_t(da_ref[j], wg[j, cut, :]) + mm_t(db_ref[j], wu[j, cut, :])
        dx_ref[:, cut] = part.astype(BF16)


def expert_pass(x, d_hid, member, router_w, pick, w_gate, w_up, experts):
    rows, width = x.shape
    own, _, ff = w_gate.shape
    tile = 256
    by_row = pl.BlockSpec((tile, width), lambda i: (i, 0))
    by_lane = pl.BlockSpec((tile, LANES), lambda i: (i, 0))
    by_expert = pl.BlockSpec((own, tile, ff), lambda i: (0, i, 0))
    return pl.pallas_call(
        functools.partial(expert_kernel, experts, own, 512),
        grid=(rows // tile,),
        in_specs=[
            by_row, by_expert, by_lane,
            pl.BlockSpec((width, LANES), lambda i: (0, 0)),
            pl.BlockSpec(pick.shape, lambda i: (0, 0)),
            pl.BlockSpec(memory_space=pl.ANY),
            pl.BlockSpec(memory_space=pl.ANY),
        ],
        out_specs=[by_expert] * 3 + [by_row, by_lane],
        out_shape=[jax.ShapeDtypeStruct((own, rows, ff), BF16)] * 3
        + [jax.ShapeDtypeStruct((rows, width), BF16), jax.ShapeDtypeStruct((rows, LANES), BF16)],
        scratch_shapes=[
            pltpu.VMEM((own, width, ff), BF16),
            pltpu.VMEM((own, width, ff), BF16),
            pltpu.SemaphoreType.DMA((2, own)),
        ],
        compiler_params=pltpu.CompilerParams(vmem_limit_bytes=56 * MIB),
        cost_estimate=pl.CostEstimate(
            flops=8 * rows * width * ff * own, bytes_accessed=40 * MIB, transcendentals=0
        ),
    )(x, d_hid, member, router_w, pick, w_gate, w_up)


def weight_kernel(n, *refs):
    total = t_mm(refs[0][...], refs[n][...])
    for h in range(1, n):
        total = total + t_mm(refs[h][...], refs[n + h][...])
    refs[-1][...] = total.astype(BF16)


def weight_grad(lefts, rights, block, tall, earlier):
    n = len(lefts)

    def by_column(a):
        return pl.BlockSpec((a.shape[0], block), lambda i: (0, i))

    def fixed(a):
        return pl.BlockSpec(a.shape, lambda i: (0, 0))

    columns = rights[0].shape[1] if tall else block
    rows = block if tall else lefts[0].shape[1]
    count = (lefts if tall else rights)[0].shape[1] // block
    return pl.pallas_call(
        functools.partial(weight_kernel, n),
        grid=(count,),
        in_specs=[(by_column if tall else fixed)(a) for a in lefts]
        + [(fixed if tall else by_column)(a) for a in rights]
        + [pl.BlockSpec(memory_space=pl.ANY)] * len(earlier),
        out_specs=pl.BlockSpec((rows, columns), lambda i: (i, 0)),
        out_shape=jax.ShapeDtypeStruct((count * rows, columns), BF16),
        compiler_params=pltpu.CompilerParams(vmem_limit_bytes=48 * MIB),
    )(*lefts, *rights, *earlier)


def partial_kernel(n, part, d_ref, w_ref, *refs):
    out_ref = refs[-1]
    rows, halves = n * part, d_ref.shape[0] // (n * part)
    for h in range(halves):
        total = mm_t(d_ref[h * rows : (h + 1) * rows, :], w_ref[...]).astype(BF16)
        for c in range(n):
            out_ref[0, c, h * part : (h + 1) * part, :] = total[c * part : (c + 1) * part, :]


def input_partial(d_qkv, weights, part, earlier):
    n = lax.axis_size("ctx")
    seq, depth = d_qkv.shape
    width = weights.shape[0]
    rows = seq // n
    return pl.pallas_call(
        functools.partial(partial_kernel, n, part),
        grid=(2,),
        in_specs=[
            pl.BlockSpec((seq, depth), lambda i: (0, 0)),
            pl.BlockSpec((width // 2, depth), lambda i: (i, 0)),
        ]
        + [pl.BlockSpec(memory_space=pl.ANY)] * len(earlier),
        out_specs=pl.BlockSpec((1, n, rows, width // 2), lambda i: (i, 0, 0, 0)),
        out_shape=jax.ShapeDtypeStruct((2, n, rows, width // 2), BF16),
        compiler_params=pltpu.CompilerParams(vmem_limit_bytes=48 * MIB),
    )(d_qkv, weights, *earlier)


def give_kernel(n, count, table, *refs):
    for k in range(count):
        total = t_mm(refs[0][...], refs[(k + 1) * n][0])
        for h in range(1, n):
            total = total + t_mm(refs[h][...], refs[(k + 1) * n + h][0])
        refs[len(refs) - count + k][0] = total.astype(BF16)


def given_grads(table, lefts, rights, block, j, earlier):
    n, blocks = len(lefts), table.shape[0]
    flat = [a for right in rights for a in right]
    columns = flat[0].shape[2]
    return pl.pallas_call(
        functools.partial(give_kernel, n, len(rights)),
        grid_spec=pltpu.PrefetchScalarGridSpec(
            num_scalar_prefetch=1,
            grid=(blocks,),
            in_specs=[pl.BlockSpec((a.shape[0], block), lambda i, t: (0, t[i])) for a in lefts]
            + [pl.BlockSpec((1,) + a.shape[1:], lambda i, t: (j, 0, 0)) for a in flat]
            + [pl.BlockSpec(memory_space=pl.ANY)] * len(earlier),
            out_specs=[pl.BlockSpec((1, block, columns), lambda i, t: (i, 0, 0))] * len(rights),
        ),
        out_shape=[jax.ShapeDtypeStruct((blocks, block, columns), BF16)] * len(rights),
        compiler_params=pltpu.CompilerParams(vmem_limit_bytes=48 * MIB),
    )(table, *lefts, *flat, *earlier)


def mid_kernel(n, x_ref, own_ref, gain_ref, *refs):
    total = x_ref[...].astype(F32) + own_ref[...]
    for got in refs[: n - 1]:
        total = total + got[...].astype(F32)
    res_ref, scale_ref, low_ref = refs[-3:]
    scale = lax.rsqrt(jnp.mean(total * total, axis=1, keepdims=True) + EPSILON)
    res_ref[...] = total
    scale_ref[...] = scale
    low_ref[...] = (total * scale * gain_ref[...]).astype(BF16)


def middle(x, own_block, got, gain, earlier):
    rows, width = x.shape
    whole = pl.BlockSpec(memory_space=pltpu.VMEM)
    return pl.pallas_call(
        functools.partial(mid_kernel, len(got) + 1),
        in_specs=[whole] * (3 + len(got)) + [pl.BlockSpec(memory_space=pl.ANY)] * len(earlier),
        out_specs=[whole] * 3,
        out_shape=[
            jax.ShapeDtypeStruct((rows, width), F32),
            jax.ShapeDtypeStruct((rows, 1), F32),
            jax.ShapeDtypeStruct((rows, width), BF16),
        ],
        compiler_params=pltpu.CompilerParams(vmem_limit_bytes=60 * MIB),
    )(x, own_block, gain[None], *got, *earlier)


def res_kernel(res_ref, scale_ref, gain_ref, grad_ref, mid_ref, *refs):
    out_ref, low_ref, gain_out = refs[-3:]
    rows, scale = res_ref[...], scale_ref[...]
    grad_in = mid_ref[...].astype(F32)
    weighted = grad_in * gain_ref[...]
    inner = jnp.mean(weighted * rows, axis=1, keepdims=True)
    total = grad_ref[...] + scale * weighted - rows * (scale * scale * scale) * inner
    out_ref[...] = total
    low_ref[...] = total.astype(BF16)
    gain_out[...] = jnp.sum(grad_in * rows * scale, axis=0, keepdims=True)


def residual_back(residual, scale, gain, grad, d_mid, earlier):
    rows, width = residual.shape
    whole = pl.BlockSpec(memory_space=pltpu.VMEM)
    return pl.pallas_call(
        res_kernel,
        in_specs=[whole] * 5 + [pl.BlockSpec(memory_space=pl.ANY)] * len(earlier),
        out_specs=[whole] * 3,
        out_shape=[
            jax.ShapeDtypeStruct((rows, width), F32),
            jax.ShapeDtypeStruct((rows, width), BF16),
            jax.ShapeDtypeStruct((1, width), F32),
        ],
        compiler_params=pltpu.CompilerParams(vmem_limit_bytes=60 * MIB),
    )(residual, scale, gain[None], grad, d_mid, *earlier)


def meet(peers):
    barrier = pltpu.get_barrier_semaphore()
    for peer in peers:
        pl.semaphore_signal(barrier, inc=1, device_id=peer, device_id_type=pl.DeviceIdType.MESH)
    pl.semaphore_wait(barrier, len(peers))


def ctx_sum_kernel(n, x_ref, *refs):
    out_ref, slots, send, recv = refs[-4:]
    me = lax.axis_index("ctx")
    peers = [{"ctx": lax.rem(me + d, n)} for d in range(1, n)]
    meet(peers)
    slots[me] = x_ref[...]
    copies = [
        pltpu.make_async_remote_copy(
            src_ref=x_ref, dst_ref=slots.at[me], send_sem=send.at[d], recv_sem=recv.at[d],
            device_id=peer, device_id_type=pl.DeviceIdType.MESH,
        )
        for d, peer in enumerate(peers)
    ]
    for copy in copies:
        copy.start()
    for copy in copies:
        copy.wait()
    total = slots[0]
    for k in range(1, n):
        total = total + slots[k]
    out_ref[...] = total


def ctx_sum(x, number, earlier=()):
    n = lax.axis_size("ctx")
    whole = pl.BlockSpec(memory_space=pltpu.VMEM)
    return pl.pallas_call(
        functools.partial(ctx_sum_kernel, n),
        in_specs=[whole] + [pl.BlockSpec(memory_space=pl.ANY)] * len(earlier),
        out_specs=whole,
        out_shape=jax.ShapeDtypeStruct(x.shape, F32),
        scratch_shapes=[
            pltpu.VMEM((n,) + x.shape, F32),
            pltpu.SemaphoreType.DMA((n - 1,)),
            pltpu.SemaphoreType.DMA((n - 1,)),
        ],
        compiler_params=pltpu.CompilerParams(collective_id=number, has_side_effects=True),
    )(x, *earlier)


class SmallSum:
    def __init__(self, n_ctx, n_exp, x, first, second, sems):
        self.x, self.first, self.second, self.sems = x, first, second, sems
        self.c_at, self.e_at = lax.axis_index("ctx"), lax.axis_index("exp")
        self.across = [{"exp": lax.rem(self.e_at + d, n_exp)} for d in range(1, n_exp)]
        self.along = [{"ctx": lax.rem(self.c_at + d, n_ctx)} for d in range(1, n_ctx)]

    def copy(self, src, dst, step, d, peer):
        return pltpu.make_async_remote_copy(
            src_ref=src, dst_ref=dst, send_sem=self.sems.at[2 * step, d],
            recv_sem=self.sems.at[2 * step + 1, d], device_id=peer,
            device_id_type=pl.DeviceIdType.MESH,
        )

    def over_exp(self):
        return [
            self.copy(self.x.at[peer["exp"]], self.first.at[self.e_at], 0, d, peer)
            for d, peer in enumerate(self.across)
        ]

    def over_ctx(self):
        mine = self.second.at[self.c_at]
        return [self.copy(mine, mine, 1, d, peer) for d, peer in enumerate(self.along)]

    def begin(self):
        for copy in self.over_exp():
            copy.start()
        self.first[self.e_at] = self.x[self.e_at]

    def pass_on(self):
        for copy in self.over_exp():
            copy.wait()
        total = self.first[0]
        for k in range(1, self.first.shape[0]):
            total = total + self.first[k]
        self.second[self.c_at] = total
        for copy in self.over_ctx():
            copy.start()

    def finish(self, out):
        for copy in self.over_ctx():
            copy.wait()
        total = self.second[0]
        for k in range(1, self.second.shape[0]):
            total = total + self.second[k]
        out[...] = total

    @staticmethod
    def scratch(n_ctx, shape):
        return [
            pltpu.VMEM(shape, F32),
            pltpu.VMEM((n_ctx,) + shape[1:], F32),
            pltpu.SemaphoreType.DMA((4, max(n_ctx, shape[0]) - 1)),
        ]


def halving_masks(order):
    masks = [0]
    for bit in order[::-1]:
        masks = masks + [m | (1 << bit) for m in masks]
    return masks


def flip(value, mask):
    bit = 0
    while mask >> bit:
        if (mask >> bit) & 1:
            value = value + (1 << bit) * (1 - 2 * lax.rem(lax.div(value, 1 << bit), 2))
        bit += 1
    return value


class Halving:
    def __init__(
        self, n, me, source, blocks, got, send, recv, out, first=None, acc=None, kept=None
    ):
        self.n, self.me, self.source, self.blocks, self.got = n, me, source, blocks, got
        self.send, self.recv, self.out = send, recv, out
        self.first, self.acc, self.kept = first, out if acc is None else acc, kept
        bits = list(range(n.bit_length() - 1))
        self.own = out.shape[0]
        self.orders = [bits if j % 2 == 0 else bits[::-1] for j in range(self.own)]
        self.masks = [halving_masks(order) for order in self.orders]
        self.steps = len(bits)

    def target(self, j, k):
        return flip(self.me, self.masks[j][k])

    def slot(self, s, k):
        made = 0 if self.first is None else self.n >> 1
        return self.n - (self.n >> s) + k - (self.n >> (s + 1)) - made

    def copy(self, j, s, k):
        given = self.source is not None and s == 0
        at = self.slot(s, k)
        return pltpu.make_async_remote_copy(
            src_ref=self.source.at[j, self.target(j, k)] if given else self.blocks.at[j, k - 1],
            dst_ref=self.got.at[j, at],
            send_sem=self.send.at[j, at],
            recv_sem=self.recv.at[j, at],
            device_id={"ctx": flip(self.me, 1 << self.orders[j][s])},
            device_id_type=pl.DeviceIdType.MESH,
        )

    def going(self, s):
        return [
            (j, k)
            for k in range((self.n >> s) - 1, (self.n >> (s + 1)) - 1, -1)
            for j in range(self.own)
        ]

    def begin(self, value=None):
        for j, k in self.going(0) if self.first is None else []:
            if value is not None:
                self.blocks[j, k - 1] = value(j, self.target(j, k)).astype(BF16)
            self.copy(j, 0, k).start()
        for k in range(self.n // 2 - 1, 0, -1):
            for j in range(self.own):
                at = self.target(j, k)
                mine = self.source[j, at] if value is None else value(j, at)
                self.blocks[j, k - 1] = mine.astype(BF16)

    def rest(self, value=None):
        for j in range(self.own):
            self.acc[j] = self.source[j, self.me].astype(F32) if value is None else value(j, self.me)

    def arrived(self, j, k, steps):
        total = None
        for s in range(steps):
            sent = k + (self.n >> (s + 1))
            if s == 0 and self.first is not None:
                part = self.first[j][k].astype(F32)
            else:
                self.copy(j, s, sent).wait_recv()
                part = self.got[j, self.slot(s, sent)].astype(F32)
            total = part if total is None else total + part
        return total

    def pass_on(self):
        for s in range(1, self.steps):
            for j, k in self.going(s):
                mine = self.blocks[j, k - 1] if self.kept is None else self.kept[j, k]
                total = mine.astype(F32) + self.arrived(j, k, s)
                self.blocks[j, k - 1] = total.astype(BF16)
                self.copy(j, s, k).start()

    def finish(self):
        for j in range(self.own):
            mine = self.acc[j] if self.kept is None else self.kept[j, 0].astype(F32)
            self.out[j] = (mine + self.arrived(j, 0, self.steps)).astype(self.out.dtype)
        for s in range(0 if self.first is None else 1, self.steps):
            for j, k in self.going(s):
                self.copy(j, s, k).wait_send()

    @staticmethod
    def scratch(own, n, rows, columns):
        return [
            pltpu.VMEM((own, n - 1, rows, columns), BF16),
            pltpu.VMEM((own, n - 1, rows, columns), BF16),
            pltpu.SemaphoreType.DMA((own, n - 1)),
            pltpu.SemaphoreType.DMA((own, n - 1)),
        ]


def ctx_peers(n, me):
    return [{"ctx": lax.rem(me + d, n)} for d in range(1, n)]


def entry(ref, j):
    return ref.at[j] if len(ref.shape) == 3 else ref


def product(lefts, rights, block):
    def value(j, at):
        total = None
        for left, right in zip(lefts, rights):
            columns = pl.ds(pl.multiple_of(at * block, LANES), block)
            part = t_mm(entry(left, j)[:, columns], entry(right, j)[...])
            total = part if total is None else total + part
        return total

    return value


def down_kernel(n, halves, *refs):
    hid, grad, w_hbm = refs[:halves], refs[halves : 2 * halves], refs[2 * halves]
    refs = refs[2 * halves + 1 :]
    out, y_hbm, scratch = refs[0], refs[1 : 1 + halves], refs[1 + halves :]
    w_down, ys, local_sems = scratch[5], scratch[6 : 6 + halves], scratch[6 + halves]
    load = pltpu.make_async_copy(w_hbm, w_down, local_sems.at[halves])
    stores = [pltpu.make_async_copy(ys[h], y_hbm[h], local_sems.at[h]) for h in range(halves)]
    load.start()
    me = lax.axis_index("ctx")
    meet(ctx_peers(n, me))
    sums = Halving(n, me, None, *scratch[:4], out, acc=scratch[4])
    value = product(hid, grad, hid[0].shape[2] // n)
    sums.begin(value)
    sums.rest(value)
    load.wait()
    width = w_down.shape[2]
    for h in range(halves):
        for start in range(0, width, 512):
            cut = slice(start, start + 512)
            total = mm(hid[h][0], w_down[0, :, cut])
            for j in range(1, w_down.shape[0]):
                total = total + mm(hid[h][j], w_down[j, :, cut])
            ys[h][:, cut] = total.astype(BF16)
        stores[h].start()
        if h == 0:
            sums.pass_on()
    sums.finish()
    for store in stores:
        store.wait()


def gate_kernel(n, halves, *refs):
    mids, gate_pres, up_pres = [refs[k * halves : (k + 1) * halves] for k in range(3)]
    own = gate_pres[0].shape[0]
    partial, first = refs[3 * halves], refs[3 * halves + 1 : 3 * halves + 1 + own]
    out, dxn, kept = refs[-12:-9]
    me = lax.axis_index("ctx")
    meet(ctx_peers(n, me))
    rows = Halving(n, me, partial, *refs[-9:-5], dxn)
    rows.begin()
    block = mids[0].shape[1] // n
    sums = Halving(n, me, None, *refs[-5:-1], out, first, refs[-1])
    value = product(mids, gate_pres, block)
    sums.begin(value)
    sums.pass_on()
    rows.pass_on()
    sums.rest(value)
    rows.rest()
    value = product(mids, up_pres, block)
    for k in range(n // 2):
        for j in range(own):
            kept[j, k] = value(j, sums.target(j, k)).astype(BF16)
    rows.finish()
    sums.finish()


def up_kernel(n, *refs):
    piece, x, kept = refs[:3]
    out, *whole = refs[-16:-11]
    small_out, slots, send, recv = refs[-11:-7]
    me = lax.axis_index("ctx")
    smalls = SmallSum(n, x.shape[0], x, *refs[-7:-4])
    meet(smalls.across + smalls.along)
    smalls.begin()
    bits = list(range(n.bit_length() - 1))
    half = piece.shape[0] // 2

    def doubling(i, s):
        order = bits if i == 0 else bits[::-1]
        lines = pl.ds(i * half, half)
        copies = []
        for m in halving_masks(order[:s]):
            at = flip(me, m)
            sem = i, (1 << s) - 1 + len(copies)
            copies.append(
                pltpu.make_async_remote_copy(
                    src_ref=slots.at[at, lines] if m else piece.at[lines],
                    dst_ref=slots.at[at, lines],
                    send_sem=send.at[sem],
                    recv_sem=recv.at[sem],
                    device_id={"ctx": flip(me, 1 << order[s])},
                    device_id_type=pl.DeviceIdType.MESH,
                )
            )
        return copies

    first = refs[3 : 3 + kept.shape[0]]
    sums = Halving(n, me, None, *refs[-4:], out, first, kept=kept)
    for i in range(2):
        for copy in doubling(i, 0):
            copy.start()
    sums.pass_on()
    smalls.pass_on()
    slots[me] = piece[...]
    for s in range(1, len(bits)):
        for i in range(2):
            for copy in doubling(i, s - 1):
                copy.wait_recv()
            for copy in doubling(i, s):
                copy.start()
    smalls.finish(small_out)
    sums.finish()
    for i in range(2):
        for copy in doubling(i, len(bits) - 1):
            copy.wait_recv()
        for s in range(len(bits)):
            for copy in doubling(i, s):
                copy.wait_send()
    cols = piece.shape[1] // len(whole)
    for c in range(n):
        for k, ref in enumerate(whole):
            ref[:, c * cols : (c + 1) * cols] = slots[c, :, k * cols : (k + 1) * cols]


class Doubling:
    def __init__(self, axis, order, last, block, slot, sems, base):
        self.me, self.axis, self.order, self.last = lax.axis_index(axis), axis, order, last
        self.block, self.slot, self.sems, self.base = block, slot, sems, base
        self.steps = [halving_masks(order[:s]) for s in range(len(order) + 1)]
        self.keys = [(bit, m) for bit, ms in zip(order, self.steps) for m in ms]
        if last is not None:
            self.keys += [(last, m) for m in self.steps[-1]]

    def copy(self, bit, m):
        at = self.base + self.keys.index((bit, m))
        place = self.slot(flip(self.me, m))
        return pltpu.make_async_remote_copy(
            src_ref=place if m else self.block,
            dst_ref=place,
            send_sem=self.sems.at[0, at],
            recv_sem=self.sems.at[1, at],
            device_id={self.axis: flip(self.me, 1 << bit)},
            device_id_type=pl.DeviceIdType.MESH,
        )

    def step(self, s):
        fresh = [0]
        if s:
            fresh = [m | (1 << self.order[s - 1]) for m in self.steps[s - 1]]
            for m in self.steps[s - 1]:
                self.copy(self.order[s - 1], m).wait_recv()
        if s < len(self.order):
            for m in self.steps[s]:
                self.copy(self.order[s], m).start()
        if self.last is not None:
            for m in fresh:
                self.copy(self.last, m).start()

    def finish(self):
        if self.last is not None:
            for m in self.steps[-1]:
                self.copy(self.last, m).wait_recv()
        for key in self.keys:
            self.copy(*key).wait_send()


def start_kernel(n_ctx, n_exp, w_ref, x_ref, small_ref, w_out, x_out, small_out, sems, local_sems):
    c_at, e_at = lax.axis_index("ctx"), lax.axis_index("exp")
    c_bits, e_bits = n_ctx.bit_length() - 1, n_exp.bit_length() - 1
    meet(
        [{"ctx": flip(c_at, 1 << b)} for b in range(c_bits)]
        + [{"exp": flip(e_at, 1 << b)} for b in range(e_bits)]
    )
    far = list(range(1, e_bits))
    near = list(range(c_bits))
    half = w_ref.shape[0] // 2
    moves, base = [], 0

    def add(axis, order, last, block, slot):
        moves.append(Doubling(axis, order, last, block, slot, sems, base))
        return base + len(moves[-1].keys)

    base = add("exp", far, 0, small_ref, lambda at: small_out.at[at])
    for i, order in enumerate((far[::-1], far)):
        lines = pl.ds(i * half, half)
        base = add(
            "exp", order, 0, w_ref.at[lines], lambda at, lines=lines: w_out.at[at, lines]
        )
    for i, order in enumerate((near[::-1], near)):
        base = add("ctx", order, None, x_ref.at[i], lambda at, i=i: x_out.at[i, at])
    own = [
        pltpu.make_async_copy(w_ref, w_out.at[e_at], local_sems.at[0]),
        pltpu.make_async_copy(small_ref, small_out.at[e_at], local_sems.at[1]),
        pltpu.make_async_copy(x_ref.at[0], x_out.at[0, c_at], local_sems.at[2]),
        pltpu.make_async_copy(x_ref.at[1], x_out.at[1, c_at], local_sems.at[3]),
    ]
    for s in range(max(len(far), len(near)) + 1):
        for move in moves:
            if s <= len(move.order):
                move.step(s)
        if s == 0:
            for copy in own:
                copy.start()
    for move in moves:
        move.finish()
    for copy in own:
        copy.wait()


def gather_start(w, x, small):
    n_ctx, n_exp = lax.axis_size("ctx"), lax.axis_size("exp")
    count = 3 * (n_exp - 1) + 2 * (n_ctx - 1)
    return pl.pallas_call(
        functools.partial(start_kernel, n_ctx, n_exp),
        in_specs=[ANY] * 3,
        out_specs=[ANY] * 3,
        out_shape=[
            jax.ShapeDtypeStruct((n_exp,) + w.shape, BF16),
            jax.ShapeDtypeStruct((x.shape[0], n_ctx) + x.shape[1:], BF16),
            jax.ShapeDtypeStruct((n_exp,) + small.shape, BF16),
        ],
        scratch_shapes=[pltpu.SemaphoreType.DMA((2, count)), pltpu.SemaphoreType.DMA((4,))],
        compiler_params=pltpu.CompilerParams(collective_id=6, has_side_effects=True),
    )(w, x, small)


def hold_kernel(*refs):
    pass


def held(arrays, earlier):
    n = len(arrays)
    return pl.pallas_call(
        hold_kernel,
        in_specs=[ANY] * (n + len(earlier)),
        out_specs=[ANY] * n,
        out_shape=[jax.ShapeDtypeStruct(a.shape, a.dtype) for a in arrays],
        input_output_aliases={i: i for i in range(n)},
        compiler_params=pltpu.CompilerParams(vmem_limit_bytes=60 * MIB),
    )(*arrays, *earlier)


def mask_kernel(x_ref, valid_ref, *refs):
    refs[-1][...] = (x_ref[...].astype(F32) * valid_ref[...]).astype(BF16)


def masked(x, valid, earlier):
    blocks = [pl.BlockSpec(a.shape, lambda i: (0, 0)) for a in (x, valid)]
    return pl.pallas_call(
        mask_kernel,
        grid=(1,),
        in_specs=blocks + [ANY] * len(earlier),
        out_specs=blocks[0],
        out_shape=jax.ShapeDtypeStruct(x.shape, BF16),
    )(x, valid, *earlier)


VMEM = pl.BlockSpec(memory_space=pltpu.VMEM)
ANY = pl.BlockSpec(memory_space=pl.ANY)


def exchange(kernel, number, operands, earlier, outs, scratch, far=()):
    n = lax.axis_size("ctx")
    return pl.pallas_call(
        kernel,
        in_specs=[VMEM] * len(operands) + [ANY] * len(earlier),
        out_specs=[VMEM] * len(outs) + [ANY] * len(far),
        out_shape=[*outs, *far],
        scratch_shapes=scratch,
        compiler_params=pltpu.CompilerParams(
            collective_id=number, has_side_effects=True, vmem_limit_bytes=60 * MIB
        ),
    )(*operands, *earlier)


def down_sums(hid, grad, w_down):
    n, halves = lax.axis_size("ctx"), len(hid)
    own, ff, width = w_down.shape
    outs = [jax.ShapeDtypeStruct((own, ff // n, width), BF16)]
    ys = [jax.ShapeDtypeStruct((h.shape[1], width), BF16) for h in hid]
    return exchange(
        functools.partial(down_kernel, n, halves), 3, [*hid, *grad], (w_down,), outs,
        Halving.scratch(own, n, ff // n, width)
        + [pltpu.VMEM((own, ff // n, width), F32), pltpu.VMEM(w_down.shape, BF16)]
        + [pltpu.VMEM(y.shape, BF16) for y in ys]
        + [pltpu.SemaphoreType.DMA((halves + 1,))],
        ys,
    )


def gate_sums(mids, gate_pres, up_pres, partial, first, earlier):
    n, halves = lax.axis_size("ctx"), len(mids)
    own, _, ff = gate_pres[0].shape
    rows = mids[0].shape[1] // n
    shape = partial.shape
    outs = [
        jax.ShapeDtypeStruct((own, rows, ff), BF16),
        jax.ShapeDtypeStruct((shape[0],) + shape[2:], F32),
        jax.ShapeDtypeStruct((own, n // 2, rows, ff), BF16),
    ]
    return exchange(
        functools.partial(gate_kernel, n, halves), 4,
        [*mids, *gate_pres, *up_pres, partial, *first], earlier, outs,
        Halving.scratch(shape[0], n, *shape[2:])
        + Halving.scratch(own, n // 2, rows, ff)
        + [pltpu.VMEM((own, rows, ff), F32)],
    )


def up_sums(kept, first, piece, smalls):
    n = lax.axis_size("ctx")
    own, _, rows, ff = kept.shape
    shard, width = piece.shape
    outs = [jax.ShapeDtypeStruct((own, rows, ff), BF16)]
    outs += [jax.ShapeDtypeStruct((shard, n * width // 4), BF16) for _ in range(4)]
    outs += [jax.ShapeDtypeStruct(smalls.shape[1:], F32)]
    return exchange(
        functools.partial(up_kernel, n), 5, [piece, smalls, kept, *first], (), outs,
        [
            pltpu.VMEM((n,) + piece.shape, BF16),
            pltpu.SemaphoreType.DMA((2, n - 1)),
            pltpu.SemaphoreType.DMA((2, n - 1)),
        ]
        + SmallSum.scratch(n, smalls.shape)
        + Halving.scratch(own, n // 2, rows, ff),
    )


def gather(block, axis):
    return lax.all_gather(block, axis, axis=0, tiled=True)


def scatter_sum(block, axis, dimension=0):
    return lax.psum_scatter(block, axis, scatter_dimension=dimension, tiled=True)


def after(value, *earlier):
    return lax.optimization_barrier((value,) + earlier)[0]


def swap(block, bits):
    n = lax.axis_size("ctx")
    return lax.ppermute(block, "ctx", [(i, i ^ bits) for i in range(n)])


def take(block, at, size=1, axis=0):
    return lax.dynamic_slice_in_dim(block, at, size, axis)


def gather_ctx(block, axis):
    n, me = lax.axis_size("ctx"), lax.axis_index("ctx")
    parts = [block] + [swap(block, d) for d in range(1, n)]
    shape = block.shape[:axis] + (n,) + block.shape[axis:]
    out = jnp.zeros(shape, block.dtype)
    for d, piece in enumerate(parts):
        out = lax.dynamic_update_slice_in_dim(out, jnp.expand_dims(piece, axis), me ^ d, axis)
    return out


def local(
    tokens, cotangent, lengths, span_order, routes,
    w_query, w_key, w_value, w_output, w_router,
    gain_attn, gain_query, gain_key, gain_mlp,
    w_gate, w_up, w_down,
):
    n_ctx, n_exp = lax.axis_size("ctx"), lax.axis_size("exp")
    c_at, e_at = lax.axis_index("ctx"), lax.axis_index("exp")
    rows = tokens.shape[1]
    width = tokens.shape[2]
    seq = rows * n_ctx
    cols = width // n_ctx
    shard = width // n_exp
    own = w_gate.shape[0]
    ff = w_gate.shape[2]
    experts = w_router.shape[1]
    seq_length = lengths[0]
    halves = 2
    part = rows // halves
    half_seq = part * n_ctx

    ratio = n_exp // n_ctx
    moves = []
    for c in range(n_ctx):
        for e in range(n_exp):
            moves.append(((e // ratio) * n_exp + c * ratio + e % ratio, c * n_exp + e))
    out_piece = lax.ppermute(take(w_output, c_at * cols, cols, 1), ("ctx", "exp"), moves)

    storage = jnp.arange(seq, dtype=jnp.int32)
    storage = (storage % half_seq // part) * rows + storage // half_seq * part + storage % part
    positions = positions_of(span_order, storage, rows // 2)
    my_positions = positions_of(
        span_order, c_at * rows + jnp.arange(rows, dtype=jnp.int32), rows // 2
    )
    valid = (my_positions < seq_length).astype(F32)[:, None]
    small = jnp.concatenate(
        [
            w_router.reshape(-1), gain_attn, gain_query, gain_key, gain_mlp,
            routes[0].astype(BF16).reshape(-1),
        ]
    )
    used = small.shape[0]
    lines = -(-used // (16 * LANES)) * 16
    small = jnp.pad(small, (0, lines * LANES - used)).reshape(lines, LANES)
    pieces = [take(w, c_at * cols, cols, 1) for w in (w_query, w_key, w_value)]
    weights, x_low, small_all = gather_start(
        jnp.concatenate(pieces + [out_piece], axis=1), tokens[0].reshape(halves, part, width), small
    )
    weights = weights.reshape(width, 4 * cols)
    x_low = x_low.reshape(seq, width)
    small_all = small_all.reshape(n_exp, lines * LANES)[:, :used]
    at = shard * experts
    router_w = small_all[:, :at].reshape(width, experts)
    router_w = jnp.pad(router_w, ((0, 0), (0, LANES - experts)))
    gains = []
    for _ in range(4):
        gains.append(small_all[:, at : at + shard].reshape(width).astype(F32))
        at += shard
    attn_gain, query_gain_all, key_gain_all, mlp_gain = gains
    routes_all = small_all[:, at:].reshape(n_exp, rows, routes.shape[2])
    lane = jnp.arange(LANES, dtype=jnp.int32)[None, :]
    query_gain = take(query_gain_all, c_at * cols, cols)
    key_gain = take(key_gain_all, c_at * cols, cols)

    qkv_w = weights[:, : 3 * cols]
    out_w = weights[:, 3 * cols :].reshape(n_ctx, cols, cols).transpose(1, 0, 2).reshape(cols, width)
    x_all = x_low.astype(F32)

    grad_low = masked(cotangent[0], valid, (weights,))
    grad_mine = grad_low.astype(F32)
    grad_parts = [gather(grad_low[h * part : (h + 1) * part], "exp") for h in range(halves)]
    d_hid_parts = [
        jnp.stack([mm_t(g, w_down[j]).astype(BF16) for j in range(own)]) for g in grad_parts
    ]

    cosine, sine = rope_tables(positions)
    xn = (x_all * rms_scale(x_all) * attn_gain).astype(BF16)
    qkv = mm(xn, qkv_w)
    qp, kp = qkv[:, :cols], qkv[:, cols : 2 * cols]
    squares = jnp.stack([jnp.sum(qp * qp, axis=-1), jnp.sum(kp * kp, axis=-1)], axis=0)
    squares = ctx_sum(jnp.pad(squares, ((0, 6), (0, 0))), 0)[:2] / width
    q_scale = lax.rsqrt(squares[0] + EPSILON)[:, None]
    k_scale = lax.rsqrt(squares[1] + EPSILON)[:, None]
    key_positions = jnp.where(positions < seq_length, positions, jnp.int32(1 << 30))
    base = (
        qkv, qkv, qkv, q_scale, k_scale, query_gain[None], key_gain[None],
        cosine, sine, cosine, sine, positions[:, None], key_positions[None],
    )

    attended_parts, mids, residual_parts, scale_parts = [], [], [], []
    for h in range(halves):
        attended = attend(base, half_seq, h)
        attended_parts.append(attended)
        got = []
        for d in range(n_ctx - 1, -1, -1):
            block = mm(take(attended, (c_at ^ d) * part, part), out_w)
            if d:
                got.append(swap(block.astype(BF16), d))
        residual, scale, mid = middle(
            tokens[0, h * part : (h + 1) * part], block, got, mlp_gain,
            (d_hid_parts[h],),
        )
        residual_parts.append(residual)
        scale_parts.append(scale)
        mids.append(gather(mid, "exp"))

    pick = (lane == e_at * own + jnp.arange(max(own, 8), dtype=jnp.int32)[:, None]).astype(F32)
    hid_parts, da_parts, db_parts, coef_parts = [], [], [], []
    dxs = []
    for h in range(halves):
        named = routes_all[:, h * part : (h + 1) * part].reshape(n_exp * part, -1)
        member_h = sum(
            (named[:, k : k + 1] == lane.astype(BF16)).astype(BF16) for k in range(named.shape[1])
        )
        hid, da, db, dx, coef = expert_pass(
            mids[h], d_hid_parts[h], member_h, router_w, pick, w_gate, w_up, experts
        )
        hid_parts.append(hid)
        da_parts.append(da)
        db_parts.append(db)
        coef_parts.append(coef)
        dxs.append(dx)
    d_mids = [scatter_sum(after(dx, mids[-1]), "exp") for dx in dxs]

    def back_to_rows(h, *earlier):
        d_residual, low, g_gain = residual_back(
            residual_parts[h], scale_parts[h], mlp_gain,
            grad_mine[h * part : (h + 1) * part], d_mids[h], earlier,
        )
        dl = gather_ctx(low, 0).reshape(half_seq, width)
        return d_residual, low, g_gain, dl

    g_router = sum(t_mm(c, m) for m, c in zip(mids, coef_parts))[:experts]

    g_down, *y_parts = down_sums(hid_parts, grad_parts, w_down)
    d_res0, low0, gain0, dl0 = back_to_rows(0, y_parts[0])
    d_res1, low1, gain1, dl1 = back_to_rows(1, y_parts[0])
    bits = list(range(n_ctx.bit_length() - 1))
    gives, first_gate, give_up = [], [], []
    for j in range(own):
        order = bits if j % 2 == 0 else bits[::-1]
        table = c_at ^ jnp.asarray(halving_masks(order)[n_ctx // 2 :], jnp.int32)
        give = given_grads(
            table, mids, [da_parts, db_parts], width // n_ctx, j, (low0, low1, *gives)
        )
        first_gate.append(swap(give[0], 1 << order[0]))
        give_up.append(give[1])
        gives.append(give[0])
    g_mid_gain = gain0 + gain1
    d_res_parts, dl_parts = [d_res0, d_res1], [dl0, dl1]
    d_att_parts = [mm_t(dl, out_w).astype(BF16) for dl in dl_parts]
    y_mine = [scatter_sum(y, "exp") for y in y_parts]
    mixed = jnp.concatenate(
        [(r + y.astype(F32)).astype(BF16) for r, y in zip(residual_parts, y_mine)], axis=0
    )

    dq_parts = []
    dk_n = jnp.zeros((seq, cols), F32)
    dv = jnp.zeros((seq, cols), F32)
    g_out = weight_grad(attended_parts, dl_parts, cols, False, (*gives, y_mine[0]))
    for h in range(halves):
        dq, dk_n, dv = attend_back(base, half_seq, h, d_att_parts[h], dk_n, dv, (g_out,))
        dq_parts.append(dq)
    g_out = lax.ppermute(scatter_sum(g_out, "exp"), ("ctx", "exp"), [(b, a) for a, b in moves])
    dq_n = jnp.concatenate(dq_parts, axis=0)
    inner = jnp.stack(
        [
            jnp.sum(dq_n * query_gain * qp, axis=-1),
            jnp.sum(dk_n * key_gain * kp, axis=-1),
        ],
        axis=0,
    )
    inner = ctx_sum(jnp.pad(inner, ((0, 6), (0, 0))), 1, first_gate)
    give_up = held(give_up, (inner,))
    first_up = [swap(g, 1 << (bits[0] if j % 2 == 0 else bits[-1])) for j, g in enumerate(give_up)]
    inner = inner[:2] / width
    dqp = q_scale * dq_n * query_gain - qp * (q_scale**3) * inner[0][:, None]
    dkp = k_scale * dk_n * key_gain - kp * (k_scale**3) * inner[1][:, None]
    g_query_gain = jnp.sum(dq_n * qp * q_scale, axis=0)
    g_key_gain = jnp.sum(dk_n * kp * k_scale, axis=0)
    d_qkv = jnp.concatenate([dqp.astype(BF16), dkp.astype(BF16), dv.astype(BF16)], axis=1)
    partial = input_partial(d_qkv, weights, part, ())
    g_mine = weight_grad([xn], [d_qkv], cols, True, (partial, g_out, y_mine[1], *first_up))
    g_gate, dxn, kept_up = gate_sums(mids, da_parts, db_parts, partial, first_gate, (g_mine,))
    dxn = jnp.concatenate([dxn[0], dxn[1]], axis=1)
    block_input = tokens[0].astype(F32)
    in_scale = rms_scale(block_input)
    d_in_norm, g_attn_gain = rms_backward(block_input, in_scale, attn_gain, dxn)
    d_tokens = (jnp.concatenate(d_res_parts, axis=0) + d_in_norm).astype(BF16)

    g_mine = scatter_sum(g_mine, "exp")
    g_mine = jnp.concatenate([g_mine, g_out], axis=1)
    gain_grads = [g_attn_gain[None], g_mid_gain]
    for piece in (g_query_gain, g_key_gain):
        gain_grads.append(
            lax.dynamic_update_slice_in_dim(jnp.zeros((1, width), F32), piece[None], c_at * cols, 1)
        )
    spare = -(experts + 4) % 8
    smalls = jnp.concatenate([g_router] + gain_grads + [jnp.zeros((spare, width), F32)], axis=0)
    smalls = smalls.reshape(-1, n_exp, shard).transpose(1, 0, 2)
    g_up, *g_full, smalls = up_sums(kept_up, first_up, g_mine, smalls)
    return (
        mixed[None], d_tokens[None],
        *[g.astype(F32) for g in g_full],
        smalls[:experts].T,
        smalls[experts], smalls[experts + 2], smalls[experts + 3], smalls[experts + 1],
        g_gate.astype(F32), g_up.astype(F32), g_down.astype(F32),
    )


def solution(mesh):
    tok = P("exp", "ctx", None)
    two, three, one = P("exp", None), P("exp", None, None), P("exp")
    return jax.shard_map(
        local,
        mesh=mesh,
        in_specs=(tok, tok, one, P(), tok) + (two,) * 5 + (one,) * 4 + (three,) * 3,
        out_specs=(tok, tok) + (two,) * 5 + (one,) * 4 + (tok,) * 3,
        check_vma=False,
    )
```
